32 devices in a mesh: group: 4 (over x, core), fsdp: 8 (over z, y).
Axes of the slice: x: 2, y: 2, z: 4, core: 2. Of those that a mesh axis runs over, the one named last changes fastest.
Arguments:
- inputs: bfloat16 [4, 8192, 768], P('group', 'fsdp'), may hold values from -6 to 6
- segments: int32 [4, 128, 64], P('group', 'fsdp'), may hold values from 0 to 7, never falling along the last dimension, each value on 1 to 32 neighbouring positions
- cotangent: bfloat16 [4, 8192, 768], P('group', 'fsdp'), may hold values from -6 to 6
- attn_weight: float32 [768, 3072], P('fsdp'), may hold values from -0.5412659 to 0.5412659
- attn_first: float32 [4, 768, 3072], P('group', 'fsdp'), may hold values from -64 to 64
- attn_second: float32 [4, 768, 3072], P('group', 'fsdp'), may hold values from 8.192 to 32.768
- attn_outer: float32 [768, 3072], P('fsdp'), may hold values from -0.125 to 0.125
- mlp_weight: float32 [2, 768, 3072], P(None, 'fsdp'), may hold values from -0.21875 to 0.21875
- mlp_first: float32 [4, 2, 768, 3072], P('group', None, 'fsdp'), may hold values from -64 to 64
- mlp_second: float32 [4, 2, 768, 3072], P('group', None, 'fsdp'), may hold values from 8.192 to 32.768
- mlp_outer: float32 [2, 768, 3072], P(None, 'fsdp'), may hold values from -0.125 to 0.125
- vector_weight: float32 [12, 768], P(None, 'fsdp'), may hold values from -0.9 to 1.75
- vector_first: float32 [4, 12, 768], P('group', None, 'fsdp'), may hold values from -64 to 64
- vector_second: float32 [4, 12, 768], P('group', None, 'fsdp'), may hold values from 8.192 to 32.768
- vector_outer: float32 [12, 768], P(None, 'fsdp'), may hold values from -1.25 to 1.25
Outputs:
- block_out: bfloat16 [4, 8192, 768], P('group', 'fsdp')
- input_grad: float32 [4, 8192, 768], P('group', 'fsdp')
- attn_moment: float32 [4, 768, 3072], P('group', 'fsdp')
- attn_square: float32 [4, 768, 3072], P('group', 'fsdp')
- attn_momentum: float32 [768, 3072], P('fsdp')
- attn_master: float32 [768, 3072], P('fsdp')
- mlp_moment: float32 [4, 2, 768, 3072], P('group', None, 'fsdp')
- mlp_square: float32 [4, 2, 768, 3072], P('group', None, 'fsdp')
- mlp_momentum: float32 [2, 768, 3072], P(None, 'fsdp')
- mlp_master: float32 [2, 768, 3072], P(None, 'fsdp')
- vector_moment: float32 [4, 12, 768], P('group', None, 'fsdp')
- vector_square: float32 [4, 12, 768], P('group', None, 'fsdp')
- vector_momentum: float32 [12, 768], P(None, 'fsdp')
- vector_master: float32 [12, 768], P(None, 'fsdp')
The draws below stay inside these ranges and needn't reach their ends.
Inputs may be any that keep to these rules, and one draw needn't show every extreme that they name: `segments`: segments of a packed row are numbered from 0 upwards, never falling; each has 1 to 32 tokens.
All inputs are finite; a program needn't handle non-finite values.
Results may differ from the reference program's by a relative error of at most 0.012.
Values may be sent and summed in bfloat16 or wider, within the bound.
A program may use at most 192 MiB of HBM per device.

```python
import math
import jax
import jax.numpy as jnp
import numpy as np
from jax import lax

D = 768
HEADS = 12
FF = 3072
SEQ = 64
TOK_DEV = 1024
STEP = 10
TOKENS = 8192
N_GROUP = 4
N_FSDP = 8


def draw_attn_weight(key, part):
    key = jax.random.fold_in(key, 11)
    base = jnp.clip(jax.random.normal(key, (D, 4 * D), jnp.float32), -5.0, 5.0)
    column = jnp.arange(4 * D)[None, :]
    factor = jnp.where(column >= 3 * D, 3.0, 1.0)
    return base * factor * D ** (-0.5)


def draw_vector_weight(key, part):
    key = jax.random.fold_in(key, 23)
    base = jnp.clip(jax.random.normal(key, (12, D), jnp.float32), -3.0, 3.0)
    row_idx = jnp.arange(12)[:, None]
    gain_row = (row_idx == 0) | (row_idx == 5)
    return jnp.where(gain_row, 1.0 + 0.25 * base, 0.3 * base)


def with_spikes(drawn, rng, source, target, shards_of, factor):
    def block_of(dim):
        return (jnp.arange(drawn.shape[dim]) // (drawn.shape[dim] // shards_of)).reshape((-1,) + (1,) * (drawn.ndim - 1 - dim))

    near = jax.random.permutation(rng, shards_of)[block_of(target)]
    other_side = (block_of(target) + shards_of // 2) % shards_of
    return jnp.where((block_of(source) == near) | (block_of(source) == other_side), factor * drawn, drawn)


def block_scale(rng, dims, cuts, least, top_value):
    def one(position, blocks):
        draws = jax.random.uniform(jax.random.fold_in(jax.random.fold_in(rng, 6), position), (blocks,), jnp.float32, least / len(cuts), top_value / len(cuts))
        return jnp.repeat(jnp.exp(draws), dims[position] // blocks).reshape((-1,) + (1,) * (len(dims) - position - 1))

    factor_of = one(*cuts[0])
    for cut in cuts[1:]:
        factor_of = factor_of * one(*cut)
    return factor_of


def length_profile(count, total, most, slope):
    loads = [(1 << 20) // math.isqrt(standing ** slope) + 1 for standing in range(2, count + 1)]
    spare, holding = total - most - (count - 1), [1] * (count - 1)
    while spare > 0:
        free = [i for i in range(count - 1) if holding[i] < most]
        mass, budget = sum([loads[i] for i in free]), spare
        for i in free:
            extra = min(most - holding[i], max(1, budget * loads[i] // mass), spare)
            holding[i] = holding[i] + extra
            spare = spare - extra
    return np.array([most] + holding)


def uneven_parts(rng, number_of, total, most, lean):
    if number_of == 2:
        one = jax.random.randint(rng, (), max(1, total - most), min(most, total - 1) + 1)
        return jnp.stack([one, total - one])
    lengths = jnp.asarray(length_profile(number_of, total, most, lean), jnp.int32)
    couples = (number_of - 1) // 2
    donor, receiver = lengths[1:1 + 2 * couples:2], lengths[2:2 + 2 * couples:2]
    margin = jnp.minimum(donor - 1, most - receiver)
    passed = jax.random.randint(jax.random.fold_in(rng, 1), (couples,), 0, 1 << 20) % (margin + 1)
    lengths = lengths.at[1:1 + 2 * couples:2].set(donor - passed).at[2:2 + 2 * couples:2].set(receiver + passed)
    return lengths[jax.random.permutation(jax.random.fold_in(rng, 2), number_of)]


def noise(key, shape, scale, reach, cuts=(), dtype=jnp.bfloat16):
    loudness = block_scale(key, shape, cuts, -0.22, 0.18) if cuts else 1.0
    values = jax.random.normal(key, shape, jnp.float32) * scale * loudness
    return jnp.minimum(jnp.maximum(values, -reach), reach).astype(dtype)


def noise_with(rng, dims, deviation, limit, split, heavy, held_as=jnp.bfloat16):
    array = deviation * jax.random.normal(rng, dims, jnp.float32)
    if split:
        array = array * block_scale(rng, dims, split, -0.22, 0.18)
    return jnp.clip(with_spikes(array, jax.random.fold_in(rng, 3), *heavy), -limit, limit).astype(held_as)


def setup_inputs(seed: int = 0) -> dict:
    key_list = jax.random.split(jax.random.key(seed), 16)
    return {
        "inputs": noise_with(key_list[0], (N_GROUP, TOKENS, D), 1.0, 6.0, ((0, 4), (1, 8)), (1, 2, 8, 2.0)),
        "segments": jax.vmap(lambda own: jnp.searchsorted(jnp.cumsum(uneven_parts(own, SEQ // 8, SEQ, SEQ // 2, 0)), jnp.arange(SEQ), side="right"))(jax.random.split(key_list[1], N_GROUP * (TOKENS // SEQ))).reshape((N_GROUP, TOKENS // SEQ, SEQ)).astype(jnp.int32),
        "cotangent": noise(key_list[2], (N_GROUP, TOKENS, D), 1.0, 6.0, ((0, 4), (1, 8))),
        "attn_weight": draw_attn_weight(jax.random.fold_in(key_list[15], 71), 0),
        "attn_first": noise(key_list[4], (N_GROUP, D, 4 * D), (0.11 * (TOK_DEV * N_FSDP) ** 0.5), 64.0, ((0, 4), (1, 8)), jnp.float32),
        "attn_second": jnp.clip(jnp.exp(math.log(32.768) - 1.3862944 * jax.random.uniform(key_list[5], (N_GROUP, D, 4 * D), jnp.float32) ** block_scale(key_list[5], (N_GROUP, D, 4 * D), ((0, 4), (1, 8)), -0.2, 0.2)), 8.192, 32.768),
        "attn_outer": noise(key_list[6], (D, 4 * D), 0.02, 0.125, ((0, 8),), jnp.float32),
        "mlp_weight": noise(key_list[7], (2, D, FF), D ** -0.5, 0.21875, ((1, 8),), jnp.float32),
        "mlp_first": noise(key_list[8], (N_GROUP, 2, D, FF), (0.11 * (TOK_DEV * N_FSDP) ** 0.5), 64.0, ((0, 4), (2, 8)), jnp.float32),
        "mlp_second": jnp.clip(jnp.exp(math.log(32.768) - 1.3862944 * jax.random.uniform(key_list[9], (N_GROUP, 2, D, FF), jnp.float32) ** block_scale(key_list[9], (N_GROUP, 2, D, FF), ((0, 4), (2, 8)), -0.2, 0.2)), 8.192, 32.768),
        "mlp_outer": noise(key_list[10], (2, D, FF), 0.02, 0.125, ((1, 8),), jnp.float32),
        "vector_weight": draw_vector_weight(jax.random.fold_in(key_list[15], 71), 0),
        "vector_first": noise(key_list[12], (N_GROUP, 12, D), (0.11 * (TOK_DEV * N_FSDP) ** 0.5), 64.0, ((0, 4), (2, 8)), jnp.float32),
        "vector_second": jnp.clip(jnp.exp(math.log(32.768) - 1.3862944 * jax.random.uniform(key_list[13], (N_GROUP, 12, D), jnp.float32) ** block_scale(key_list[13], (N_GROUP, 12, D), ((0, 4), (2, 8)), -0.2, 0.2)), 8.192, 32.768),
        "vector_outer": noise(key_list[14], (12, D), 0.2, 1.25, ((1, 8),), jnp.float32),
    }


@jax.custom_vjp
def low(v):
    return lax.optimization_barrier(v.astype(jnp.bfloat16)).astype(jnp.float32)

@jax.custom_vjp
def low_back(v):
    return v

def low_keep(v):
    return (low(v), None)

def low_pass(kept, grad):
    return (grad,)

def back_keep(v):
    return (v, None)

def back_low(kept, grad):
    return (low(grad),)
low.defvjp(low_keep, low_pass)
low_back.defvjp(back_keep, back_low)
EPS_NORM = 1e-05
BETA_ONE = 0.9
BETA_TWO = 0.999
ADAM_EPS = 1e-08
RATE_MATRIX = 0.05
RATE_VECTOR = 0.5
WEIGHT_DECAY = 0.1
OUTER_RATE = 0.7
OUTER_MOMENTUM = 0.9
NEG_LARGE = -1e+30

def product(left, right):
    return jnp.dot(left, right, precision=lax.Precision.HIGHEST, preferred_element_type=jnp.float32)

def norm_apply(values, gain, shift):
    centre = values - lax.optimization_barrier(jnp.mean(values, axis=-1, keepdims=True))
    spread = lax.optimization_barrier(jnp.mean(centre * centre, axis=-1, keepdims=True))
    return centre * lax.rsqrt(spread + EPS_NORM) * gain + shift

def layer(tokens_f, seg_ids, attn_full, mlp_full, vector_full):
    model_width = attn_full.shape[0]
    head_dim = model_width // HEADS
    score_scale = head_dim ** (-0.5)
    tok_count = tokens_f.shape[0]
    row_count = tok_count // SEQ
    shape_four = (row_count, SEQ, HEADS, head_dim)
    vectors = low(vector_full)
    attn_low = low(attn_full)
    mlp_low = low(mlp_full)
    normed = low(norm_apply(tokens_f, vectors[0], vectors[1]))
    project = product(normed, attn_low[:, :3 * model_width])
    queries = low_back(low(project[:, :model_width] + vectors[2]))
    keys_all = low_back(low(project[:, model_width:2 * model_width]))
    values_all = low_back(low(project[:, 2 * model_width:3 * model_width] + vectors[3]))
    scores = jnp.einsum('rqhd,rkhd->rhqk', queries.reshape(shape_four), keys_all.reshape(shape_four), precision=lax.Precision.HIGHEST) * score_scale
    scores = low_back(scores)
    same_seg = (seg_ids[:, :, None] == seg_ids[:, None, :])[:, None]
    masked = jnp.where(same_seg, scores, NEG_LARGE)
    exponent = jnp.exp(masked - lax.optimization_barrier(jnp.max(masked, axis=-1, keepdims=True)))
    soft = exponent / lax.optimization_barrier(jnp.sum(exponent, axis=-1, keepdims=True))
    probs = low(soft)
    mixed = jnp.einsum('rhqk,rkhd->rqhd', probs, values_all.reshape(shape_four), precision=lax.Precision.HIGHEST).reshape(tok_count, model_width)
    mixed = low_back(low(mixed))
    attended = low_back(product(mixed, attn_low[:, 3 * model_width:]) + vectors[4])
    residual = tokens_f + attended
    normed_two = low(norm_apply(residual, vectors[5], vectors[6]))
    up_pre = low_back(product(normed_two, mlp_low[0]) + vectors[8:12].reshape(-1))
    hidden = low(jax.nn.gelu(up_pre, approximate=True))
    branch = low_back(product(hidden, mlp_low[1].T) + vectors[7])
    return residual + branch

def adam_step(weight, first, second, gradient, step_rate, weight_decay):
    first_new = BETA_ONE * first + (1.0 - BETA_ONE) * gradient
    second_new = BETA_TWO * second + (1.0 - BETA_TWO) * gradient * gradient
    first_hat = first_new / (1.0 - BETA_ONE ** STEP)
    second_hat = second_new / (1.0 - BETA_TWO ** STEP)
    local_weight = weight - step_rate * (first_hat / (jnp.sqrt(second_hat) + ADAM_EPS) + weight_decay * weight)
    return (first_new, second_new, weight - local_weight)

def reference(inputs, segments, cotangent, attn_weight, attn_first, attn_second, attn_outer, mlp_weight, mlp_first, mlp_second, mlp_outer, vector_weight, vector_first, vector_second, vector_outer):
    block_tokens = min(4096, TOKENS)
    block_count = TOKENS // block_tokens
    weights = (attn_weight, mlp_weight, vector_weight)
    firsts = (attn_first, mlp_first, vector_first)
    seconds = (attn_second, mlp_second, vector_second)
    outers = (attn_outer, mlp_outer, vector_outer)
    rates = (RATE_MATRIX, RATE_MATRIX, RATE_VECTOR)
    decays = (WEIGHT_DECAY, WEIGHT_DECAY, 0.0)
    outs_all = []
    input_all = []
    moment_all = [[], [], []]
    square_all = [[], [], []]
    delta_sum = [jnp.zeros_like(w) for w in weights]
    for group_idx in range(N_GROUP):
        tokens_f = inputs[group_idx].astype(jnp.float32).reshape(block_count, block_tokens, D)
        seg_blocks = segments[group_idx].reshape(block_count, block_tokens // SEQ, SEQ)
        back_f = cotangent[group_idx].astype(jnp.float32).reshape(block_count, block_tokens, D)

        def one_block(totals, item):
            tok_block, seg_block, back_block = item

            def forward(tok_in, attn_in, mlp_in, vec_in):
                return layer(tok_in, seg_block, attn_in, mlp_in, vec_in)
            result, pull = jax.vjp(forward, tok_block, weights[0], weights[1], weights[2])
            grad_tok, grad_attn, grad_mlp, grad_vec = pull(back_block)
            totals = (totals[0] + grad_attn, totals[1] + grad_mlp, totals[2] + grad_vec)
            return (totals, (result.astype(jnp.bfloat16), grad_tok))
        start = tuple((jnp.zeros_like(w) for w in weights))
        totals, (out_blocks, grad_blocks) = lax.scan(one_block, start, (tokens_f, seg_blocks, back_f))
        outs_all.append(out_blocks.reshape(TOKENS, D))
        input_all.append(grad_blocks.reshape(TOKENS, D))
        for kind in range(3):
            first_new, second_new, delta = adam_step(weights[kind], firsts[kind][group_idx], seconds[kind][group_idx], totals[kind], rates[kind], decays[kind])
            moment_all[kind].append(first_new)
            square_all[kind].append(second_new)
            delta_sum[kind] = delta_sum[kind] + delta
    results = [jnp.stack(outs_all), jnp.stack(input_all)]
    for kind in range(3):
        mean_delta = delta_sum[kind] / N_GROUP
        momentum = OUTER_MOMENTUM * outers[kind] + mean_delta
        master = weights[kind] - OUTER_RATE * (mean_delta + OUTER_MOMENTUM * momentum)
        results.extend([jnp.stack(moment_all[kind]), jnp.stack(square_all[kind]), momentum, master])
    return (results[0], results[1], results[2], results[3], results[4], results[5], results[6], results[7], results[8], results[9], results[10], results[11], results[12], results[13])
```

```python
import jax
import jax.numpy as jnp
from jax import lax
from jax.sharding import PartitionSpec as P

HEADS = 12
SEQ = 64
STEP = 10


EPS_NORM = 1e-05
BETA_ONE = 0.9
BETA_TWO = 0.999
ADAM_EPS = 1e-08
RATE_MATRIX = 0.05
RATE_VECTOR = 0.5
WEIGHT_DECAY = 0.1
OUTER_RATE = 0.7
OUTER_MOMENTUM = 0.9
NEG_LARGE = -1e30


def norm_apply(values, gain, shift):
    centre = values - jnp.mean(values, axis=-1, keepdims=True)
    spread = jnp.mean(centre * centre, axis=-1, keepdims=True)
    return centre * lax.rsqrt(spread + EPS_NORM) * gain + shift


def gelu_tanh(values):
    return jax.nn.gelu(values, approximate=True)


def adam_step(weight, first, second, gradient, step_rate, weight_decay):
    first_new = BETA_ONE * first + (1.0 - BETA_ONE) * gradient
    second_new = BETA_TWO * second + (1.0 - BETA_TWO) * gradient * gradient
    first_hat = first_new / (1.0 - BETA_ONE**STEP)
    second_hat = second_new / (1.0 - BETA_TWO**STEP)
    local_weight = weight - step_rate * (
        first_hat / (jnp.sqrt(second_hat) + ADAM_EPS) + weight_decay * weight
    )
    return (first_new, second_new, weight - local_weight)


def local(
    inputs,
    segments,
    cotangent,
    attn_weight,
    attn_first,
    attn_second,
    attn_outer,
    mlp_weight,
    mlp_first,
    mlp_second,
    mlp_outer,
    vector_weight,
    vector_first,
    vector_second,
    vector_outer,
):
    bf16 = jnp.bfloat16
    f32 = jnp.float32
    attn_cast = attn_weight.astype(bf16)
    mlp_cast = mlp_weight.astype(bf16)
    attn_low, mlp_low, vector_low = (
        lax.all_gather(attn_cast, "fsdp", axis=0, tiled=True),
        lax.all_gather(mlp_cast, "fsdp", axis=1, tiled=True),
        lax.all_gather(vector_weight.astype(bf16), "fsdp", axis=1, tiled=True),
    )
    vectors = vector_low.astype(f32)
    tokens_f = inputs[0].astype(f32)
    seg_ids = segments[0]
    back_f = cotangent[0].astype(f32)
    model_width = attn_low.shape[0]
    head_dim = model_width // HEADS
    score_scale = head_dim ** (-0.5)
    tok_count = tokens_f.shape[0]
    row_count = tok_count // SEQ
    shape_four = (row_count, SEQ, HEADS, head_dim)
    normed_f, norm_pull = jax.vjp(norm_apply, tokens_f, vectors[0], vectors[1])
    normed = normed_f.astype(bf16)
    project = jnp.dot(normed, attn_low[:, : 3 * model_width], preferred_element_type=f32)
    queries = (project[:, :model_width] + vectors[2]).astype(bf16).reshape(shape_four)
    keys_all = project[:, model_width : 2 * model_width].astype(bf16).reshape(shape_four)
    values_all = (
        (project[:, 2 * model_width : 3 * model_width] + vectors[3])
        .astype(bf16)
        .reshape(shape_four)
    )
    scores = (
        jnp.einsum("rqhd,rkhd->rhqk", queries, keys_all, preferred_element_type=f32) * score_scale
    )
    same_seg = (seg_ids[:, :, None] == seg_ids[:, None, :])[:, None]
    masked = jnp.where(same_seg, scores, NEG_LARGE)
    exponent = jnp.exp(masked - jnp.max(masked, axis=-1, keepdims=True))
    soft = exponent / jnp.sum(exponent, axis=-1, keepdims=True)
    probs = soft.astype(bf16)
    mixed = (
        jnp.einsum("rhqk,rkhd->rqhd", probs, values_all, preferred_element_type=f32)
        .reshape(tok_count, model_width)
        .astype(bf16)
    )
    attended = (
        jnp.dot(mixed, attn_low[:, 3 * model_width :], preferred_element_type=f32) + vectors[4]
    )
    residual = tokens_f + attended
    normed_two_f, norm_two_pull = jax.vjp(norm_apply, residual, vectors[5], vectors[6])
    normed_two = normed_two_f.astype(bf16)
    up_pre = jnp.dot(normed_two, mlp_low[0], preferred_element_type=f32) + vectors[8:12].reshape(-1)
    hidden_f, gelu_pull = jax.vjp(gelu_tanh, up_pre)
    hidden = hidden_f.astype(bf16)
    branch = jnp.einsum("nf,df->nd", hidden, mlp_low[1], preferred_element_type=f32) + vectors[7]
    block_out = (residual + branch).astype(bf16)
    d_branch = cotangent[0]
    d_down_bias = jnp.sum(back_f, axis=0)
    grad_down = jnp.einsum("nd,nf->df", d_branch, hidden, preferred_element_type=f32)
    d_hidden = jnp.einsum("nd,df->nf", d_branch, mlp_low[1], preferred_element_type=f32)
    (d_up_f,) = gelu_pull(d_hidden)
    d_up = d_up_f.astype(bf16)
    d_up_bias = jnp.sum(d_up.astype(f32), axis=0)
    grad_up = jnp.einsum("nd,nf->df", normed_two, d_up, preferred_element_type=f32)
    mlp_grad = jnp.stack([grad_up, grad_down])
    d_normed_two = jnp.einsum("nf,df->nd", d_up, mlp_low[0], preferred_element_type=f32)
    d_res_norm, d_gain_two, d_shift_two = norm_two_pull(d_normed_two)
    d_res = back_f + d_res_norm
    d_att = d_res.astype(bf16)
    d_out_bias = jnp.sum(d_att.astype(f32), axis=0)
    grad_out = jnp.einsum("nc,nd->cd", mixed, d_att, preferred_element_type=f32)
    d_mixed = (
        jnp.einsum("nd,cd->nc", d_att, attn_low[:, 3 * model_width :], preferred_element_type=f32)
        .astype(bf16)
        .reshape(shape_four)
    )
    d_values = (
        jnp.einsum("rhqk,rqhd->rkhd", probs, d_mixed, preferred_element_type=f32)
        .reshape(tok_count, model_width)
        .astype(bf16)
    )
    d_probs = jnp.einsum("rqhd,rkhd->rhqk", d_mixed, values_all, preferred_element_type=f32)
    d_scores = (soft * (d_probs - jnp.sum(d_probs * soft, axis=-1, keepdims=True))).astype(bf16)
    d_queries = (
        (
            jnp.einsum("rhqk,rkhd->rqhd", d_scores, keys_all, preferred_element_type=f32)
            * score_scale
        )
        .reshape(tok_count, model_width)
        .astype(bf16)
    )
    d_keys = (
        (jnp.einsum("rhqk,rqhd->rkhd", d_scores, queries, preferred_element_type=f32) * score_scale)
        .reshape(tok_count, model_width)
        .astype(bf16)
    )
    d_query_bias = jnp.sum(d_queries.astype(f32), axis=0)
    d_value_bias = jnp.sum(d_values.astype(f32), axis=0)
    d_project = jnp.concatenate([d_queries, d_keys, d_values], axis=1)
    grad_qkv = jnp.einsum("nc,nd->cd", normed, d_project, preferred_element_type=f32)
    d_normed = jnp.einsum(
        "nd,cd->nc", d_project, attn_low[:, : 3 * model_width], preferred_element_type=f32
    )
    d_tok_norm, d_gain_one, d_shift_one = norm_pull(d_normed)
    input_grad = d_res + d_tok_norm
    attn_grad = jnp.concatenate([grad_qkv, grad_out], axis=1)
    vector_grad = jnp.concatenate(
        [
            jnp.stack(
                [
                    d_gain_one,
                    d_shift_one,
                    d_query_bias,
                    d_value_bias,
                    d_out_bias,
                    d_gain_two,
                    d_shift_two,
                    d_down_bias,
                ]
            ),
            d_up_bias.reshape(4, model_width),
        ],
        axis=0,
    )
    attn_sum, mlp_sum, vector_sum = (
        lax.psum_scatter(attn_grad.astype(bf16), "fsdp", scatter_dimension=0, tiled=True).astype(f32),
        lax.psum_scatter(mlp_grad.astype(bf16), "fsdp", scatter_dimension=1, tiled=True).astype(f32),
        lax.psum_scatter(vector_grad, "fsdp", scatter_dimension=1, tiled=True),
    )
    attn_moment, attn_square, attn_delta = adam_step(
        attn_weight, attn_first[0], attn_second[0], attn_sum, RATE_MATRIX, WEIGHT_DECAY
    )
    mlp_moment, mlp_square, mlp_delta = adam_step(
        mlp_weight, mlp_first[0], mlp_second[0], mlp_sum, RATE_MATRIX, WEIGHT_DECAY
    )
    vector_moment, vector_square, vector_delta = adam_step(
        vector_weight, vector_first[0], vector_second[0], vector_sum, RATE_VECTOR, 0.0
    )
    group_count = lax.axis_size("group")
    attn_total, mlp_total, vector_total = (
        lax.psum(attn_delta.astype(jnp.bfloat16), "group").astype(jnp.float32),
        lax.psum(mlp_delta.astype(jnp.bfloat16), "group").astype(jnp.float32),
        lax.psum(vector_delta.astype(jnp.bfloat16), "group").astype(jnp.float32),
    )
    attn_mean = attn_total / group_count
    mlp_mean = mlp_total / group_count
    vector_mean = vector_total / group_count
    attn_momentum = OUTER_MOMENTUM * attn_outer + attn_mean
    mlp_momentum = OUTER_MOMENTUM * mlp_outer + mlp_mean
    vector_momentum = OUTER_MOMENTUM * vector_outer + vector_mean
    attn_master = attn_weight - OUTER_RATE * (attn_mean + OUTER_MOMENTUM * attn_momentum)
    mlp_master = mlp_weight - OUTER_RATE * (mlp_mean + OUTER_MOMENTUM * mlp_momentum)
    vector_master = vector_weight - OUTER_RATE * (vector_mean + OUTER_MOMENTUM * vector_momentum)
    return (
        block_out[None],
        input_grad[None],
        attn_moment[None],
        attn_square[None],
        attn_momentum,
        attn_master,
        mlp_moment[None],
        mlp_square[None],
        mlp_momentum,
        mlp_master,
        vector_moment[None],
        vector_square[None],
        vector_momentum,
        vector_master,
    )


def solution(mesh):
    in_specs = (
        P("group", "fsdp", None),
        P("group", "fsdp", None),
        P("group", "fsdp", None),
        P("fsdp", None),
        P("group", "fsdp", None),
        P("group", "fsdp", None),
        P("fsdp", None),
        P(None, "fsdp", None),
        P("group", None, "fsdp", None),
        P("group", None, "fsdp", None),
        P(None, "fsdp", None),
        P(None, "fsdp"),
        P("group", None, "fsdp"),
        P("group", None, "fsdp"),
        P(None, "fsdp"),
    )
    out_specs = (
        P("group", "fsdp", None),
        P("group", "fsdp", None),
        P("group", "fsdp", None),
        P("group", "fsdp", None),
        P("fsdp", None),
        P("fsdp", None),
        P("group", None, "fsdp", None),
        P("group", None, "fsdp", None),
        P(None, "fsdp", None),
        P(None, "fsdp", None),
        P("group", None, "fsdp"),
        P("group", None, "fsdp"),
        P(None, "fsdp"),
        P(None, "fsdp"),
    )
    return jax.shard_map(local, mesh=mesh, in_specs=in_specs, out_specs=out_specs, check_vma=False)
```

```python
import functools

import jax
import jax.numpy as jnp
from jax import lax
from jax.experimental import pallas as pl
from jax.experimental.pallas import tpu as pltpu
from jax.sharding import PartitionSpec as P

EPS_NORM = 1e-05
NEG_LARGE = -1e30
HEADS = 12
SEQ = 64
STEP = 10
BETA_ONE = 0.9
BETA_TWO = 0.999
ADAM_EPS = 1e-08
RATE_MATRIX = 0.05
RATE_VECTOR = 0.5
WEIGHT_DECAY = 0.1
OUTER_RATE = 0.7
OUTER_MOMENTUM = 0.9


MESH = pl.DeviceIdType.MESH
BF = jnp.bfloat16
F32 = jnp.float32
D = 768
FF = 3072
T = 1024
TB = 256
SHARD = 96
GELU_C = 0.7978845608028654
GELU_A = 0.044715
SCALE = 0.125


def dot_nn(a, b):
    return jnp.dot(a, b, preferred_element_type=F32)


def dot_nt(a, b):
    return lax.dot_general(a, b, (((1,), (1,)), ((), ())), preferred_element_type=F32)


def dot_tn(a, b):
    return lax.dot_general(a, b, (((0,), (0,)), ((), ())), preferred_element_type=F32)


def coords():
    g = lax.axis_index("group")
    f = lax.axis_index("fsdp")
    return g // 2, g % 2, f // 2, f % 2


def dev(x, c, z, y):
    return (2 * x + c, 2 * z + y)


def remote(src, dst, ssem, rsem, to):
    return pltpu.make_async_remote_copy(
        src_ref=src, dst_ref=dst, send_sem=ssem, recv_sem=rsem, device_id=to, device_id_type=MESH
    )


def norm_parts(v):
    centre = v - jnp.mean(v, axis=-1, keepdims=True)
    spread = jnp.mean(centre * centre, axis=-1, keepdims=True)
    scale = lax.rsqrt(spread + EPS_NORM)
    return centre * scale, scale


def head_masks():
    lane = lax.broadcasted_iota(jnp.int32, (1, 128), 1)
    low = (lane < 64).astype(F32).astype(BF)
    high = (lane >= 64).astype(F32).astype(BF)
    return low, high


def segment_bias(seg_ref, i):
    row = seg_ref[pl.ds(i, 1), :]
    classes = lax.broadcasted_iota(jnp.int32, (16, 128), 0)
    hot = (classes == row).astype(F32).astype(BF)
    same = dot_tn(hot, hot)
    bias = (same - 1.0) * (-NEG_LARGE)
    return jnp.concatenate([bias, bias], axis=1)


def soft_pair(q, k2, bias):
    s = dot_nt(q, k2) * SCALE + bias
    halves = []
    for h in (0, 1):
        part = s[:, 128 * h : 128 * h + 128]
        e = jnp.exp(part - jnp.max(part, axis=-1, keepdims=True))
        halves.append(e * (1.0 / jnp.sum(e, axis=-1, keepdims=True)))
    return jnp.concatenate(halves, axis=1)


def stack_heads(v, low, high):
    return jnp.concatenate([v * low, v * high], axis=0)


def gather_stages(w, sems, where):
    x, c, z, y = where
    ys, yr, us, ds, zr, xs, xr, cs, cr = sems
    f = 2 * z + y
    other = 2 * z + 1 - y

    def rows(i):
        return pl.ds(pl.multiple_of(i * SHARD, 32), SHARD)

    def pair(i):
        return pl.ds(pl.multiple_of(i * 2 * SHARD, 64), 2 * SHARD)

    mine = 2 * x + c
    across = 2 * (1 - x) + c
    sib = 2 * x + 1 - c
    sib_across = 2 * (1 - x) + 1 - c

    def at(p, r, q):
        return w.at[p // 2, r, pl.ds(pl.multiple_of(1536 * (p % 2) + 384 * q, 128), 384)]

    def cp_y(p, r):
        return remote(at(p, r, mine), at(p, r, mine), ys.at[p], yr.at[p], dev(x, c, z, 1 - y))

    def cp_up(p, i):
        return remote(at(p, pair(i), mine), at(p, pair(i), mine), us.at[p, i], zr.at[p, i], dev(x, c, z + 1, y))

    def cp_down(p, i):
        return remote(at(p, pair(i), mine), at(p, pair(i), mine), ds.at[p, i], zr.at[p, i], dev(x, c, z - 1, y))

    def cp_x(p, r, i, q):
        return remote(at(p, r, q), at(p, r, q), xs.at[p, i], xr.at[p, i], dev(1 - x, c, z, y))

    def cp_c(p, r, i, q, k):
        return remote(at(p, r, q), at(p, r, q), cs.at[p, 4 * k + i], cr.at[p, 4 * k + i], dev(x, 1 - c, z, y))

    def others(fn):
        for k in (1, 2, 3):
            pl.when(z >= k)(functools.partial(fn, z - k))
            pl.when(z + k <= 3)(functools.partial(fn, z + k))

    def sa(p):
        cp_y(p, rows(f)).start()

    def sb(p):
        cp_y(p, rows(other)).wait_recv()
        pl.when(z < 3)(lambda: cp_up(p, z).start())
        pl.when(z > 0)(lambda: cp_down(p, z).start())
        cp_x(p, rows(other), z, mine).start()
        cp_c(p, rows(other), z, mine, 0).start()

    def hop(k, p):
        def from_below():
            i = z - k
            cp_up(p, i).wait_recv()
            pl.when(z < 3)(lambda: cp_up(p, i).start())
            cp_x(p, pair(i), i, mine).start()
            cp_c(p, pair(i), i, mine, 0).start()

        def from_above():
            i = z + k
            cp_down(p, i).wait_recv()
            pl.when(z > 0)(lambda: cp_down(p, i).start())
            cp_x(p, pair(i), i, mine).start()
            cp_c(p, pair(i), i, mine, 0).start()

        pl.when(z >= k)(from_below)
        pl.when(z + k <= 3)(from_above)

    def sf(p):
        cp_x(p, rows(other), z, across).wait_recv()
        cp_c(p, rows(other), z, across, 1).start()

        def fwd(i):
            cp_x(p, pair(i), i, across).wait_recv()
            cp_c(p, pair(i), i, across, 1).start()

        others(fwd)

    def sg(p):
        cp_c(p, rows(other), z, sib, 0).wait_recv()
        cp_c(p, rows(other), z, sib_across, 1).wait_recv()

        def got(i):
            cp_c(p, pair(i), i, sib, 0).wait_recv()
            cp_c(p, pair(i), i, sib_across, 1).wait_recv()

        others(got)

    def drain(p):
        cp_y(p, rows(f)).wait_send()
        pl.when(z < 3)(lambda: cp_up(p, z).wait_send())
        pl.when(z > 0)(lambda: cp_down(p, z).wait_send())
        cp_x(p, rows(other), z, mine).wait_send()
        cp_c(p, rows(other), z, mine, 0).wait_send()
        cp_c(p, rows(other), z, across, 1).wait_send()
        for k in (1, 2, 3):

            @pl.when(z >= k)
            def _():
                pl.when(z < 3)(lambda: cp_up(p, z - k).wait_send())

            @pl.when(z + k <= 3)
            def _():
                pl.when(z > 0)(lambda: cp_down(p, z + k).wait_send())

        def sent(i):
            cp_x(p, pair(i), i, mine).wait_send()
            cp_c(p, pair(i), i, mine, 0).wait_send()
            cp_c(p, pair(i), i, across, 1).wait_send()

        others(sent)

    stages = [sa, sb, functools.partial(hop, 1), functools.partial(hop, 2), functools.partial(hop, 3), sf, sg]
    return stages, drain


GATHER_SEMS = lambda n: [
    pltpu.SemaphoreType.DMA((n,)),
    pltpu.SemaphoreType.DMA((n,)),
    pltpu.SemaphoreType.DMA((n, 4)),
    pltpu.SemaphoreType.DMA((n, 4)),
    pltpu.SemaphoreType.DMA((n, 4)),
    pltpu.SemaphoreType.DMA((n, 4)),
    pltpu.SemaphoreType.DMA((n, 4)),
    pltpu.SemaphoreType.DMA((n, 8)),
    pltpu.SemaphoreType.DMA((n, 8)),
]
PIECES = 6


def forward_kernel(
    x_in, cot_in, seg_in, aw, mw, vw,
    w_out, qkvm_out, hid_out, gp_out, nrm_out, n2_out, res_out, xv_out, cotv_out, vec_out, seg_out,
    w, xv, nrm, qkvm, res, n2, hid, gp, vec, seg, tiles, ub,
    xsnd, xrcv, csnd, crcv, gsnd, grcv, vsnd, vrcv, osem,
    *gsems,
):
    where = coords()
    x, c, z, y = where
    f = 2 * z + y
    swapped = c != y
    partner = dev(x, y, z, c)

    barrier = pltpu.get_barrier_semaphore()

    def greet(to):
        pl.semaphore_signal(barrier, inc=1, device_id=to, device_id_type=MESH)

    for k in range(1, 8):
        greet((2 * x + c, (f + k) % 8))
    greet(dev(x, 1 - c, z, y))
    greet(dev(1 - x, c, z, y))
    pl.when(swapped)(lambda: greet(partner))

    own = pl.ds(pl.multiple_of(f * SHARD, 32), SHARD)
    w[0, own, :] = aw[...].astype(BF)
    w[1, own, :] = mw[0].astype(BF)
    w[2, own, :] = mw[1].astype(BF)
    tiles[pl.ds(f, 1)] = jnp.zeros((1, 16, 128), F32)
    tiles[f, 0:12, 0:SHARD] = vw[...].astype(BF).astype(F32)

    pl.semaphore_wait(barrier, 9 + swapped.astype(jnp.int32))

    stages, drain = gather_stages(w, gsems, where)

    def cp_vec(k, j):
        return remote(tiles.at[j], tiles.at[j], vsnd.at[k - 1], vrcv.at[k - 1], (2 * x + c, (f + k) % 8))

    def tok(b):
        return pl.ds(pl.multiple_of(b * TB, TB), TB)

    def x_remote(b):
        return remote(x_in.at[tok(b)], xv.at[tok(b)], xsnd.at[b], xrcv.at[b], partner)

    def x_local(b):
        return pltpu.make_async_copy(x_in.at[tok(b)], xv.at[tok(b)], xrcv.at[b])

    def cot_remote():
        return remote(cot_in, cotv_out, csnd, crcv, partner)

    def cot_local():
        return pltpu.make_async_copy(cot_in, cotv_out, crcv)

    def seg_remote():
        return remote(seg_in, seg, gsnd, grcv, partner)

    stages[0](0)
    for k in range(1, 8):
        cp_vec(k, f).start()

    @pl.when(swapped)
    def _():
        seg_remote().start()
        for b in range(4):
            x_remote(b).start()

    @pl.when(jnp.logical_not(swapped))
    def _():
        seg[...] = seg_in[...]
        for b in range(4):
            x_local(b).start()

    outs = []

    def write(src, dst):
        cp = pltpu.make_async_copy(src, dst, osem.at[len(outs)])
        cp.start()
        outs.append(cp)

    def tick(slot):
        for p in range(PIECES):
            s = slot - 2 * p
            if 0 <= s <= 6 and (p, s) != (0, 0):
                stages[s](p)
                if s == 6 and p % 2 == 1:
                    write(w.at[p // 2], w_out.at[p // 2])

    def vectors():
        for k in range(1, 8):
            cp_vec(k, (f + 8 - k) % 8).wait_recv()
        total = jnp.zeros((16, D), F32)
        r = lax.broadcasted_iota(jnp.int32, (128, D), 0)
        q = lax.broadcasted_iota(jnp.int32, (128, D), 1)
        for j in range(8):
            pick = jnp.logical_and(q == r + SHARD * j, r < SHARD).astype(F32).astype(BF)
            total = total + dot_nn(tiles[j].astype(BF), pick)
        vec[...] = total
        for k in range(4):
            ub[0:1, D * k : D * k + D] = total[8 + k : 9 + k, :]

    def first_norm(b):
        @pl.when(swapped)
        def _():
            x_remote(b).wait_recv()

        @pl.when(jnp.logical_not(swapped))
        def _():
            x_local(b).wait()

        hat, _ = norm_parts(xv[tok(b), :].astype(F32))
        nrm[tok(b), :] = (hat * vec[0:1, :] + vec[1:2, :]).astype(BF)

    def blocks(fn):
        def step(b, carry):
            fn(b)
            return carry

        lax.fori_loop(0, 4, step, 0)

    def queries_keys(b):
        r = dot_nn(nrm[tok(b), :], w[0, :, 0:1536])
        qkvm[tok(b), 0:D] = (r[:, 0:D] + vec[2:3, :]).astype(BF)
        qkvm[tok(b), D : 2 * D] = r[:, D : 2 * D].astype(BF)

    def values(b):
        r = dot_nn(nrm[tok(b), :], w[0, :, 1536:2304])
        qkvm[tok(b), 2 * D : 3 * D] = (r + vec[3:4, :]).astype(BF)

    def attention(i):
        low, high = head_masks()
        bias = segment_bias(seg, i)
        r = pl.ds(pl.multiple_of(i * 128, 128), 128)
        for p in range(6):
            col = 128 * p
            q = qkvm[r, col : col + 128]
            k2 = stack_heads(qkvm[r, D + col : D + col + 128], low, high)
            v2 = stack_heads(qkvm[r, 2 * D + col : 2 * D + col + 128], low, high)
            probs = soft_pair(q, k2, bias).astype(BF)
            qkvm[r, 3 * D + col : 3 * D + col + 128] = dot_nn(probs, v2).astype(BF)

    def attend(lo, hi):
        def step(i, carry):
            attention(i)
            return carry

        lax.fori_loop(lo, hi, step, 0)

    def out_norm(b):
        att = dot_nn(qkvm[tok(b), 3 * D :], w[0, :, 2304:3072]) + vec[4:5, :]
        r = xv[tok(b), :].astype(F32) + att
        res[tok(b), :] = r
        hat, _ = norm_parts(r)
        n2[tok(b), :] = (hat * vec[5:6, :] + vec[6:7, :]).astype(BF)

    def up(half, b):
        for k in range(2):
            lo = 1536 * half + 768 * k
            u = dot_nn(n2[tok(b), :], w[1, :, lo : lo + 768]) + ub[0:1, lo : lo + 768]
            u2 = u * u
            t = jnp.tanh(u * (GELU_C + (GELU_C * GELU_A) * u2))
            h = 0.5 + 0.5 * t
            out = u * h
            hid[tok(b), lo : lo + 768] = out.astype(BF)
            slope = h + out * (1.0 - h) * (2.0 * GELU_C + (6.0 * GELU_C * GELU_A) * u2)
            gp[tok(b), lo : lo + 768] = slope.astype(BF)

    for slot in range(0, 4):
        tick(slot)
    vectors()
    blocks(first_norm)

    @pl.when(swapped)
    def _():
        cot_remote().start()

    @pl.when(jnp.logical_not(swapped))
    def _():
        cot_local().start()

    tick(4)
    tick(5)
    write(xv, xv_out)
    write(nrm, nrm_out)
    tick(6)
    blocks(queries_keys)
    tick(7)
    tick(8)
    blocks(values)

    @pl.when(swapped)
    def _():
        remote(seg_in, seg, gsnd, grcv, partner).wait_recv()

    attend(0, 4)
    tick(9)
    attend(4, 8)
    write(qkvm, qkvm_out)
    tick(10)
    blocks(out_norm)
    write(res, res_out)
    write(n2, n2_out)
    tick(11)
    blocks(functools.partial(up, 0))
    tick(12)
    blocks(functools.partial(up, 1))
    write(hid, hid_out)
    write(gp, gp_out)
    for slot in range(13, 2 * PIECES + 5):
        tick(slot)
    vec_out[...] = vec[...]
    seg_out[...] = seg[...]

    for p in range(PIECES):
        drain(p)
    for k in range(1, 8):
        cp_vec(k, f).wait_send()

    @pl.when(swapped)
    def _():
        seg_remote().wait_send()
        for b in range(4):
            x_remote(b).wait_send()
        cot_remote().wait()

    @pl.when(jnp.logical_not(swapped))
    def _():
        cot_local().wait()

    for cp in outs:
        cp.wait()


def forward(x, cot, seg, aw, mw, vw):
    any_ = pl.BlockSpec(memory_space=pl.ANY)
    vm = pl.BlockSpec(memory_space=pltpu.VMEM)
    wide = jax.ShapeDtypeStruct((T, FF), BF)
    slim = jax.ShapeDtypeStruct((T, D), BF)
    dma = pltpu.SemaphoreType.DMA
    return pl.pallas_call(
        forward_kernel,
        out_shape=(
            jax.ShapeDtypeStruct((3, D, FF), BF), wide, wide, wide, slim, slim,
            jax.ShapeDtypeStruct((T, D), F32), slim, slim,
            jax.ShapeDtypeStruct((16, D), F32), jax.ShapeDtypeStruct((8, 128), jnp.int32),
        ),
        in_specs=[any_, any_, vm, vm, vm, vm],
        out_specs=(any_,) * 9 + (vm, vm),
        scratch_shapes=[
            pltpu.VMEM((3, D, FF), BF), pltpu.VMEM((T, D), BF), pltpu.VMEM((T, D), BF), pltpu.VMEM((T, FF), BF),
            pltpu.VMEM((T, D), F32), pltpu.VMEM((T, D), BF), pltpu.VMEM((T, FF), BF), pltpu.VMEM((T, FF), BF),
            pltpu.VMEM((16, D), F32), pltpu.VMEM((8, 128), jnp.int32), pltpu.VMEM((8, 16, 128), F32),
            pltpu.VMEM((1, FF), F32),
            dma((4,)), dma((4,)), dma, dma, dma, dma, dma((7,)), dma((7,)), dma((12,)),
            *GATHER_SEMS(PIECES),
        ],
        compiler_params=pltpu.CompilerParams(collective_id=1, has_side_effects=True, vmem_limit_bytes=60 * 2**20),
        name="forward",
    )(x, cot, seg, aw, mw, vw)


RS = 12
RING = 2


def adam_parts(first, second, weight, gradient, rate, decay):
    first_new = BETA_ONE * first + (1.0 - BETA_ONE) * gradient
    second_new = BETA_TWO * second + (1.0 - BETA_TWO) * gradient * gradient
    first_hat = first_new * (1.0 / (1.0 - BETA_ONE**STEP))
    second_hat = second_new * (1.0 / (1.0 - BETA_TWO**STEP))
    delta = rate * (first_hat / (jnp.sqrt(second_hat) + ADAM_EPS) + decay * weight)
    return first_new, second_new, delta


def backward_kernel(
    w_in, qkvm_in, hid_in, gp_in, nrm_in, n2_in, res_in, xv_in, cotv_in, vec, seg,
    aw, a1, a2, ao, mw, m1, m2, mo, vw, v1, v2, vo,
    out_o, ig_o, am_o, as_o, ap_o, aq_o, mm_o, ms_o, mp_o, mq_o, vm_o, vs_o, vp_o, vq_o,
    A, B, W, cot, n2, E, R, G, S, ZI, FIN, DL, IN, OUT, vg, ubs, vsl, vrc, vdl,
    lsem, d2s, d2r, zs, zr, fs, fr, ls, lr, isem, osem, bos, bor, igs, igr, vss, vsr, vds, vdr,
):
    x, c, z, y = coords()
    f = 2 * z + y
    g = 2 * x + c
    swapped = c != y
    kept = jnp.logical_not(swapped)
    partner = dev(x, y, z, c)

    barrier = pltpu.get_barrier_semaphore()

    def greet(to):
        pl.semaphore_signal(barrier, inc=1, device_id=to, device_id_type=MESH)

    me16 = c * 8 + f
    for k in range(1, 16):
        other = (me16 + k) % 16
        greet((2 * x + other // 8, other % 8))
    greet(dev(1 - x, c, z, y))
    greet(dev(1 - x, 1 - c, z, y))

    def tok(b):
        return pl.ds(pl.multiple_of(b * TB, TB), TB)

    def load(src, dst, k):
        return pltpu.make_async_copy(src, dst, lsem.at[k])

    ld_cot = load(cotv_in, cot, 0)
    ld_hid = load(hid_in, A, 1)
    ld_wd = load(w_in.at[2], W, 2)
    ld_gp = load(gp_in, B, 3)
    ld_res = load(res_in, R, 4)
    ld_n2 = load(n2_in, n2, 5)
    ld_wu = load(w_in.at[1], W, 6)
    ld_wa = load(w_in.at[0], W, 7)
    ld_qkvm = load(qkvm_in, A, 8)
    ld_nrm = load(nrm_in, E, 9)
    ld_xv = load(xv_in, cot, 10)
    for cp in (ld_cot, ld_hid, ld_wd, ld_gp, ld_res, ld_n2):
        cp.start()
    vg[...] = jnp.zeros((16, D), F32)
    vsl[...] = jnp.zeros((8, 16, 128), F32)
    vdl[...] = jnp.zeros((4, 16, 128), F32)
    pl.semaphore_wait(barrier, 17)

    def blocks(fn, lo=0, hi=4):
        def step(b, carry):
            fn(b)
            return carry

        lax.fori_loop(lo, hi, step, 0)

    def wide(i, n=768):
        return pl.ds(pl.multiple_of(i * n, 128), n)

    ones = jnp.ones((16, T), BF)

    def gradient(lhs, rhs, slot):
        out = dot_tn(lhs, rhs)
        for j in range(8):
            G[slot, j % 2, j // 2] = out[SHARD * j : SHARD * j + SHARD].astype(BF)

    def t_down(v):
        @pl.when(v == 0)
        def _():
            ld_cot.wait()
            ld_hid.wait()
            vg[7:8, :] = dot_nn(ones, cot[...])[0:1, :]

        gradient(cot[...], A[:, wide(v)], v % RING)

    def out_remote(b):
        return remote(E.at[tok(b)], out_o.at[tok(b)], bos.at[b], bor.at[b], partner)

    def out_local(b):
        return pltpu.make_async_copy(E.at[tok(b)], out_o.at[tok(b)], bor.at[b])

    def mlp_back(b):
        for k in range(4):
            lo = 768 * k
            dh = dot_nn(cot[tok(b), :], W[:, lo : lo + 768])
            B[tok(b), lo : lo + 768] = (dh * B[tok(b), lo : lo + 768].astype(F32)).astype(BF)
        branch = dot_nt(A[tok(b), :], W[...])
        E[tok(b), :] = (R[tok(b), :] + branch + vec[7:8, :]).astype(BF)
        pl.when(swapped)(lambda: out_remote(b).start())
        pl.when(kept)(lambda: out_local(b).start())

    def t_mlp0():
        ld_wd.wait()
        ld_gp.wait()
        ld_res.wait()
        blocks(mlp_back, 0, 2)

    def t_mlp1():
        blocks(mlp_back, 2, 4)
        ld_wu.start()
        ld_qkvm.start()
        ld_n2.wait()

    def t_up(v):
        u = v - 6
        ubs[0:1, wide(u)] = dot_nn(ones, B[:, wide(u)])[0:1, :]
        gradient(n2[...], B[:, wide(u)], v % RING)

    def norm_back(dn, v, gain):
        hat, scale = norm_parts(v)
        e = dn * gain
        d = (e - jnp.mean(e, axis=-1, keepdims=True) - hat * jnp.mean(e * hat, axis=-1, keepdims=True)) * scale
        return d, jnp.sum(dn * hat, axis=0, keepdims=True), jnp.sum(dn, axis=0, keepdims=True)

    def second_norm(b):
        dn = dot_nt(B[tok(b), :], W[...])
        d, dgain, dshift = norm_back(dn, R[tok(b), :], vec[5:6, :])
        d = d + cot[tok(b), :].astype(F32)
        R[tok(b), :] = d
        B[tok(b), 3 * D :] = d.astype(BF)
        vg[5:6, :] = vg[5:6, :] + dgain
        vg[6:7, :] = vg[6:7, :] + dshift

    def t_norm2():
        for k in range(4):
            vg[8 + k : 9 + k, :] = ubs[0:1, D * k : D * k + D]
        ld_wu.wait()
        blocks(second_norm)
        ld_wa.start()
        ld_xv.start()
        for b in range(4):
            pl.when(swapped)(lambda: out_remote(b).wait_send())
            pl.when(kept)(lambda: out_local(b).wait())
        ld_nrm.start()

    def mixed_back(b):
        A[tok(b), 3 * D :] = dot_nt(B[tok(b), 3 * D :], W[:, 3 * D :]).astype(BF)

    def t_out():
        ld_qkvm.wait()
        vg[4:5, :] = dot_nn(ones, B[:, 3 * D :])[0:1, :]
        gradient(A[:, 3 * D :], B[:, 3 * D :], 8 % RING)
        ld_wa.wait()
        blocks(mixed_back)

    def attention_back(i):
        low, high = head_masks()
        lane = lax.broadcasted_iota(jnp.int32, (1, 128), 1) < 64
        bias = segment_bias(seg, i)
        r = pl.ds(pl.multiple_of(i * 128, 128), 128)
        for p in range(6):
            col = 128 * p
            q = A[r, col : col + 128]
            k2 = stack_heads(A[r, D + col : D + col + 128], low, high)
            v2 = stack_heads(A[r, 2 * D + col : 2 * D + col + 128], low, high)
            dm = A[r, 3 * D + col : 3 * D + col + 128]
            soft = soft_pair(q, k2, bias)
            dp = dot_nt(dm, v2)
            both = dot_tn(soft.astype(BF), dm)
            B[r, 2 * D + col : 2 * D + col + 128] = jnp.where(lane, both[:128], both[128:]).astype(BF)
            halves = []
            for h in (0, 1):
                part = dp[:, 128 * h : 128 * h + 128]
                so = soft[:, 128 * h : 128 * h + 128]
                halves.append(so * (part - jnp.sum(part * so, axis=-1, keepdims=True)))
            ds = jnp.concatenate(halves, axis=1).astype(BF)
            B[r, col : col + 128] = (dot_nn(ds, k2) * SCALE).astype(BF)
            both = dot_tn(ds, q) * SCALE
            B[r, D + col : D + col + 128] = jnp.where(lane, both[:128], both[128:]).astype(BF)

    def t_att(v):
        lo = (v - 12) * 4
        blocks(lambda i: attention_back(lo + i))

    def t_qkv(v):
        u = v - 14

        @pl.when(u == 0)
        def _():
            ld_nrm.wait()
            vg[2:3, :] = dot_nn(ones, B[:, 0:D])[0:1, :]
            vg[3:4, :] = dot_nn(ones, B[:, 2 * D : 3 * D])[0:1, :]

        gradient(E[...], B[:, wide(u)], (v - 5) % RING)

    def ig_remote(b):
        return remote(R.at[tok(b)], ig_o.at[tok(b)], igs.at[b], igr.at[b], partner)

    def ig_local(b):
        return pltpu.make_async_copy(R.at[tok(b)], ig_o.at[tok(b)], igr.at[b])

    def first_norm_back(b):
        dn = dot_nt(B[tok(b), : 3 * D], W[:, : 3 * D])
        d, dgain, dshift = norm_back(dn, cot[tok(b), :].astype(F32), vec[0:1, :])
        R[tok(b), :] = R[tok(b), :] + d
        vg[0:1, :] = vg[0:1, :] + dgain
        vg[1:2, :] = vg[1:2, :] + dshift
        pl.when(swapped)(lambda: ig_remote(b).start())
        pl.when(kept)(lambda: ig_local(b).start())

    def cp_slice(j):
        return remote(vsl.at[j], vrc.at[2 * z + c], vss.at[j], vsr.at[2 * z + c], (2 * x + y, j))

    def each_slice(fn):
        def step(j, carry):
            pl.when(jnp.logical_or(swapped, j != f))(lambda: fn(j))
            return carry

        lax.fori_loop(0, 8, step, 0)

    def t_norm1():
        ld_xv.wait()
        blocks(first_norm_back)
        for j in range(8):
            vsl[j, :, 0:SHARD] = vg[:, SHARD * j : SHARD * j + SHARD]

        @pl.when(kept)
        def _():
            vrc[pl.ds(2 * z + c, 1)] = vsl[pl.ds(f, 1)]

        each_slice(lambda j: cp_slice(j).start())

    def cp_change(k):
        return remote(vdl.at[g], vdl.at[g], vds.at[k], vdr.at[g], members[k])

    def t_vec_adam():
        def step(s, carry):
            pl.when(jnp.logical_or(swapped, s != 2 * z + c))(
                lambda: remote(vrc.at[s], vrc.at[s], vss.at[0], vsr.at[s], partner).wait_recv()
            )
            return carry

        lax.fori_loop(0, 8, step, 0)
        grad = jnp.sum(vrc[...], axis=0)[0:12, 0:SHARD]
        mom, sq, delta = adam_parts(v1[...], v2[...], vw[...], grad, RATE_VECTOR, 0.0)
        vm_o[...] = mom
        vs_o[...] = sq
        vdl[g, 0:12, 0:SHARD] = delta
        for k in range(3):
            cp_change(k).start()

    def t_vec_outer():
        for k in range(3):
            remote(vdl.at[froms[k]], vdl.at[froms[k]], vds.at[k], vdr.at[froms[k]], members[k]).wait_recv()
        mean = jnp.sum(vdl[...], axis=0)[0:12, 0:SHARD] * 0.25
        mom = OUTER_MOMENTUM * vo[...] + mean
        vp_o[...] = mom
        vq_o[...] = vw[...] - OUTER_RATE * (mean + OUTER_MOMENTUM * mom)

    members = [dev(x, 1 - c, z, y), dev(1 - x, c, z, y), dev(1 - x, 1 - c, z, y)]
    froms = [2 * x + 1 - c, 2 * (1 - x) + c, 2 * (1 - x) + 1 - c]

    def tasks(v):
        pl.when(v < 4)(lambda: t_down(v))
        pl.when(v == 4)(t_mlp0)
        pl.when(v == 5)(t_mlp1)
        pl.when(jnp.logical_and(v >= 6, v <= 9))(lambda: t_up(v))
        pl.when(v == 10)(t_norm2)
        pl.when(v == 11)(t_out)
        pl.when(jnp.logical_and(v >= 12, v <= 13))(lambda: t_att(v))
        pl.when(jnp.logical_and(v >= 14, v <= 16))(lambda: t_qkv(v))
        pl.when(v == 17)(t_norm1)
        pl.when(v == 19)(t_vec_adam)
        pl.when(v == 21)(t_vec_outer)

    def piece(v):
        first = jnp.logical_and(v >= 0, v < 4)
        second = jnp.logical_and(v >= 6, v < 10)
        third = v == 11
        fourth = jnp.logical_and(v >= 14, v < 17)
        real = jnp.logical_or(jnp.logical_or(first, second), jnp.logical_or(third, fourth))
        p = jnp.where(v < 4, v, jnp.where(v < 10, v - 2, jnp.where(v < 12, 8, v - 5)))
        return real, p

    def cp_core(p):
        return remote(G.at[p % RING, 1 - c], S.at[p], d2s.at[p], d2r.at[p], dev(x, 1 - c, z, y))

    def hop_up(p, t, k):
        return remote(S.at[p, t], ZI.at[p, t - z - 1], zs.at[p, k], zr.at[p, t - z - 1], dev(x, c, z + 1, y))

    def hop_down(p, t, k):
        return remote(S.at[p, t], ZI.at[p, 5 - z + t], zs.at[p, k], zr.at[p, 5 - z + t], dev(x, c, z - 1, y))

    def got(p, k):
        remote(ZI.at[p, k], ZI.at[p, k], zs.at[p, 0], zr.at[p, k], partner).wait_recv()

    def add_in(p, t, k):
        got(p, k)
        S[p, t] = (S[p, t].astype(F32) + ZI[p, k].astype(F32)).astype(BF)

    def s0(p):
        cp_core(p).start()

    def s1(p):
        cp_core(p).wait_recv()
        for t in range(4):
            S[p, t] = (S[p, t].astype(F32) + G[p % RING, c, t].astype(F32)).astype(BF)

        @pl.when(z == 0)
        def _():
            for k, t in enumerate((3, 2, 1)):
                hop_up(p, t, k).start()

        @pl.when(z == 3)
        def _():
            for k, t in enumerate((0, 1, 2)):
                hop_down(p, t, k).start()

        cp_core(p).wait_send()

    def s2(p):
        @pl.when(z == 1)
        def _():
            for k, t in enumerate((3, 2)):
                add_in(p, t, t - 1)
                hop_up(p, t, k).start()

        @pl.when(z == 2)
        def _():
            for k, t in enumerate((0, 1)):
                add_in(p, t, 2 + t)
                hop_down(p, t, k).start()

    def s3(p):
        @pl.when(z == 2)
        def _():
            add_in(p, 3, 1)
            hop_up(p, 3, 2).start()

        @pl.when(z == 1)
        def _():
            add_in(p, 0, 3)
            hop_down(p, 0, 2).start()

    def cp_final(p):
        return remote(S.at[p, z], FIN.at[p], fs.at[p], fr.at[p], partner)

    def col(p):
        return pl.ds(pl.multiple_of(768 * jnp.where(p < 8, p % 4, (p + 3) % 4), 128), 768)

    def state_loads(p, fn):
        q = p % 2

        @pl.when(p < 8)
        def _():
            m = 1 - p // 4
            for k, src in enumerate((m1, m2, mw, mo)):
                fn(pltpu.make_async_copy(src.at[m, :, col(p)], IN.at[q, k], isem.at[q, k]))

        @pl.when(p >= 8)
        def _():
            for k, src in enumerate((a1, a2, aw, ao)):
                fn(pltpu.make_async_copy(src.at[:, col(p)], IN.at[q, k], isem.at[q, k]))

    def state_stores(p, ks, fn):
        q = p % 2

        @pl.when(p < 8)
        def _():
            m = 1 - p // 4
            for k in ks:
                dst = (mm_o, ms_o, mp_o, mq_o)[k]
                fn(pltpu.make_async_copy(OUT.at[q, k], dst.at[m, :, col(p)], osem.at[q, k]))

        @pl.when(p >= 8)
        def _():
            for k in ks:
                dst = (am_o, as_o, ap_o, aq_o)[k]
                fn(pltpu.make_async_copy(OUT.at[q, k], dst.at[:, col(p)], osem.at[q, k]))

    def start(cp):
        cp.start()

    def wait(cp):
        cp.wait()

    def s4(p):
        state_loads(p, start)
        pl.when(z > 0)(lambda: add_in(p, z, 0))
        pl.when(z < 3)(lambda: add_in(p, z, 4))

        @pl.when(swapped)
        def _():
            cp_final(p).start()

        @pl.when(kept)
        def _():
            FIN[p] = S[p, z]

    def cp_delta(p, k):
        return remote(DL.at[p, g], DL.at[p, g], ls.at[p, k], lr.at[p, g], members[k])

    def s5(p):
        pl.when(swapped)(lambda: cp_final(p).wait_recv())
        state_loads(p, wait)
        pl.when(p >= 2)(lambda: state_stores(p - 2, (0, 1), wait))
        q = p % 2

        def rows(i, carry):
            r = pl.ds(pl.multiple_of(i * 32, 32), 32)
            mom, sq, delta = adam_parts(
                IN[q, 0, r, :], IN[q, 1, r, :], IN[q, 2, r, :], FIN[p, r, :].astype(F32), RATE_MATRIX, WEIGHT_DECAY
            )
            OUT[q, 0, r, :] = mom
            OUT[q, 1, r, :] = sq
            DL[p, g, r, :] = delta.astype(BF)
            return carry

        lax.fori_loop(0, 3, rows, 0)
        for k in (1, 2, 0):
            cp_delta(p, k).start()
        state_stores(p, (0, 1), start)

    def s6(p):
        for k in range(3):
            remote(DL.at[p, froms[k]], DL.at[p, froms[k]], ls.at[p, k], lr.at[p, froms[k]], members[k]).wait_recv()
        pl.when(p >= 2)(lambda: state_stores(p - 2, (2, 3), wait))
        q = p % 2

        def rows(i, carry):
            r = pl.ds(pl.multiple_of(i * 32, 32), 32)
            total = DL[p, 0, r, :].astype(F32)
            for k in (1, 2, 3):
                total = total + DL[p, k, r, :].astype(F32)
            mean = total * 0.25
            mom = OUTER_MOMENTUM * IN[q, 3, r, :] + mean
            OUT[q, 2, r, :] = mom
            OUT[q, 3, r, :] = IN[q, 2, r, :] - OUTER_RATE * (mean + OUTER_MOMENTUM * mom)
            return carry

        lax.fori_loop(0, 3, rows, 0)
        state_stores(p, (2, 3), start)

    def slot(v, carry):
        tasks(v)
        for k, fn in ((0, s0), (1, s1), (2, s2), (3, s3), (6, s6), (4, s4), (5, s5)):
            real, p = piece(v - k)
            pl.when(real)(functools.partial(fn, p))
        return carry

    lax.fori_loop(0, 23, slot, 0)

    def drain(p, carry):
        @pl.when(jnp.logical_or(z == 0, z == 3))
        def _():
            for k in range(3):
                remote(S.at[p, k], ZI.at[p, k], zs.at[p, k], zr.at[p, k], partner).wait_send()

        @pl.when(jnp.logical_and(z > 0, z < 3))
        def _():
            for k in range(3):
                remote(S.at[p, k], ZI.at[p, k], zs.at[p, k], zr.at[p, k], partner).wait_send()

        pl.when(swapped)(lambda: cp_final(p).wait_send())
        for k in range(3):
            cp_delta(p, k).wait_send()
        return carry

    lax.fori_loop(0, RS, drain, 0)
    for p in (RS - 2, RS - 1):
        state_stores(jnp.int32(p), (0, 1, 2, 3), wait)
    each_slice(lambda j: cp_slice(j).wait_send())
    for k in range(3):
        cp_change(k).wait_send()
    for b in range(4):

        @pl.when(swapped)
        def _():
            out_remote(b).wait_recv()
            ig_remote(b).wait()

        @pl.when(kept)
        def _():
            ig_local(b).wait()


def backward(fwd, states):
    any_ = pl.BlockSpec(memory_space=pl.ANY)
    vm = pl.BlockSpec(memory_space=pltpu.VMEM)
    dma = pltpu.SemaphoreType.DMA
    attn = jax.ShapeDtypeStruct((SHARD, FF), F32)
    mlp = jax.ShapeDtypeStruct((2, SHARD, FF), F32)
    vect = jax.ShapeDtypeStruct((12, SHARD), F32)
    return pl.pallas_call(
        backward_kernel,
        out_shape=(
            jax.ShapeDtypeStruct((T, D), BF), jax.ShapeDtypeStruct((T, D), F32),
            attn, attn, attn, attn, mlp, mlp, mlp, mlp, vect, vect, vect, vect,
        ),
        in_specs=[any_] * 9 + [vm, vm] + [any_] * 8 + [vm] * 4,
        out_specs=(any_,) * 10 + (vm,) * 4,
        scratch_shapes=[
            pltpu.VMEM((T, FF), BF), pltpu.VMEM((T, FF), BF), pltpu.VMEM((D, FF), BF),
            pltpu.VMEM((T, D), BF), pltpu.VMEM((T, D), BF), pltpu.VMEM((T, D), BF), pltpu.VMEM((T, D), F32),
            pltpu.VMEM((RING, 2, 4, SHARD, 768), BF), pltpu.VMEM((RS, 4, SHARD, 768), BF),
            pltpu.VMEM((RS, 5, SHARD, 768), BF), pltpu.VMEM((RS, SHARD, 768), BF),
            pltpu.VMEM((RS, 4, SHARD, 768), BF),
            pltpu.VMEM((2, 4, SHARD, 768), F32), pltpu.VMEM((2, 4, SHARD, 768), F32),
            pltpu.VMEM((16, D), F32), pltpu.VMEM((1, FF), F32),
            pltpu.VMEM((8, 16, 128), F32), pltpu.VMEM((8, 16, 128), F32), pltpu.VMEM((4, 16, 128), F32),
            dma((11,)), dma((RS,)), dma((RS,)), dma((RS, 3)), dma((RS, 5)), dma((RS,)), dma((RS,)),
            dma((RS, 3)), dma((RS, 4)), dma((2, 4)), dma((2, 4)), dma((4,)), dma((4,)), dma((4,)), dma((4,)),
            dma((8,)), dma((8,)), dma((3,)), dma((4,)),
        ],
        compiler_params=pltpu.CompilerParams(collective_id=2, has_side_effects=True, vmem_limit_bytes=63 * 2**20),
        name="backward",
    )(*fwd, *states)


def fast(
    inputs, segments, cotangent,
    attn_weight, attn_first, attn_second, attn_outer,
    mlp_weight, mlp_first, mlp_second, mlp_outer,
    vector_weight, vector_first, vector_second, vector_outer,
):
    seg = segments[0].reshape(8, 128) + 8 * (lax.broadcasted_iota(jnp.int32, (8, 128), 1) // SEQ)
    fwd = forward(inputs[0], cotangent[0], seg, attn_weight, mlp_weight, vector_weight)
    out = backward(
        fwd,
        (
            attn_weight, attn_first[0], attn_second[0], attn_outer,
            mlp_weight, mlp_first[0], mlp_second[0], mlp_outer,
            vector_weight, vector_first[0], vector_second[0], vector_outer,
        ),
    )
    lead = (1, 1, 1, 1, 0, 0, 1, 1, 0, 0, 1, 1, 0, 0)
    return tuple(v[None] if k else v for v, k in zip(out, lead))


def norm_apply(values, gain, shift):
    centre = values - jnp.mean(values, axis=-1, keepdims=True)
    spread = jnp.mean(centre * centre, axis=-1, keepdims=True)
    return centre * lax.rsqrt(spread + EPS_NORM) * gain + shift


def gelu_tanh(values):
    return jax.nn.gelu(values, approximate=True)


def adam_step(weight, first, second, gradient, step_rate, weight_decay):
    first_new = BETA_ONE * first + (1.0 - BETA_ONE) * gradient
    second_new = BETA_TWO * second + (1.0 - BETA_TWO) * gradient * gradient
    first_hat = first_new / (1.0 - BETA_ONE**STEP)
    second_hat = second_new / (1.0 - BETA_TWO**STEP)
    local_weight = weight - step_rate * (
        first_hat / (jnp.sqrt(second_hat) + ADAM_EPS) + weight_decay * weight
    )
    return (first_new, second_new, weight - local_weight)


def local(
    inputs,
    segments,
    cotangent,
    attn_weight,
    attn_first,
    attn_second,
    attn_outer,
    mlp_weight,
    mlp_first,
    mlp_second,
    mlp_outer,
    vector_weight,
    vector_first,
    vector_second,
    vector_outer,
):
    bf16 = jnp.bfloat16
    f32 = jnp.float32
    attn_cast = attn_weight.astype(bf16)
    mlp_cast = mlp_weight.astype(bf16)
    attn_low, mlp_low, vector_low = (
        lax.all_gather(attn_cast, "fsdp", axis=0, tiled=True),
        lax.all_gather(mlp_cast, "fsdp", axis=1, tiled=True),
        lax.all_gather(vector_weight.astype(bf16), "fsdp", axis=1, tiled=True),
    )
    vectors = vector_low.astype(f32)
    tokens_f = inputs[0].astype(f32)
    seg_ids = segments[0]
    back_f = cotangent[0].astype(f32)
    model_width = attn_low.shape[0]
    head_dim = model_width // HEADS
    score_scale = head_dim ** (-0.5)
    tok_count = tokens_f.shape[0]
    row_count = tok_count // SEQ
    shape_four = (row_count, SEQ, HEADS, head_dim)
    normed_f, norm_pull = jax.vjp(norm_apply, tokens_f, vectors[0], vectors[1])
    normed = normed_f.astype(bf16)
    project = jnp.dot(normed, attn_low[:, : 3 * model_width], preferred_element_type=f32)
    queries = (project[:, :model_width] + vectors[2]).astype(bf16).reshape(shape_four)
    keys_all = project[:, model_width : 2 * model_width].astype(bf16).reshape(shape_four)
    values_all = (
        (project[:, 2 * model_width : 3 * model_width] + vectors[3])
        .astype(bf16)
        .reshape(shape_four)
    )
    scores = (
        jnp.einsum("rqhd,rkhd->rhqk", queries, keys_all, preferred_element_type=f32) * score_scale
    )
    same_seg = (seg_ids[:, :, None] == seg_ids[:, None, :])[:, None]
    masked = jnp.where(same_seg, scores, NEG_LARGE)
    exponent = jnp.exp(masked - jnp.max(masked, axis=-1, keepdims=True))
    soft = exponent / jnp.sum(exponent, axis=-1, keepdims=True)
    probs = soft.astype(bf16)
    mixed = (
        jnp.einsum("rhqk,rkhd->rqhd", probs, values_all, preferred_element_type=f32)
        .reshape(tok_count, model_width)
        .astype(bf16)
    )
    attended = (
        jnp.dot(mixed, attn_low[:, 3 * model_width :], preferred_element_type=f32) + vectors[4]
    )
    residual = tokens_f + attended
    normed_two_f, norm_two_pull = jax.vjp(norm_apply, residual, vectors[5], vectors[6])
    normed_two = normed_two_f.astype(bf16)
    up_pre = jnp.dot(normed_two, mlp_low[0], preferred_element_type=f32) + vectors[8:12].reshape(-1)
    hidden_f, gelu_pull = jax.vjp(gelu_tanh, up_pre)
    hidden = hidden_f.astype(bf16)
    branch = jnp.einsum("nf,df->nd", hidden, mlp_low[1], preferred_element_type=f32) + vectors[7]
    block_out = (residual + branch).astype(bf16)
    d_branch = cotangent[0]
    d_down_bias = jnp.sum(back_f, axis=0)
    grad_down = jnp.einsum("nd,nf->df", d_branch, hidden, preferred_element_type=f32)
    d_hidden = jnp.einsum("nd,df->nf", d_branch, mlp_low[1], preferred_element_type=f32)
    (d_up_f,) = gelu_pull(d_hidden)
    d_up = d_up_f.astype(bf16)
    d_up_bias = jnp.sum(d_up.astype(f32), axis=0)
    grad_up = jnp.einsum("nd,nf->df", normed_two, d_up, preferred_element_type=f32)
    mlp_grad = jnp.stack([grad_up, grad_down])
    d_normed_two = jnp.einsum("nf,df->nd", d_up, mlp_low[0], preferred_element_type=f32)
    d_res_norm, d_gain_two, d_shift_two = norm_two_pull(d_normed_two)
    d_res = back_f + d_res_norm
    d_att = d_res.astype(bf16)
    d_out_bias = jnp.sum(d_att.astype(f32), axis=0)
    grad_out = jnp.einsum("nc,nd->cd", mixed, d_att, preferred_element_type=f32)
    d_mixed = (
        jnp.einsum("nd,cd->nc", d_att, attn_low[:, 3 * model_width :], preferred_element_type=f32)
        .astype(bf16)
        .reshape(shape_four)
    )
    d_values = (
        jnp.einsum("rhqk,rqhd->rkhd", probs, d_mixed, preferred_element_type=f32)
        .reshape(tok_count, model_width)
        .astype(bf16)
    )
    d_probs = jnp.einsum("rqhd,rkhd->rhqk", d_mixed, values_all, preferred_element_type=f32)
    d_scores = (soft * (d_probs - jnp.sum(d_probs * soft, axis=-1, keepdims=True))).astype(bf16)
    d_queries = (
        (
            jnp.einsum("rhqk,rkhd->rqhd", d_scores, keys_all, preferred_element_type=f32)
            * score_scale
        )
        .reshape(tok_count, model_width)
        .astype(bf16)
    )
    d_keys = (
        (jnp.einsum("rhqk,rqhd->rkhd", d_scores, queries, preferred_element_type=f32) * score_scale)
        .reshape(tok_count, model_width)
        .astype(bf16)
    )
    d_query_bias = jnp.sum(d_queries.astype(f32), axis=0)
    d_value_bias = jnp.sum(d_values.astype(f32), axis=0)
    d_project = jnp.concatenate([d_queries, d_keys, d_values], axis=1)
    grad_qkv = jnp.einsum("nc,nd->cd", normed, d_project, preferred_element_type=f32)
    d_normed = jnp.einsum(
        "nd,cd->nc", d_project, attn_low[:, : 3 * model_width], preferred_element_type=f32
    )
    d_tok_norm, d_gain_one, d_shift_one = norm_pull(d_normed)
    input_grad = d_res + d_tok_norm
    attn_grad = jnp.concatenate([grad_qkv, grad_out], axis=1)
    vector_grad = jnp.concatenate(
        [
            jnp.stack(
                [
                    d_gain_one,
                    d_shift_one,
                    d_query_bias,
                    d_value_bias,
                    d_out_bias,
                    d_gain_two,
                    d_shift_two,
                    d_down_bias,
                ]
            ),
            d_up_bias.reshape(4, model_width),
        ],
        axis=0,
    )
    attn_sum, mlp_sum, vector_sum = (
        lax.psum_scatter(attn_grad.astype(bf16), "fsdp", scatter_dimension=0, tiled=True).astype(f32),
        lax.psum_scatter(mlp_grad.astype(bf16), "fsdp", scatter_dimension=1, tiled=True).astype(f32),
        lax.psum_scatter(vector_grad, "fsdp", scatter_dimension=1, tiled=True),
    )
    attn_moment, attn_square, attn_delta = adam_step(
        attn_weight, attn_first[0], attn_second[0], attn_sum, RATE_MATRIX, WEIGHT_DECAY
    )
    mlp_moment, mlp_square, mlp_delta = adam_step(
        mlp_weight, mlp_first[0], mlp_second[0], mlp_sum, RATE_MATRIX, WEIGHT_DECAY
    )
    vector_moment, vector_square, vector_delta = adam_step(
        vector_weight, vector_first[0], vector_second[0], vector_sum, RATE_VECTOR, 0.0
    )
    group_count = lax.axis_size("group")
    attn_total, mlp_total, vector_total = (
        lax.psum(attn_delta.astype(jnp.bfloat16), "group").astype(jnp.float32),
        lax.psum(mlp_delta.astype(jnp.bfloat16), "group").astype(jnp.float32),
        lax.psum(vector_delta.astype(jnp.bfloat16), "group").astype(jnp.float32),
    )
    attn_mean = attn_total / group_count
    mlp_mean = mlp_total / group_count
    vector_mean = vector_total / group_count
    attn_momentum = OUTER_MOMENTUM * attn_outer + attn_mean
    mlp_momentum = OUTER_MOMENTUM * mlp_outer + mlp_mean
    vector_momentum = OUTER_MOMENTUM * vector_outer + vector_mean
    attn_master = attn_weight - OUTER_RATE * (attn_mean + OUTER_MOMENTUM * attn_momentum)
    mlp_master = mlp_weight - OUTER_RATE * (mlp_mean + OUTER_MOMENTUM * mlp_momentum)
    vector_master = vector_weight - OUTER_RATE * (vector_mean + OUTER_MOMENTUM * vector_momentum)
    return (
        block_out[None],
        input_grad[None],
        attn_moment[None],
        attn_square[None],
        attn_momentum,
        attn_master,
        mlp_moment[None],
        mlp_square[None],
        mlp_momentum,
        mlp_master,
        vector_moment[None],
        vector_square[None],
        vector_momentum,
        vector_master,
    )


def solution(mesh):
    in_specs = (
        P("group", "fsdp", None),
        P("group", "fsdp", None),
        P("group", "fsdp", None),
        P("fsdp", None),
        P("group", "fsdp", None),
        P("group", "fsdp", None),
        P("fsdp", None),
        P(None, "fsdp", None),
        P("group", None, "fsdp", None),
        P("group", None, "fsdp", None),
        P(None, "fsdp", None),
        P(None, "fsdp"),
        P("group", None, "fsdp"),
        P("group", None, "fsdp"),
        P(None, "fsdp"),
    )
    out_specs = (
        P("group", "fsdp", None),
        P("group", "fsdp", None),
        P("group", "fsdp", None),
        P("group", "fsdp", None),
        P("fsdp", None),
        P("fsdp", None),
        P("group", None, "fsdp", None),
        P("group", None, "fsdp", None),
        P(None, "fsdp", None),
        P(None, "fsdp", None),
        P("group", None, "fsdp"),
        P("group", None, "fsdp"),
        P(None, "fsdp"),
        P(None, "fsdp"),
    )
    fits = mesh.shape["group"] == 4 and mesh.shape["fsdp"] == 8
    return jax.shard_map(fast if fits else local, mesh=mesh, in_specs=in_specs, out_specs=out_specs, check_vma=False)
```

```python
import functools

import jax
import jax.numpy as jnp
from jax import lax
from jax.experimental import pallas as pl
from jax.experimental.pallas import tpu as pltpu
from jax.sharding import PartitionSpec as P

EPS_NORM = 1e-05
NEG_LARGE = -1e30
HEADS = 12
SEQ = 64
STEP = 10
BETA_ONE = 0.9
BETA_TWO = 0.999
ADAM_EPS = 1e-08
RATE_MATRIX = 0.05
RATE_VECTOR = 0.5
WEIGHT_DECAY = 0.1
OUTER_RATE = 0.7
OUTER_MOMENTUM = 0.9


ORDER_FORWARD = (
    ("cast", 0), ("g", 0, 0), ("g", 1, 0), ("xs", 3), ("cast", 1), ("g", 2, 0), ("vec", 0), ("g", 0, 1),
    ("g", 1, 1), ("g", 0, 2), ("xs", 2), ("xs", 0), ("g", 3, 0), ("xs", 1), ("g", 2, 1), ("g", 0, 3), ("g", 1, 2),
    ("g", 0, 4), ("g", 1, 3), ("cs", 0), ("g", 3, 1), ("g", 0, 5), ("g", 1, 4), ("g", 2, 2), ("g", 0, 6),
    ("ln", 0, 4), ("qk", 0, 4), ("g", 1, 5), ("g", 2, 3), ("g", 1, 6), ("g", 3, 2), ("v", 0, 4), ("g", 2, 4),
    ("at", 0, 2), ("g", 3, 3), ("at", 2, 2), ("g", 2, 5), ("g", 3, 4), ("on", 0, 4), ("g", 2, 6), ("u", 0, 0, 2),
    ("g", 3, 5), ("u", 0, 2, 2), ("g", 3, 6), ("u", 1, 0, 2), ("u", 1, 2, 2), ("end", 0),
)

ORDER_BACKWARD = (
    ("st", 0), ("g", 0, 0), ("gd", 0, 2), ("g", 0, 1), ("r", 1, 0), ("g", 1, 0), ("r", 0, 0), ("g", 1, 1),
    ("g", 0, 2), ("r", 0, 1), ("r", 1, 1), ("gd", 2, 2), ("g", 0, 3), ("g", 1, 2), ("r", 2, 0), ("r", 0, 2),
    ("g", 0, 4), ("g", 1, 3), ("r", 2, 1), ("il", 0), ("r", 3, 0), ("r", 0, 3), ("g", 1, 4), ("g", 0, 5),
    ("r", 1, 2), ("r", 0, 4), ("r", 3, 1), ("g", 1, 5), ("il", 1), ("r", 1, 3), ("r", 0, 5), ("g", 1, 6),
    ("g", 0, 6), ("dh", 0, 2), ("r", 1, 4), ("r", 2, 2), ("dh", 2, 2), ("r", 1, 5), ("gu", 0, 2), ("r", 4, 0),
    ("r", 1, 6), ("r", 0, 6), ("r", 2, 3), ("r", 3, 2), ("r", 5, 0), ("r", 4, 1), ("r", 0, 7), ("r", 1, 7),
    ("r", 2, 4), ("il", 2), ("r", 5, 1), ("r", 3, 3), ("gu", 2, 2), ("il", 3), ("r", 2, 5), ("r", 3, 4),
    ("bo", 0, 4), ("r", 6, 0), ("r", 7, 0), ("r", 4, 2), ("r", 5, 2), ("r", 2, 6), ("ld", 0), ("r", 6, 1),
    ("r", 3, 5), ("r", 2, 7), ("r", 4, 3), ("n2", 0, 2), ("r", 7, 1), ("r", 5, 3), ("r", 4, 4), ("il", 4),
    ("r", 6, 2), ("r", 3, 6), ("n2", 2, 2), ("go", 0), ("ld", 1), ("r", 3, 7), ("r", 8, 0), ("r", 6, 3),
    ("r", 5, 4), ("r", 4, 5), ("dm", 0, 4), ("r", 8, 1), ("r", 7, 2), ("il", 5), ("r", 5, 5), ("r", 4, 6),
    ("ab", 0, 2), ("r", 6, 4), ("r", 4, 7), ("r", 8, 2), ("r", 7, 3), ("ab", 2, 2), ("r", 5, 6), ("r", 7, 4),
    ("il", 6), ("r", 6, 5), ("gq", 0, 2), ("r", 9, 0), ("r", 8, 3), ("r", 10, 0), ("r", 5, 7), ("il", 7),
    ("r", 7, 5), ("r", 9, 1), ("r", 6, 6), ("n1", 0, 2), ("r", 7, 6), ("r", 6, 7), ("r", 10, 1), ("il", 8),
    ("r", 9, 2), ("r", 8, 4), ("n1", 2, 2), ("r", 10, 2), ("gq", 2, 1), ("r", 7, 7), ("r", 11, 0), ("r", 9, 3),
    ("vs", 0), ("r", 8, 5), ("r", 11, 1), ("r", 9, 4), ("r", 10, 3), ("r", 11, 2), ("r", 8, 6), ("il", 9),
    ("r", 10, 4), ("va", 0), ("r", 11, 3), ("r", 9, 5), ("vo", 0), ("r", 8, 7), ("il", 10), ("r", 11, 4),
    ("r", 10, 5), ("r", 9, 6), ("r", 9, 7), ("il", 11), ("r", 11, 5), ("ic", 0), ("r", 10, 6), ("r", 11, 6),
    ("r", 10, 7), ("r", 11, 7),
)


MESH = pl.DeviceIdType.MESH
BF = jnp.bfloat16
F32 = jnp.float32
D = 768
FF = 3072
T = 1024
TB = 256
SHARD = 96
GELU_C = 0.7978845608028654
GELU_A = 0.044715
SCALE = 0.125


def dot_nn(a, b):
    return jnp.dot(a, b, preferred_element_type=F32)


def dot_nt(a, b):
    return lax.dot_general(a, b, (((1,), (1,)), ((), ())), preferred_element_type=F32)


def dot_tn(a, b):
    return lax.dot_general(a, b, (((0,), (0,)), ((), ())), preferred_element_type=F32)


def coords():
    g = lax.axis_index("group")
    f = lax.axis_index("fsdp")
    return g // 2, g % 2, f // 2, f % 2


def dev(x, c, z, y):
    return (2 * x + c, 2 * z + y)


def remote(src, dst, ssem, rsem, to):
    return pltpu.make_async_remote_copy(
        src_ref=src, dst_ref=dst, send_sem=ssem, recv_sem=rsem, device_id=to, device_id_type=MESH
    )


def norm_parts(v):
    centre = v - jnp.mean(v, axis=-1, keepdims=True)
    spread = jnp.mean(centre * centre, axis=-1, keepdims=True)
    scale = lax.rsqrt(spread + EPS_NORM)
    return centre * scale, scale


def head_masks():
    lane = lax.broadcasted_iota(jnp.int32, (1, 128), 1)
    low = (lane < 64).astype(F32).astype(BF)
    high = (lane >= 64).astype(F32).astype(BF)
    return low, high


def segment_bias(seg_ref, i):
    row = seg_ref[pl.ds(i, 1), :]
    classes = lax.broadcasted_iota(jnp.int32, (16, 128), 0)
    hot = (classes == row).astype(F32).astype(BF)
    same = dot_tn(hot, hot)
    bias = (same - 1.0) * (-NEG_LARGE)
    return jnp.concatenate([bias, bias], axis=1)


def soft_pair(q, k2, bias):
    s = dot_nt(q, k2) * SCALE + bias
    halves = []
    for h in (0, 1):
        part = s[:, 128 * h : 128 * h + 128]
        e = jnp.exp(part - jnp.max(part, axis=-1, keepdims=True))
        halves.append(e * (1.0 / jnp.sum(e, axis=-1, keepdims=True)))
    return jnp.concatenate(halves, axis=1)


def stack_heads(v, low, high):
    return jnp.concatenate([v * low, v * high], axis=0)


def gather_stages(view, sems, where):
    x, c, z, y = where
    ys, yr, us, ds, zr, xs, xr, cs, cr = sems
    f = 2 * z + y
    other = 2 * z + 1 - y

    def rows(i):
        return pl.ds(pl.multiple_of(i * SHARD, 32), SHARD)

    def pair(i):
        return pl.ds(pl.multiple_of(i * 2 * SHARD, 64), 2 * SHARD)

    mine = 2 * x + c
    across = 2 * (1 - x) + c
    sib = 2 * x + 1 - c
    sib_across = 2 * (1 - x) + 1 - c

    def at(p, r, q):
        return view(p, r, pl.ds(pl.multiple_of(1536 * (p % 2) + 384 * q, 128), 384))

    def cp_y(p, r):
        return remote(at(p, r, mine), at(p, r, mine), ys.at[p], yr.at[p], dev(x, c, z, 1 - y))

    def cp_up(p, i):
        return remote(at(p, pair(i), mine), at(p, pair(i), mine), us.at[p, i], zr.at[p, i], dev(x, c, z + 1, y))

    def cp_down(p, i):
        return remote(at(p, pair(i), mine), at(p, pair(i), mine), ds.at[p, i], zr.at[p, i], dev(x, c, z - 1, y))

    def cp_x(p, r, i, q):
        return remote(at(p, r, q), at(p, r, q), xs.at[p, i], xr.at[p, i], dev(1 - x, c, z, y))

    def cp_c(p, r, i, q, k):
        return remote(at(p, r, q), at(p, r, q), cs.at[p, 4 * k + i], cr.at[p, 4 * k + i], dev(x, 1 - c, z, y))

    def others(fn):
        for k in (1, 2, 3):
            pl.when(z >= k)(functools.partial(fn, z - k))
            pl.when(z + k <= 3)(functools.partial(fn, z + k))

    def sa(p):
        cp_y(p, rows(f)).start()

    def sb(p):
        cp_y(p, rows(other)).wait_recv()
        pl.when(z < 3)(lambda: cp_up(p, z).start())
        pl.when(z > 0)(lambda: cp_down(p, z).start())
        cp_x(p, rows(other), z, mine).start()
        cp_c(p, rows(other), z, mine, 0).start()

    def hop(k, p):
        def from_below():
            i = z - k
            cp_up(p, i).wait_recv()
            pl.when(z < 3)(lambda: cp_up(p, i).start())
            cp_x(p, pair(i), i, mine).start()
            cp_c(p, pair(i), i, mine, 0).start()

        def from_above():
            i = z + k
            cp_down(p, i).wait_recv()
            pl.when(z > 0)(lambda: cp_down(p, i).start())
            cp_x(p, pair(i), i, mine).start()
            cp_c(p, pair(i), i, mine, 0).start()

        pl.when(z >= k)(from_below)
        pl.when(z + k <= 3)(from_above)

    def sf(p):
        cp_x(p, rows(other), z, across).wait_recv()
        cp_c(p, rows(other), z, across, 1).start()

        def fwd(i):
            cp_x(p, pair(i), i, across).wait_recv()
            cp_c(p, pair(i), i, across, 1).start()

        others(fwd)

    def sg(p):
        cp_c(p, rows(other), z, sib, 0).wait_recv()
        cp_c(p, rows(other), z, sib_across, 1).wait_recv()

        def got(i):
            cp_c(p, pair(i), i, sib, 0).wait_recv()
            cp_c(p, pair(i), i, sib_across, 1).wait_recv()

        others(got)

    def drain(p):
        cp_y(p, rows(f)).wait_send()
        pl.when(z < 3)(lambda: cp_up(p, z).wait_send())
        pl.when(z > 0)(lambda: cp_down(p, z).wait_send())
        cp_x(p, rows(other), z, mine).wait_send()
        cp_c(p, rows(other), z, mine, 0).wait_send()
        cp_c(p, rows(other), z, across, 1).wait_send()
        for k in (1, 2, 3):

            @pl.when(z >= k)
            def _():
                pl.when(z < 3)(lambda: cp_up(p, z - k).wait_send())

            @pl.when(z + k <= 3)
            def _():
                pl.when(z > 0)(lambda: cp_down(p, z + k).wait_send())

        def sent(i):
            cp_x(p, pair(i), i, mine).wait_send()
            cp_c(p, pair(i), i, mine, 0).wait_send()
            cp_c(p, pair(i), i, across, 1).wait_send()

        others(sent)

    stages = [sa, sb, functools.partial(hop, 1), functools.partial(hop, 2), functools.partial(hop, 3), sf, sg]
    return stages, drain


GATHER_SEMS = lambda n: [
    pltpu.SemaphoreType.DMA((n,)),
    pltpu.SemaphoreType.DMA((n,)),
    pltpu.SemaphoreType.DMA((n, 4)),
    pltpu.SemaphoreType.DMA((n, 4)),
    pltpu.SemaphoreType.DMA((n, 4)),
    pltpu.SemaphoreType.DMA((n, 4)),
    pltpu.SemaphoreType.DMA((n, 4)),
    pltpu.SemaphoreType.DMA((n, 8)),
    pltpu.SemaphoreType.DMA((n, 8)),
]
PIECES = 4


def forward_kernel(
    x_in, cot_in, seg_raw, aw, mw, vw,
    w_out, qkvm_out, hid_out, gp_out, nrm_out, n2_out, res_out, xv_out, cotv_out, vec_out, seg_out,
    w, xv, nrm, qkvm, res, n2, hid, gp, vec, seg, seg_in, tiles, ub,
    xsnd, xrcv, csnd, crcv, gsnd, grcv, vsnd, vrcv, osem,
    *gsems,
):
    where = coords()
    x, c, z, y = where
    f = 2 * z + y
    swapped = c != y
    partner = dev(x, y, z, c)

    barrier = pltpu.get_barrier_semaphore()

    def greet(to):
        pl.semaphore_signal(barrier, inc=1, device_id=to, device_id_type=MESH)

    for k in range(1, 8):
        greet((2 * x + c, (f + k) % 8))
    greet(dev(x, 1 - c, z, y))
    greet(dev(1 - x, c, z, y))
    pl.when(swapped)(lambda: greet(partner))

    for i in range(8):
        seg_in[i : i + 1, :] = jnp.concatenate([seg_raw[2 * i : 2 * i + 1, :], seg_raw[2 * i + 1 : 2 * i + 2, :] + 8], axis=1)
    own = pl.ds(pl.multiple_of(f * SHARD, 32), SHARD)
    tiles[pl.ds(f, 1)] = jnp.zeros((1, 16, 128), F32)
    tiles[f, 0:12, 0:SHARD] = vw[...].astype(BF).astype(F32)

    pl.semaphore_wait(barrier, 9 + swapped.astype(jnp.int32))

    stages, drain = gather_stages(lambda p, r, q: w.at[p // 2, r, q], gsems, where)

    def cp_vec(k, j):
        return remote(tiles.at[j], tiles.at[j], vsnd.at[k - 1], vrcv.at[k - 1], (2 * x + c, (f + k) % 8))

    def tok(b, n=1):
        if isinstance(b, int):
            return pl.ds(b * TB, n * TB)
        return pl.ds(pl.multiple_of(b * TB, TB), n * TB)

    def span(fn, lo, n):
        def step(b, carry):
            fn(b)
            return carry

        lax.fori_loop(lo, lo + n, step, 0)

    def x_remote(b):
        return remote(x_in.at[tok(b)], xv.at[tok(b)], xsnd.at[b], xrcv.at[b], partner)

    def x_local(b):
        return pltpu.make_async_copy(x_in.at[tok(b)], xv.at[tok(b)], xrcv.at[b])

    def cot_remote():
        return remote(cot_in, cotv_out, csnd, crcv, partner)

    def seg_remote():
        return remote(seg_in, seg, gsnd, grcv, partner)

    outs = []

    def write(src, dst):
        cp = pltpu.make_async_copy(src, dst, osem.at[len(outs)])
        cp.start()
        outs.append(cp)

    def cast(m):
        if m:
            w[1, own, :] = mw[0].astype(BF)
            return
        w[0, own, :] = aw[...].astype(BF)
        for k in range(1, 8):
            cp_vec(k, f).start()

        @pl.when(swapped)
        def _():
            seg_remote().start()

        @pl.when(jnp.logical_not(swapped))
        def _():
            seg[...] = seg_in[...]
            for b in range(4):
                x_local(b).start()

    def send_x(b):
        pl.when(swapped)(lambda: x_remote(b).start())

    def send_cot(k):
        pl.when(swapped)(lambda: cot_remote().start())

    def gather(p, s):
        stages[s](p)
        if s == 6 and p % 2 == 1:
            write(w.at[p // 2], w_out.at[p // 2])

    def vectors():
        for k in range(1, 8):
            cp_vec(k, (f + 8 - k) % 8).wait_recv()
        total = jnp.zeros((16, D), F32)
        r = lax.broadcasted_iota(jnp.int32, (128, D), 0)
        q = lax.broadcasted_iota(jnp.int32, (128, D), 1)
        for j in range(8):
            pick = jnp.logical_and(q == r + SHARD * j, r < SHARD).astype(F32).astype(BF)
            total = total + dot_nn(tiles[j].astype(BF), pick)
        vec[...] = total
        for k in range(4):
            ub[0:1, D * k : D * k + D] = total[8 + k : 9 + k, :]

    def first_norm(b):
        @pl.when(swapped)
        def _():
            x_remote(b).wait_recv()

        @pl.when(jnp.logical_not(swapped))
        def _():
            x_local(b).wait()

        hat, _ = norm_parts(xv[tok(b), :].astype(F32))
        nrm[tok(b), :] = (hat * vec[0:1, :] + vec[1:2, :]).astype(BF)

    def queries_keys(b):
        r = dot_nn(nrm[tok(b), :], w[0, :, 0:1536])
        qkvm[tok(b), 0:D] = (r[:, 0:D] + vec[2:3, :]).astype(BF)
        qkvm[tok(b), D : 2 * D] = r[:, D : 2 * D].astype(BF)

    def values(b):
        r = dot_nn(nrm[tok(b), :], w[0, :, 1536:2304])
        qkvm[tok(b), 2 * D : 3 * D] = (r + vec[3:4, :]).astype(BF)

    def attention(i):
        low, high = head_masks()
        bias = segment_bias(seg, i)
        r = pl.ds(pl.multiple_of(i * 128, 128), 128)
        for p in range(6):
            col = 128 * p
            q = qkvm[r, col : col + 128]
            k2 = stack_heads(qkvm[r, D + col : D + col + 128], low, high)
            v2 = stack_heads(qkvm[r, 2 * D + col : 2 * D + col + 128], low, high)
            probs = soft_pair(q, k2, bias).astype(BF)
            qkvm[r, 3 * D + col : 3 * D + col + 128] = dot_nn(probs, v2).astype(BF)

    greeted = []

    def attend(lo, n):
        if not greeted:
            greeted.append(lo)
            pl.when(swapped)(lambda: seg_remote().wait_recv())
        span(attention, 2 * lo, 2 * n)
        write(qkvm.at[tok(lo, n)], qkvm_out.at[tok(lo, n)])

    def out_norm(b):
        att = dot_nn(qkvm[tok(b), 3 * D :], w[0, :, 2304:3072]) + vec[4:5, :]
        r = xv[tok(b), :].astype(F32) + att
        res[tok(b), :] = r
        hat, _ = norm_parts(r)
        n2[tok(b), :] = (hat * vec[5:6, :] + vec[6:7, :]).astype(BF)

    def up(half, b):
        for k in range(2):
            lo = 1536 * half + 768 * k
            u = dot_nn(n2[tok(b), :], w[1, :, lo : lo + 768]) + ub[0:1, lo : lo + 768]
            u2 = u * u
            t = jnp.tanh(u * (GELU_C + (GELU_C * GELU_A) * u2))
            h = 0.5 + 0.5 * t
            out = u * h
            hid[tok(b), lo : lo + 768] = out.astype(BF)
            slope = h + out * (1.0 - h) * (2.0 * GELU_C + (6.0 * GELU_C * GELU_A) * u2)
            gp[tok(b), lo : lo + 768] = slope.astype(BF)

    def spanned(fn, *pairs):
        def run(lo, n):
            span(fn, lo, n)
            for src, dst in pairs:
                write(src.at[tok(lo, n)], dst.at[tok(lo, n)])

        return run

    def up_half(half, lo, n):
        span(functools.partial(up, half), lo, n)
        if half:
            write(hid.at[tok(lo, n)], hid_out.at[tok(lo, n)])
            write(gp.at[tok(lo, n)], gp_out.at[tok(lo, n)])

    does = {
        "g": gather, "cast": cast, "xs": send_x, "cs": send_cot, "vec": lambda k: vectors(),
        "ln": spanned(first_norm, (xv, xv_out), (nrm, nrm_out)), "qk": spanned(queries_keys), "v": spanned(values),
        "at": attend, "on": spanned(out_norm, (res, res_out), (n2, n2_out)), "u": up_half, "end": lambda k: None,
    }
    for name, *at in ORDER_FORWARD:
        does[name](*at)
    vec_out[...] = vec[...]
    seg_out[...] = seg[...]

    for p in range(PIECES):
        drain(p)
    for k in range(1, 8):
        cp_vec(k, f).wait_send()

    @pl.when(swapped)
    def _():
        seg_remote().wait_send()
        for b in range(4):
            x_remote(b).wait_send()
        cot_remote().wait()

    for cp in outs:
        cp.wait()


def forward(x, cot, seg, aw, mw, vw):
    any_ = pl.BlockSpec(memory_space=pl.ANY)
    vm = pl.BlockSpec(memory_space=pltpu.VMEM)
    wide = jax.ShapeDtypeStruct((T, FF), BF)
    slim = jax.ShapeDtypeStruct((T, D), BF)
    dma = pltpu.SemaphoreType.DMA
    return pl.pallas_call(
        forward_kernel,
        out_shape=(
            jax.ShapeDtypeStruct((2, D, FF), BF), wide, wide, wide, slim, slim,
            jax.ShapeDtypeStruct((T, D), F32), slim, slim,
            jax.ShapeDtypeStruct((16, D), F32), jax.ShapeDtypeStruct((8, 128), jnp.int32),
        ),
        in_specs=[any_, any_, vm, vm, vm, vm],
        out_specs=(any_,) * 9 + (vm, vm),
        scratch_shapes=[
            pltpu.VMEM((2, D, FF), BF), pltpu.VMEM((T, D), BF), pltpu.VMEM((T, D), BF), pltpu.VMEM((T, FF), BF),
            pltpu.VMEM((T, D), F32), pltpu.VMEM((T, D), BF), pltpu.VMEM((T, FF), BF), pltpu.VMEM((T, FF), BF),
            pltpu.VMEM((16, D), F32), pltpu.VMEM((8, 128), jnp.int32), pltpu.VMEM((8, 128), jnp.int32),
            pltpu.VMEM((8, 16, 128), F32),
            pltpu.VMEM((1, FF), F32),
            dma((4,)), dma((4,)), dma, dma, dma, dma, dma((7,)), dma((7,)), dma((40,)),
            *GATHER_SEMS(PIECES),
        ],
        compiler_params=pltpu.CompilerParams(collective_id=1, has_side_effects=True, vmem_limit_bytes=60 * 2**20),
        name="forward",
    )(x, cot, seg, aw, mw, vw)


def final_kernel(*refs):
    ins, small, outs, small_outs = refs[:10], refs[10:14], refs[14:24], refs[24:28]
    bufs, rsem, wsem = refs[28:38], refs[38], refs[39]
    reads = [pltpu.make_async_copy(a, b, rsem.at[k]) for k, (a, b) in enumerate(zip(ins, bufs))]
    for cp in reads:
        cp.start()
    for k in range(4):
        if k < 2:
            for r in range(12):
                small_outs[k][r] = small[k][r : r + 1, :]
        else:
            small_outs[k][...] = small[k][...]
    writes = [pltpu.make_async_copy(b, a, wsem.at[k]) for k, (a, b) in enumerate(zip(outs, bufs))]
    for r, w in zip(reads, writes):
        r.wait()
        w.start()
    for w in writes:
        w.wait()


def finish(arrays):
    any_ = pl.BlockSpec(memory_space=pl.ANY)
    vm = pl.BlockSpec(memory_space=pltpu.VMEM)
    big, small = arrays[:10], arrays[10:14]
    shapes = [jax.ShapeDtypeStruct(a.shape, a.dtype) for a in big]
    thin = jax.ShapeDtypeStruct((12, 1, SHARD), F32)
    out = pl.pallas_call(
        final_kernel,
        out_shape=(*shapes, thin, thin, *[jax.ShapeDtypeStruct(a.shape, a.dtype) for a in small[2:]]),
        in_specs=[any_] * 10 + [vm] * 4,
        out_specs=(any_,) * 10 + (vm,) * 4,
        scratch_shapes=[pltpu.VMEM(a.shape, a.dtype) for a in big]
        + [pltpu.SemaphoreType.DMA((10,)), pltpu.SemaphoreType.DMA((10,))],
        compiler_params=pltpu.CompilerParams(vmem_limit_bytes=63 * 2**20),
        name="finish",
    )(*big, *small)
    return (*out[:10], jnp.transpose(out[10], (1, 0, 2)), jnp.transpose(out[11], (1, 0, 2)), out[12], out[13])


RS = 12
RING = 2


def adam_parts(first, second, weight, gradient, rate, decay):
    first_new = BETA_ONE * first + (1.0 - BETA_ONE) * gradient
    second_new = BETA_TWO * second + (1.0 - BETA_TWO) * gradient * gradient
    first_hat = first_new * (1.0 / (1.0 - BETA_ONE**STEP))
    second_hat = second_new * (1.0 / (1.0 - BETA_TWO**STEP))
    delta = rate * (first_hat / (jnp.sqrt(second_hat) + ADAM_EPS) + decay * weight)
    return first_new, second_new, delta


def backward_kernel(
    cot_in, w_in, qkvm_in, hid_in, gp_in, nrm_in, n2_in, res_in, xv_in, cotv_in, vec, seg,
    aw, a1, a2, ao, mw, m1, m2, mo, vw, v1, v2, vo,
    out_o, ig_o, am_o, as_o, ap_o, aq_o, mm_o, ms_o, mp_o, mq_o, vm_o, vs_o, vp_o, vq_o, ig_land,
    A, B, W, cot, n2, E, R, G, S, ZI, FIN, DL, IN, OUT, vg, ubs, vsl, vrc, vdl,
    lsem, d2s, d2r, zs, zr, fs, fr, ls, lr, isem, osem, bos, bor, igs, igr, vss, vsr, vds, vdr, *gsems,
):
    x, c, z, y = coords()
    f = 2 * z + y
    g = 2 * x + c
    swapped = c != y
    kept = jnp.logical_not(swapped)
    partner = dev(x, y, z, c)

    barrier = pltpu.get_barrier_semaphore()

    def greet(to):
        pl.semaphore_signal(barrier, inc=1, device_id=to, device_id_type=MESH)

    me16 = c * 8 + f
    for k in range(1, 16):
        other = (me16 + k) % 16
        greet((2 * x + other // 8, other % 8))
    greet(dev(1 - x, c, z, y))
    greet(dev(1 - x, 1 - c, z, y))

    def tok(b, n=1):
        if isinstance(b, int):
            return pl.ds(b * TB, n * TB)
        return pl.ds(pl.multiple_of(b * TB, TB), n * TB)

    def span(fn, lo, n):
        def step(b, carry):
            fn(b)
            return carry

        lax.fori_loop(lo, lo + n, step, 0)

    def spanned(fn, *cps):
        def run(lo, n):
            once(*cps)
            span(fn, lo, n)

        return run

    own = pl.ds(pl.multiple_of(f * SHARD, 32), SHARD)
    stages, gather_drain = gather_stages(lambda p, r, q: W.at[r, q], gsems, (x, c, z, y))

    def load(src, dst, k):
        return pltpu.make_async_copy(src, dst, lsem.at[k])

    ld_cot = load(cotv_in, cot, 0)
    ld_own = load(cot_in, cot, 0)
    ld_hid = load(hid_in, A, 1)
    ld_own_w = [load(mw.at[1, :, pl.ds(768 * k, 768)], IN.at[0, k], 11 + k) for k in range(4)]
    ld_gp = load(gp_in, B, 3)
    ld_res = load(res_in, R, 4)
    ld_n2 = load(n2_in, n2, 5)
    ld_wu = load(w_in.at[1], W, 6)
    ld_wa = load(w_in.at[0], W, 7)
    ld_qkvm = load(qkvm_in, A, 8)
    ld_nrm = load(nrm_in, E, 9)
    ld_xv = load(xv_in, cot, 10)
    pl.when(swapped)(lambda: ld_cot.start())
    pl.when(kept)(lambda: ld_own.start())
    for cp in (*ld_own_w, ld_hid, ld_gp, ld_res, ld_n2):
        cp.start()
    vg[...] = jnp.zeros((16, D), F32)
    vsl[...] = jnp.zeros((8, 16, 128), F32)
    vdl[...] = jnp.zeros((4, 16, 128), F32)
    for k, cp in enumerate(ld_own_w):
        cp.wait()
        W[own, 768 * k : 768 * k + 768] = IN[0, k].astype(BF)
    pl.semaphore_wait(barrier, 17)

    def wide(i, n=768):
        return pl.ds(i * n if isinstance(i, int) else pl.multiple_of(i * n, n), n)

    ones = jnp.ones((16, T), BF)

    def gradient(lhs, rhs, slot):
        out = dot_tn(lhs, rhs)
        for j in range(8):
            G[slot, j % 2, j // 2] = out[SHARD * j : SHARD * j + SHARD].astype(BF)

    def t_down(lo, n):
        if lo == 0:
            ld_cot.wait()
            ld_hid.wait()
            vg[7:8, :] = dot_nn(ones, cot[...])[0:1, :]
        span(lambda v: gradient(cot[...], A[:, wide(v)], v % RING), lo, n)

    def out_remote(b):
        return remote(E.at[tok(b)], out_o.at[tok(b)], bos.at[b], bor.at[b], partner)

    def out_local(b):
        return pltpu.make_async_copy(E.at[tok(b)], out_o.at[tok(b)], bor.at[b])

    waited = set()

    def once(*cps):
        for cp in cps:
            if id(cp) not in waited:
                waited.add(id(cp))
                cp.wait()

    def hidden_back(b):
        for k in range(4):
            lo = 768 * k
            dh = dot_nn(cot[tok(b), :], W[:, lo : lo + 768])
            B[tok(b), lo : lo + 768] = (dh * B[tok(b), lo : lo + 768].astype(F32)).astype(BF)

    def block_output(b):
        branch = dot_nt(A[tok(b), :], W[...])
        E[tok(b), :] = (R[tok(b), :] + branch + vec[7:8, :]).astype(BF)
        send_out(b)

    def send_out(b):
        pl.when(swapped)(lambda: out_remote(b).start())
        pl.when(kept)(lambda: out_local(b).start())

    def loads(k):
        if k == 0:
            for p in range(2):
                gather_drain(p)
            ld_wu.start()
            ld_qkvm.start()
            return
        ld_wa.start()
        ld_xv.start()
        for b in range(4):
            pl.when(swapped)(lambda: out_remote(b).wait_send())
            pl.when(kept)(lambda: out_local(b).wait())
        ld_nrm.start()

    def t_up(lo, n):
        once(ld_n2)

        def one(u):
            ubs[pl.ds(u, 1), :] = dot_nn(ones, B[:, wide(u)])[0:1, :]
            gradient(n2[...], B[:, wide(u)], u % RING)

        span(one, lo, n)
        if lo + n == 4:
            vg[8:12, :] = ubs[0:4, :]

    def norm_back(dn, v, gain):
        hat, scale = norm_parts(v)
        e = dn * gain
        d = (e - jnp.mean(e, axis=-1, keepdims=True) - hat * jnp.mean(e * hat, axis=-1, keepdims=True)) * scale
        return d, jnp.sum(dn * hat, axis=0, keepdims=True), jnp.sum(dn, axis=0, keepdims=True)

    def second_norm(b):
        dn = dot_nt(B[tok(b), :], W[...])
        d, dgain, dshift = norm_back(dn, R[tok(b), :], vec[5:6, :])
        d = d + cot[tok(b), :].astype(F32)
        R[tok(b), :] = d
        B[tok(b), 3 * D :] = d.astype(BF)
        vg[5:6, :] = vg[5:6, :] + dgain
        vg[6:7, :] = vg[6:7, :] + dshift

    def t_out(k):
        once(ld_qkvm)
        vg[4:5, :] = dot_nn(ones, B[:, 3 * D :])[0:1, :]
        gradient(A[:, 3 * D :], B[:, 3 * D :], 8 % RING)

    def mixed_back(b):
        A[tok(b), 3 * D :] = dot_nt(B[tok(b), 3 * D :], W[:, 3 * D :]).astype(BF)

    def attention_back(i):
        low, high = head_masks()
        lane = lax.broadcasted_iota(jnp.int32, (1, 128), 1) < 64
        bias = segment_bias(seg, i)
        r = pl.ds(pl.multiple_of(i * 128, 128), 128)
        for p in range(6):
            col = 128 * p
            q = A[r, col : col + 128]
            k2 = stack_heads(A[r, D + col : D + col + 128], low, high)
            v2 = stack_heads(A[r, 2 * D + col : 2 * D + col + 128], low, high)
            dm = A[r, 3 * D + col : 3 * D + col + 128]
            soft = soft_pair(q, k2, bias)
            dp = dot_nt(dm, v2)
            both = dot_tn(soft.astype(BF), dm)
            B[r, 2 * D + col : 2 * D + col + 128] = jnp.where(lane, both[:128], both[128:]).astype(BF)
            halves = []
            for h in (0, 1):
                part = dp[:, 128 * h : 128 * h + 128]
                so = soft[:, 128 * h : 128 * h + 128]
                halves.append(so * (part - jnp.sum(part * so, axis=-1, keepdims=True)))
            ds = jnp.concatenate(halves, axis=1).astype(BF)
            B[r, col : col + 128] = (dot_nn(ds, k2) * SCALE).astype(BF)
            both = dot_tn(ds, q) * SCALE
            B[r, D + col : D + col + 128] = jnp.where(lane, both[:128], both[128:]).astype(BF)

    def t_att(lo, n):
        span(attention_back, 2 * lo, 2 * n)

    def t_qkv(lo, n):
        once(ld_nrm)
        if lo == 0:
            vg[2:3, :] = dot_nn(ones, B[:, 0:D])[0:1, :]
            vg[3:4, :] = dot_nn(ones, B[:, 2 * D : 3 * D])[0:1, :]
        span(lambda u: gradient(E[...], B[:, wide(u)], (u + 1) % RING), lo, n)

    def ig_remote(b):
        return remote(n2.at[tok(b)], ig_land.at[tok(b)], igs.at[b], igr.at[b], partner)

    def ig_local(b):
        return pltpu.make_async_copy(R.at[tok(b)], ig_o.at[tok(b)], igr.at[b])

    ld_land = load(ig_land, cot, 15)
    ld_ig = pltpu.make_async_copy(R, ig_o, lsem.at[16])

    def land(k):
        @pl.when(swapped)
        def _():
            for b in range(4):
                ig_remote(b).wait_recv()
            ld_land.start()
            ld_land.wait()

            def one(b):
                R[tok(b), :] = cot[tok(b), :].astype(F32)

            span(one, 0, 4)
            ld_ig.start()

    def first_norm_back(b):
        dn = dot_nt(B[tok(b), : 3 * D], W[:, : 3 * D])
        d, dgain, dshift = norm_back(dn, cot[tok(b), :].astype(F32), vec[0:1, :])
        R[tok(b), :] = R[tok(b), :] + d
        vg[0:1, :] = vg[0:1, :] + dgain
        vg[1:2, :] = vg[1:2, :] + dshift
        send_ig(b)

    def send_ig(b):
        @pl.when(swapped)
        def _():
            n2[tok(b), :] = R[tok(b), :].astype(BF)
            ig_remote(b).start()

        pl.when(kept)(lambda: ig_local(b).start())

    def cp_slice(j):
        return remote(vsl.at[j], vrc.at[2 * z + c], vss.at[j], vsr.at[2 * z + c], (2 * x + y, j))

    def each_slice(fn):
        def step(j, carry):
            pl.when(jnp.logical_or(swapped, j != f))(lambda: fn(j))
            return carry

        lax.fori_loop(0, 8, step, 0)

    def send_slices(k):
        for j in range(8):
            vsl[j, :, 0:SHARD] = vg[:, SHARD * j : SHARD * j + SHARD]

        @pl.when(kept)
        def _():
            vrc[pl.ds(2 * z + c, 1)] = vsl[pl.ds(f, 1)]

        each_slice(lambda j: cp_slice(j).start())

    def cp_change(k):
        return remote(vdl.at[g], vdl.at[g], vds.at[k], vdr.at[g], members[k])

    def t_vec_adam(k):
        def step(s, carry):
            pl.when(jnp.logical_or(swapped, s != 2 * z + c))(
                lambda: remote(vrc.at[s], vrc.at[s], vss.at[0], vsr.at[s], partner).wait_recv()
            )
            return carry

        lax.fori_loop(0, 8, step, 0)
        grad = jnp.sum(vrc[...], axis=0)[0:12, 0:SHARD]
        first = jnp.concatenate([v1[r] for r in range(12)], axis=0)
        second = jnp.concatenate([v2[r] for r in range(12)], axis=0)
        mom, sq, delta = adam_parts(first, second, vw[...], grad, RATE_VECTOR, 0.0)
        vm_o[...] = mom
        vs_o[...] = sq
        vdl[g, 0:12, 0:SHARD] = delta
        for k in range(3):
            cp_change(k).start()

    def t_vec_outer(k):
        for k in range(3):
            remote(vdl.at[froms[k]], vdl.at[froms[k]], vds.at[k], vdr.at[froms[k]], members[k]).wait_recv()
        mean = jnp.sum(vdl[...], axis=0)[0:12, 0:SHARD] * 0.25
        mom = OUTER_MOMENTUM * vo[...] + mean
        vp_o[...] = mom
        vq_o[...] = vw[...] - OUTER_RATE * (mean + OUTER_MOMENTUM * mom)

    members = [dev(x, 1 - c, z, y), dev(1 - x, c, z, y), dev(1 - x, 1 - c, z, y)]
    froms = [2 * x + 1 - c, 2 * (1 - x) + c, 2 * (1 - x) + 1 - c]

    def cp_core(p):
        return remote(G.at[p % RING, 1 - c], S.at[p], d2s.at[p], d2r.at[p], dev(x, 1 - c, z, y))

    def hop_up(p, t, k):
        return remote(S.at[p, t], ZI.at[p, t - z - 1], zs.at[p, k], zr.at[p, t - z - 1], dev(x, c, z + 1, y))

    def hop_down(p, t, k):
        return remote(S.at[p, t], ZI.at[p, 5 - z + t], zs.at[p, k], zr.at[p, 5 - z + t], dev(x, c, z - 1, y))

    def got(p, k):
        remote(ZI.at[p, k], ZI.at[p, k], zs.at[p, 0], zr.at[p, k], partner).wait_recv()

    def add_in(p, t, k):
        got(p, k)
        S[p, t] = (S[p, t].astype(F32) + ZI[p, k].astype(F32)).astype(BF)

    def s0(p):
        cp_core(p).start()

    def s1(p):
        cp_core(p).wait_recv()

        def one(t):
            S[p, t] = (S[p, t].astype(F32) + G[p % RING, c, t].astype(F32)).astype(BF)

        span(one, 0, 4)

        @pl.when(z == 0)
        def _():
            for k, t in enumerate((3, 2, 1)):
                hop_up(p, t, k).start()

        @pl.when(z == 3)
        def _():
            for k, t in enumerate((0, 1, 2)):
                hop_down(p, t, k).start()

        cp_core(p).wait_send()

    def s2(p):
        @pl.when(z == 1)
        def _():
            for k, t in enumerate((3, 2)):
                add_in(p, t, t - 1)
                hop_up(p, t, k).start()

        @pl.when(z == 2)
        def _():
            for k, t in enumerate((0, 1)):
                add_in(p, t, 2 + t)
                hop_down(p, t, k).start()

    def s3(p):
        @pl.when(z == 2)
        def _():
            add_in(p, 3, 1)
            hop_up(p, 3, 2).start()

        @pl.when(z == 1)
        def _():
            add_in(p, 0, 3)
            hop_down(p, 0, 2).start()

    def cp_final(p):
        return remote(S.at[p, z], FIN.at[p], fs.at[p], fr.at[p], partner)

    def col(p):
        return pl.ds(768 * (p % 4 if p < 8 else (p + 3) % 4), 768)

    def state_loads(p, fn):
        q = p % 2
        m = 1 - p // 4
        for k, src in enumerate((m1, m2, mw, mo) if p < 8 else (a1, a2, aw, ao)):
            src = src.at[m, :, col(p)] if p < 8 else src.at[:, col(p)]
            fn(pltpu.make_async_copy(src, IN.at[q, k], isem.at[q, k]))

    def state_stores(p, ks, fn):
        q = p % 2
        m = 1 - p // 4
        for k in ks:
            dst = ((mm_o, ms_o, mp_o, mq_o) if p < 8 else (am_o, as_o, ap_o, aq_o))[k]
            dst = dst.at[m, :, col(p)] if p < 8 else dst.at[:, col(p)]
            fn(pltpu.make_async_copy(OUT.at[q, k], dst, osem.at[q, k]))

    def start(cp):
        cp.start()

    def wait(cp):
        cp.wait()

    def s4(p):
        pl.when(z > 0)(lambda: add_in(p, z, 0))
        pl.when(z < 3)(lambda: add_in(p, z, 4))

        @pl.when(swapped)
        def _():
            cp_final(p).start()

        @pl.when(kept)
        def _():
            FIN[p] = S[p, z]

    def cp_delta(p, k):
        i = (g, g, froms[1])[k]
        return remote(DL.at[p, i], DL.at[p, i], ls.at[p, k], lr.at[p, i], members[1 if k == 1 else 0])

    def got_delta(p, k):
        i = froms[k]
        remote(DL.at[p, i], DL.at[p, i], ls.at[p, 0], lr.at[p, i], members[k]).wait_recv()

    def s5(p):
        pl.when(swapped)(lambda: cp_final(p).wait_recv())
        state_loads(p, wait)
        if p >= 2:
            state_stores(p - 2, (0, 1), wait)
        q = p % 2

        def rows(i, carry):
            r = pl.ds(pl.multiple_of(i * 32, 32), 32)
            mom, sq, delta = adam_parts(
                IN[q, 0, r, :], IN[q, 1, r, :], IN[q, 2, r, :], FIN[p, r, :].astype(F32), RATE_MATRIX, WEIGHT_DECAY
            )
            OUT[q, 0, r, :] = mom
            OUT[q, 1, r, :] = sq
            DL[p, g, r, :] = delta.astype(BF)
            return carry

        lax.fori_loop(0, 3, rows, 0)
        for k in (1, 0):
            cp_delta(p, k).start()
        state_stores(p, (0, 1), start)

    def s6(p):
        got_delta(p, 1)
        cp_delta(p, 2).start()

    def s7(p):
        got_delta(p, 0)
        got_delta(p, 2)
        if p >= 2:
            state_stores(p - 2, (2, 3), wait)
        q = p % 2

        def rows(i, carry):
            r = pl.ds(pl.multiple_of(i * 32, 32), 32)
            total = DL[p, 0, r, :].astype(F32)
            for k in (1, 2, 3):
                total = total + DL[p, k, r, :].astype(F32)
            mean = total * 0.25
            mom = OUTER_MOMENTUM * IN[q, 3, r, :] + mean
            OUT[q, 2, r, :] = mom
            OUT[q, 3, r, :] = IN[q, 2, r, :] - OUTER_RATE * (mean + OUTER_MOMENTUM * mom)
            return carry

        lax.fori_loop(0, 3, rows, 0)
        state_stores(p, (2, 3), start)

    sums = (s0, s1, s2, s3, s4, s5, s6, s7)
    does = {
        "g": lambda p, s: stages[s](p), "r": lambda p, k: sums[k](p), "il": lambda p: state_loads(p, start),
        "st": lambda k: None, "gd": t_down, "dh": spanned(hidden_back, ld_gp), "bo": spanned(block_output, ld_res),
        "ld": loads, "gu": t_up, "n2": spanned(second_norm, ld_wu), "go": t_out, "dm": spanned(mixed_back, ld_wa),
        "ab": t_att, "gq": t_qkv, "n1": spanned(first_norm_back, ld_xv), "ic": land,
        "vs": send_slices, "va": t_vec_adam, "vo": t_vec_outer,
    }
    for name, *at in ORDER_BACKWARD:
        does[name](*at)

    for p in range(RS):
        for k in range(3):
            remote(S.at[p, k], ZI.at[p, k], zs.at[p, k], zr.at[p, k], partner).wait_send()
        pl.when(swapped)(lambda: cp_final(p).wait_send())
        for k in range(3):
            cp_delta(p, k).wait_send()
    for p in (RS - 2, RS - 1):
        state_stores(p, (0, 1, 2, 3), wait)
    each_slice(lambda j: cp_slice(j).wait_send())
    for k in range(3):
        cp_change(k).wait_send()
    for b in range(4):

        @pl.when(swapped)
        def _():
            out_remote(b).wait_recv()
            ig_remote(b).wait_send()

        @pl.when(kept)
        def _():
            ig_local(b).wait()

    pl.when(swapped)(lambda: ld_ig.wait())


def backward(cot, fwd, states):
    any_ = pl.BlockSpec(memory_space=pl.ANY)
    vm = pl.BlockSpec(memory_space=pltpu.VMEM)
    dma = pltpu.SemaphoreType.DMA
    attn = jax.ShapeDtypeStruct((SHARD, FF), F32)
    mlp = jax.ShapeDtypeStruct((2, SHARD, FF), F32)
    vect = jax.ShapeDtypeStruct((12, SHARD), F32)
    return pl.pallas_call(
        backward_kernel,
        out_shape=(
            jax.ShapeDtypeStruct((T, D), BF), jax.ShapeDtypeStruct((T, D), F32),
            attn, attn, attn, attn, mlp, mlp, mlp, mlp, vect, vect, vect, vect,
            jax.ShapeDtypeStruct((T, D), BF),
        ),
        in_specs=[any_] * 10 + [vm, vm] + [any_] * 8 + [vm] * 4,
        out_specs=(any_,) * 10 + (vm,) * 4 + (any_,),
        scratch_shapes=[
            pltpu.VMEM((T, FF), BF), pltpu.VMEM((T, FF), BF), pltpu.VMEM((D, FF), BF),
            pltpu.VMEM((T, D), BF), pltpu.VMEM((T, D), BF), pltpu.VMEM((T, D), BF), pltpu.VMEM((T, D), F32),
            pltpu.VMEM((RING, 2, 4, SHARD, 768), BF), pltpu.VMEM((RS, 4, SHARD, 768), BF),
            pltpu.VMEM((RS, 5, SHARD, 768), BF), pltpu.VMEM((RS, SHARD, 768), BF),
            pltpu.VMEM((RS, 4, SHARD, 768), BF),
            pltpu.VMEM((2, 4, SHARD, 768), F32), pltpu.VMEM((2, 4, SHARD, 768), F32),
            pltpu.VMEM((16, D), F32), pltpu.VMEM((8, D), F32),
            pltpu.VMEM((8, 16, 128), F32), pltpu.VMEM((8, 16, 128), F32), pltpu.VMEM((4, 16, 128), F32),
            dma((17,)), dma((RS,)), dma((RS,)), dma((RS, 3)), dma((RS, 5)), dma((RS,)), dma((RS,)),
            dma((RS, 3)), dma((RS, 4)), dma((2, 4)), dma((2, 4)), dma((4,)), dma((4,)), dma((4,)), dma((4,)),
            dma((8,)), dma((8,)), dma((3,)), dma((4,)),
            *GATHER_SEMS(2),
        ],
        compiler_params=pltpu.CompilerParams(collective_id=2, has_side_effects=True, vmem_limit_bytes=63 * 2**20),
        name="backward",
    )(cot, *fwd, *states)


def fast(
    inputs, segments, cotangent,
    attn_weight, attn_first, attn_second, attn_outer,
    mlp_weight, mlp_first, mlp_second, mlp_outer,
    vector_weight, vector_first, vector_second, vector_outer,
):
    fwd = forward(inputs[0], cotangent[0], segments[0], attn_weight, mlp_weight, vector_weight)
    out = backward(
        cotangent[0],
        fwd,
        (
            attn_weight, attn_first[0], attn_second[0], attn_outer,
            mlp_weight, mlp_first[0], mlp_second[0], mlp_outer,
            vector_weight, jnp.transpose(vector_first, (1, 0, 2)), jnp.transpose(vector_second, (1, 0, 2)), vector_outer,
        ),
    )
    lead = (1, 1, 1, 1, 0, 0, 1, 1, 0, 0, 0, 0, 0, 0)
    return tuple(v[None] if k else v for v, k in zip(finish(out[:14]), lead))


def norm_apply(values, gain, shift):
    centre = values - jnp.mean(values, axis=-1, keepdims=True)
    spread = jnp.mean(centre * centre, axis=-1, keepdims=True)
    return centre * lax.rsqrt(spread + EPS_NORM) * gain + shift


def gelu_tanh(values):
    return jax.nn.gelu(values, approximate=True)


def adam_step(weight, first, second, gradient, step_rate, weight_decay):
    first_new = BETA_ONE * first + (1.0 - BETA_ONE) * gradient
    second_new = BETA_TWO * second + (1.0 - BETA_TWO) * gradient * gradient
    first_hat = first_new / (1.0 - BETA_ONE**STEP)
    second_hat = second_new / (1.0 - BETA_TWO**STEP)
    local_weight = weight - step_rate * (
        first_hat / (jnp.sqrt(second_hat) + ADAM_EPS) + weight_decay * weight
    )
    return (first_new, second_new, weight - local_weight)


def local(
    inputs,
    segments,
    cotangent,
    attn_weight,
    attn_first,
    attn_second,
    attn_outer,
    mlp_weight,
    mlp_first,
    mlp_second,
    mlp_outer,
    vector_weight,
    vector_first,
    vector_second,
    vector_outer,
):
    bf16 = jnp.bfloat16
    f32 = jnp.float32
    attn_cast = attn_weight.astype(bf16)
    mlp_cast = mlp_weight.astype(bf16)
    attn_low, mlp_low, vector_low = (
        lax.all_gather(attn_cast, "fsdp", axis=0, tiled=True),
        lax.all_gather(mlp_cast, "fsdp", axis=1, tiled=True),
        lax.all_gather(vector_weight.astype(bf16), "fsdp", axis=1, tiled=True),
    )
    vectors = vector_low.astype(f32)
    tokens_f = inputs[0].astype(f32)
    seg_ids = segments[0]
    back_f = cotangent[0].astype(f32)
    model_width = attn_low.shape[0]
    head_dim = model_width // HEADS
    score_scale = head_dim ** (-0.5)
    tok_count = tokens_f.shape[0]
    row_count = tok_count // SEQ
    shape_four = (row_count, SEQ, HEADS, head_dim)
    normed_f, norm_pull = jax.vjp(norm_apply, tokens_f, vectors[0], vectors[1])
    normed = normed_f.astype(bf16)
    project = jnp.dot(normed, attn_low[:, : 3 * model_width], preferred_element_type=f32)
    queries = (project[:, :model_width] + vectors[2]).astype(bf16).reshape(shape_four)
    keys_all = project[:, model_width : 2 * model_width].astype(bf16).reshape(shape_four)
    values_all = (
        (project[:, 2 * model_width : 3 * model_width] + vectors[3])
        .astype(bf16)
        .reshape(shape_four)
    )
    scores = (
        jnp.einsum("rqhd,rkhd->rhqk", queries, keys_all, preferred_element_type=f32) * score_scale
    )
    same_seg = (seg_ids[:, :, None] == seg_ids[:, None, :])[:, None]
    masked = jnp.where(same_seg, scores, NEG_LARGE)
    exponent = jnp.exp(masked - jnp.max(masked, axis=-1, keepdims=True))
    soft = exponent / jnp.sum(exponent, axis=-1, keepdims=True)
    probs = soft.astype(bf16)
    mixed = (
        jnp.einsum("rhqk,rkhd->rqhd", probs, values_all, preferred_element_type=f32)
        .reshape(tok_count, model_width)
        .astype(bf16)
    )
    attended = (
        jnp.dot(mixed, attn_low[:, 3 * model_width :], preferred_element_type=f32) + vectors[4]
    )
    residual = tokens_f + attended
    normed_two_f, norm_two_pull = jax.vjp(norm_apply, residual, vectors[5], vectors[6])
    normed_two = normed_two_f.astype(bf16)
    up_pre = jnp.dot(normed_two, mlp_low[0], preferred_element_type=f32) + vectors[8:12].reshape(-1)
    hidden_f, gelu_pull = jax.vjp(gelu_tanh, up_pre)
    hidden = hidden_f.astype(bf16)
    branch = jnp.einsum("nf,df->nd", hidden, mlp_low[1], preferred_element_type=f32) + vectors[7]
    block_out = (residual + branch).astype(bf16)
    d_branch = cotangent[0]
    d_down_bias = jnp.sum(back_f, axis=0)
    grad_down = jnp.einsum("nd,nf->df", d_branch, hidden, preferred_element_type=f32)
    d_hidden = jnp.einsum("nd,df->nf", d_branch, mlp_low[1], preferred_element_type=f32)
    (d_up_f,) = gelu_pull(d_hidden)
    d_up = d_up_f.astype(bf16)
    d_up_bias = jnp.sum(d_up.astype(f32), axis=0)
    grad_up = jnp.einsum("nd,nf->df", normed_two, d_up, preferred_element_type=f32)
    mlp_grad = jnp.stack([grad_up, grad_down])
    d_normed_two = jnp.einsum("nf,df->nd", d_up, mlp_low[0], preferred_element_type=f32)
    d_res_norm, d_gain_two, d_shift_two = norm_two_pull(d_normed_two)
    d_res = back_f + d_res_norm
    d_att = d_res.astype(bf16)
    d_out_bias = jnp.sum(d_att.astype(f32), axis=0)
    grad_out = jnp.einsum("nc,nd->cd", mixed, d_att, preferred_element_type=f32)
    d_mixed = (
        jnp.einsum("nd,cd->nc", d_att, attn_low[:, 3 * model_width :], preferred_element_type=f32)
        .astype(bf16)
        .reshape(shape_four)
    )
    d_values = (
        jnp.einsum("rhqk,rqhd->rkhd", probs, d_mixed, preferred_element_type=f32)
        .reshape(tok_count, model_width)
        .astype(bf16)
    )
    d_probs = jnp.einsum("rqhd,rkhd->rhqk", d_mixed, values_all, preferred_element_type=f32)
    d_scores = (soft * (d_probs - jnp.sum(d_probs * soft, axis=-1, keepdims=True))).astype(bf16)
    d_queries = (
        (
            jnp.einsum("rhqk,rkhd->rqhd", d_scores, keys_all, preferred_element_type=f32)
            * score_scale
        )
        .reshape(tok_count, model_width)
        .astype(bf16)
    )
    d_keys = (
        (jnp.einsum("rhqk,rqhd->rkhd", d_scores, queries, preferred_element_type=f32) * score_scale)
        .reshape(tok_count, model_width)
        .astype(bf16)
    )
    d_query_bias = jnp.sum(d_queries.astype(f32), axis=0)
    d_value_bias = jnp.sum(d_values.astype(f32), axis=0)
    d_project = jnp.concatenate([d_queries, d_keys, d_values], axis=1)
    grad_qkv = jnp.einsum("nc,nd->cd", normed, d_project, preferred_element_type=f32)
    d_normed = jnp.einsum(
        "nd,cd->nc", d_project, attn_low[:, : 3 * model_width], preferred_element_type=f32
    )
    d_tok_norm, d_gain_one, d_shift_one = norm_pull(d_normed)
    input_grad = d_res + d_tok_norm
    attn_grad = jnp.concatenate([grad_qkv, grad_out], axis=1)
    vector_grad = jnp.concatenate(
        [
            jnp.stack(
                [
                    d_gain_one,
                    d_shift_one,
                    d_query_bias,
                    d_value_bias,
                    d_out_bias,
                    d_gain_two,
                    d_shift_two,
                    d_down_bias,
                ]
            ),
            d_up_bias.reshape(4, model_width),
        ],
        axis=0,
    )
    attn_sum, mlp_sum, vector_sum = (
        lax.psum_scatter(attn_grad.astype(bf16), "fsdp", scatter_dimension=0, tiled=True).astype(f32),
        lax.psum_scatter(mlp_grad.astype(bf16), "fsdp", scatter_dimension=1, tiled=True).astype(f32),
        lax.psum_scatter(vector_grad, "fsdp", scatter_dimension=1, tiled=True),
    )
    attn_moment, attn_square, attn_delta = adam_step(
        attn_weight, attn_first[0], attn_second[0], attn_sum, RATE_MATRIX, WEIGHT_DECAY
    )
    mlp_moment, mlp_square, mlp_delta = adam_step(
        mlp_weight, mlp_first[0], mlp_second[0], mlp_sum, RATE_MATRIX, WEIGHT_DECAY
    )
    vector_moment, vector_square, vector_delta = adam_step(
        vector_weight, vector_first[0], vector_second[0], vector_sum, RATE_VECTOR, 0.0
    )
    group_count = lax.axis_size("group")
    attn_total, mlp_total, vector_total = (
        lax.psum(attn_delta.astype(jnp.bfloat16), "group").astype(jnp.float32),
        lax.psum(mlp_delta.astype(jnp.bfloat16), "group").astype(jnp.float32),
        lax.psum(vector_delta.astype(jnp.bfloat16), "group").astype(jnp.float32),
    )
    attn_mean = attn_total / group_count
    mlp_mean = mlp_total / group_count
    vector_mean = vector_total / group_count
    attn_momentum = OUTER_MOMENTUM * attn_outer + attn_mean
    mlp_momentum = OUTER_MOMENTUM * mlp_outer + mlp_mean
    vector_momentum = OUTER_MOMENTUM * vector_outer + vector_mean
    attn_master = attn_weight - OUTER_RATE * (attn_mean + OUTER_MOMENTUM * attn_momentum)
    mlp_master = mlp_weight - OUTER_RATE * (mlp_mean + OUTER_MOMENTUM * mlp_momentum)
    vector_master = vector_weight - OUTER_RATE * (vector_mean + OUTER_MOMENTUM * vector_momentum)
    return (
        block_out[None],
        input_grad[None],
        attn_moment[None],
        attn_square[None],
        attn_momentum,
        attn_master,
        mlp_moment[None],
        mlp_square[None],
        mlp_momentum,
        mlp_master,
        vector_moment[None],
        vector_square[None],
        vector_momentum,
        vector_master,
    )


def solution(mesh):
    in_specs = (
        P("group", "fsdp", None),
        P("group", "fsdp", None),
        P("group", "fsdp", None),
        P("fsdp", None),
        P("group", "fsdp", None),
        P("group", "fsdp", None),
        P("fsdp", None),
        P(None, "fsdp", None),
        P("group", None, "fsdp", None),
        P("group", None, "fsdp", None),
        P(None, "fsdp", None),
        P(None, "fsdp"),
        P("group", None, "fsdp"),
        P("group", None, "fsdp"),
        P(None, "fsdp"),
    )
    out_specs = (
        P("group", "fsdp", None),
        P("group", "fsdp", None),
        P("group", "fsdp", None),
        P("group", "fsdp", None),
        P("fsdp", None),
        P("fsdp", None),
        P("group", None, "fsdp", None),
        P("group", None, "fsdp", None),
        P(None, "fsdp", None),
        P(None, "fsdp", None),
        P("group", None, "fsdp"),
        P("group", None, "fsdp"),
        P(None, "fsdp"),
        P(None, "fsdp"),
    )
    fits = mesh.shape["group"] == 4 and mesh.shape["fsdp"] == 8
    return jax.shard_map(fast if fits else local, mesh=mesh, in_specs=in_specs, out_specs=out_specs, check_vma=False)
```

```python
import functools

import jax
import jax.numpy as jnp
from jax import lax
from jax.experimental import pallas as pl
from jax.experimental.pallas import tpu as pltpu
from jax.sharding import PartitionSpec as P

EPS_NORM = 1e-05
NEG_LARGE = -1e30
HEADS = 12
SEQ = 64
STEP = 10
BETA_ONE = 0.9
BETA_TWO = 0.999
ADAM_EPS = 1e-08
RATE_MATRIX = 0.05
RATE_VECTOR = 0.5
WEIGHT_DECAY = 0.1
OUTER_RATE = 0.7
OUTER_MOMENTUM = 0.9


ORDER_FORWARD = (
    ("cast", 0), ("g", 0, 0), ("cast", 1), ("g", 2, 0), ("g", 1, 0), ("xs", 0), ("g", 3, 0), ("cast", 2),
    ("g", 4, 0), ("xs", 1), ("xs", 2), ("g", 0, 1), ("g", 2, 1), ("vec", 0), ("g", 0, 2), ("xs", 3), ("g", 1, 1),
    ("g", 0, 3), ("g", 1, 2), ("g", 0, 4), ("g", 1, 3), ("g", 1, 4), ("g", 2, 2), ("g", 0, 5), ("g", 3, 1),
    ("cs", 0), ("ln", 0, 4), ("g", 2, 3), ("g", 4, 1), ("g", 1, 5), ("g", 3, 2), ("g", 0, 6), ("g", 1, 6),
    ("v", 0, 4), ("qk", 0, 4), ("g", 2, 4), ("at", 2, 2), ("g", 3, 3), ("at", 0, 2), ("g", 3, 4), ("g", 4, 2),
    ("g", 2, 5), ("on", 0, 4), ("g", 4, 3), ("g", 2, 6), ("u", 0, 0, 2), ("g", 3, 5), ("g", 4, 4), ("g", 3, 6),
    ("u", 0, 2, 2), ("u", 1, 0, 2), ("u", 1, 2, 2), ("g", 4, 5), ("g", 4, 6), ("end", 0),
)

ORDER_BACKWARD = (
    ("st", 0), ("g", 0, 0), ("gd", 0, 2), ("r", 0, 0), ("il", 1), ("il", 0), ("r", 1, 0), ("g", 0, 1), ("r", 0, 1),
    ("r", 1, 1), ("gd", 2, 2), ("g", 0, 2), ("r", 3, 0), ("r", 2, 0), ("dh", 0, 0, 4), ("r", 2, 1), ("r", 0, 2),
    ("r", 3, 1), ("g", 0, 3), ("gu", 0, 2), ("r", 4, 0), ("r", 0, 3), ("r", 5, 0), ("g", 0, 4), ("r", 1, 2),
    ("g", 0, 5), ("r", 4, 1), ("r", 0, 4), ("r", 5, 1), ("g", 0, 6), ("dh", 1, 0, 4), ("r", 1, 3), ("gu", 2, 2),
    ("r", 6, 0), ("r", 1, 4), ("r", 2, 2), ("r", 7, 0), ("bo", 0, 4), ("r", 2, 3), ("ld", 0), ("r", 3, 2),
    ("r", 0, 5), ("r", 6, 1), ("n2", 0, 2), ("r", 2, 4), ("r", 3, 3), ("r", 1, 5), ("r", 0, 6), ("r", 4, 2),
    ("r", 7, 1), ("n2", 2, 2), ("ld", 1), ("r", 0, 7), ("r", 1, 6), ("go", 0), ("r", 3, 4), ("r", 5, 2),
    ("r", 4, 3), ("r", 8, 0), ("r", 1, 7), ("il", 2), ("il", 3), ("r", 2, 5), ("dm", 0, 4), ("r", 3, 5),
    ("r", 5, 3), ("ab", 0, 2), ("r", 6, 2), ("r", 4, 4), ("r", 2, 6), ("r", 8, 1), ("r", 3, 6), ("r", 5, 4),
    ("r", 7, 2), ("r", 2, 7), ("il", 4), ("r", 3, 7), ("r", 4, 5), ("r", 6, 3), ("ab", 2, 2), ("r", 7, 3),
    ("r", 4, 6), ("il", 5), ("r", 5, 5), ("r", 8, 2), ("r", 6, 4), ("gq", 0, 2), ("r", 9, 0), ("r", 4, 7),
    ("il", 6), ("r", 5, 6), ("r", 10, 0), ("r", 6, 5), ("r", 8, 3), ("r", 7, 4), ("r", 9, 1), ("n1", 0, 2),
    ("r", 8, 4), ("r", 6, 6), ("r", 5, 7), ("gq", 2, 1), ("r", 9, 2), ("il", 7), ("r", 7, 5), ("r", 11, 0),
    ("r", 10, 1), ("n1", 2, 2), ("r", 10, 2), ("r", 9, 3), ("r", 7, 6), ("r", 11, 1), ("vs", 0), ("r", 6, 7),
    ("il", 8), ("r", 8, 5), ("r", 7, 7), ("r", 10, 3), ("r", 9, 4), ("il", 9), ("r", 11, 2), ("r", 8, 6),
    ("r", 10, 4), ("r", 11, 3), ("r", 8, 7), ("r", 9, 5), ("il", 10), ("ic", 0), ("r", 11, 4), ("r", 10, 5),
    ("r", 9, 6), ("r", 9, 7), ("va", 0), ("il", 11), ("r", 11, 5), ("r", 10, 6), ("r", 10, 7), ("r", 11, 6),
    ("vo", 0), ("r", 11, 7),
)


MESH = pl.DeviceIdType.MESH
BF = jnp.bfloat16
F32 = jnp.float32
D = 768
FF = 3072
T = 1024
TB = 256
SHARD = 96
GELU_C = 0.7978845608028654
GELU_A = 0.044715
SCALE = 0.125


def dot_nn(a, b):
    return jnp.dot(a, b, preferred_element_type=F32)


def dot_nt(a, b):
    return lax.dot_general(a, b, (((1,), (1,)), ((), ())), preferred_element_type=F32)


def dot_tn(a, b):
    return lax.dot_general(a, b, (((0,), (0,)), ((), ())), preferred_element_type=F32)


def coords():
    g = lax.axis_index("group")
    f = lax.axis_index("fsdp")
    return g // 2, g % 2, f // 2, f % 2


def dev(x, c, z, y):
    return (2 * x + c, 2 * z + y)


def remote(src, dst, ssem, rsem, to):
    return pltpu.make_async_remote_copy(
        src_ref=src, dst_ref=dst, send_sem=ssem, recv_sem=rsem, device_id=to, device_id_type=MESH
    )


def norm_parts(v):
    centre = v - jnp.mean(v, axis=-1, keepdims=True)
    spread = jnp.mean(centre * centre, axis=-1, keepdims=True)
    scale = lax.rsqrt(spread + EPS_NORM)
    return centre * scale, scale


def head_masks():
    lane = lax.broadcasted_iota(jnp.int32, (1, 128), 1)
    low = (lane < 64).astype(F32).astype(BF)
    high = (lane >= 64).astype(F32).astype(BF)
    return low, high


def segment_bias(seg_ref, i):
    row = seg_ref[pl.ds(i, 1), :]
    classes = lax.broadcasted_iota(jnp.int32, (16, 128), 0)
    hot = (classes == row).astype(F32).astype(BF)
    same = dot_tn(hot, hot)
    bias = (same - 1.0) * (-NEG_LARGE)
    return jnp.concatenate([bias, bias], axis=1)


def soft_pair(q, k2, bias):
    s = dot_nt(q, k2) * SCALE + bias
    halves = []
    for h in (0, 1):
        part = s[:, 128 * h : 128 * h + 128]
        e = jnp.exp(part - jnp.max(part, axis=-1, keepdims=True))
        halves.append(e * (1.0 / jnp.sum(e, axis=-1, keepdims=True)))
    return jnp.concatenate(halves, axis=1)


def stack_heads(v, low, high):
    return jnp.concatenate([v * low, v * high], axis=0)


def gather_stages(view, sems, where, shift=0):
    x, c, z, y = where
    ys, yr, us, ds, zr, xs, xr, cs, cr = sems
    f = 2 * z + y
    other = 2 * z + 1 - y

    def rows(i):
        return pl.ds(pl.multiple_of(i * SHARD, 32), SHARD)

    def pair(i):
        return pl.ds(pl.multiple_of(i * 2 * SHARD, 64), 2 * SHARD)

    mine = 2 * x + c
    across = 2 * (1 - x) + c
    sib = 2 * x + 1 - c
    sib_across = 2 * (1 - x) + 1 - c

    def at(p, r, q):
        return view(p, r, pl.ds(pl.multiple_of(1536 * ((p + shift) % 2) + 384 * q, 128), 384))

    def cp_y(p, r):
        return remote(at(p, r, mine), at(p, r, mine), ys.at[p], yr.at[p], dev(x, c, z, 1 - y))

    def cp_up(p, i):
        return remote(at(p, pair(i), mine), at(p, pair(i), mine), us.at[p, i], zr.at[p, i], dev(x, c, z + 1, y))

    def cp_down(p, i):
        return remote(at(p, pair(i), mine), at(p, pair(i), mine), ds.at[p, i], zr.at[p, i], dev(x, c, z - 1, y))

    def cp_x(p, r, i, q):
        return remote(at(p, r, q), at(p, r, q), xs.at[p, i], xr.at[p, i], dev(1 - x, c, z, y))

    def cp_c(p, r, i, q, k):
        return remote(at(p, r, q), at(p, r, q), cs.at[p, 4 * k + i], cr.at[p, 4 * k + i], dev(x, 1 - c, z, y))

    def others(fn):
        for k in (1, 2, 3):
            pl.when(z >= k)(functools.partial(fn, z - k))
            pl.when(z + k <= 3)(functools.partial(fn, z + k))

    def sa(p):
        cp_y(p, rows(f)).start()

    def sb(p):
        cp_y(p, rows(other)).wait_recv()
        pl.when(z < 3)(lambda: cp_up(p, z).start())
        pl.when(z > 0)(lambda: cp_down(p, z).start())
        cp_x(p, rows(other), z, mine).start()
        cp_c(p, rows(other), z, mine, 0).start()

    def hop(k, p):
        def from_below():
            i = z - k
            cp_up(p, i).wait_recv()
            pl.when(z < 3)(lambda: cp_up(p, i).start())
            cp_x(p, pair(i), i, mine).start()
            cp_c(p, pair(i), i, mine, 0).start()

        def from_above():
            i = z + k
            cp_down(p, i).wait_recv()
            pl.when(z > 0)(lambda: cp_down(p, i).start())
            cp_x(p, pair(i), i, mine).start()
            cp_c(p, pair(i), i, mine, 0).start()

        pl.when(z >= k)(from_below)
        pl.when(z + k <= 3)(from_above)

    def sf(p):
        cp_x(p, rows(other), z, across).wait_recv()
        cp_c(p, rows(other), z, across, 1).start()

        def fwd(i):
            cp_x(p, pair(i), i, across).wait_recv()
            cp_c(p, pair(i), i, across, 1).start()

        others(fwd)

    def sg(p):
        cp_c(p, rows(other), z, sib, 0).wait_recv()
        cp_c(p, rows(other), z, sib_across, 1).wait_recv()

        def got(i):
            cp_c(p, pair(i), i, sib, 0).wait_recv()
            cp_c(p, pair(i), i, sib_across, 1).wait_recv()

        others(got)

    def drain(p):
        cp_y(p, rows(f)).wait_send()
        pl.when(z < 3)(lambda: cp_up(p, z).wait_send())
        pl.when(z > 0)(lambda: cp_down(p, z).wait_send())
        cp_x(p, rows(other), z, mine).wait_send()
        cp_c(p, rows(other), z, mine, 0).wait_send()
        cp_c(p, rows(other), z, across, 1).wait_send()
        for k in (1, 2, 3):

            @pl.when(z >= k)
            def _():
                pl.when(z < 3)(lambda: cp_up(p, z - k).wait_send())

            @pl.when(z + k <= 3)
            def _():
                pl.when(z > 0)(lambda: cp_down(p, z + k).wait_send())

        def sent(i):
            cp_x(p, pair(i), i, mine).wait_send()
            cp_c(p, pair(i), i, mine, 0).wait_send()
            cp_c(p, pair(i), i, across, 1).wait_send()

        others(sent)

    stages = [sa, sb, functools.partial(hop, 1), functools.partial(hop, 2), functools.partial(hop, 3), sf, sg]
    return stages, drain


GATHER_SEMS = lambda n: [
    pltpu.SemaphoreType.DMA((n,)),
    pltpu.SemaphoreType.DMA((n,)),
    pltpu.SemaphoreType.DMA((n, 4)),
    pltpu.SemaphoreType.DMA((n, 4)),
    pltpu.SemaphoreType.DMA((n, 4)),
    pltpu.SemaphoreType.DMA((n, 4)),
    pltpu.SemaphoreType.DMA((n, 4)),
    pltpu.SemaphoreType.DMA((n, 8)),
    pltpu.SemaphoreType.DMA((n, 8)),
]
PIECES = 5


def forward_kernel(
    x_in, cot_in, seg_raw, aw, mw, vw,
    w_out, qkvm_out, hid_out, gp_out, nrm_out, n2_out, res_out, xv_out, cotv_out, wd_out, vec_out, seg_out,
    w, xv, nrm, qkvm, res, n2, hid, gp, vec, seg, seg_in, tiles, ub,
    xsnd, xrcv, csnd, crcv, gsnd, grcv, vsnd, vrcv, osem,
    *gsems,
):
    where = coords()
    x, c, z, y = where
    f = 2 * z + y
    swapped = c != y
    partner = dev(x, y, z, c)

    barrier = pltpu.get_barrier_semaphore()

    def greet(to):
        pl.semaphore_signal(barrier, inc=1, device_id=to, device_id_type=MESH)

    for k in range(1, 8):
        greet((2 * x + c, (f + k) % 8))
    greet(dev(x, 1 - c, z, y))
    greet(dev(1 - x, c, z, y))
    pl.when(swapped)(lambda: greet(partner))

    for i in range(8):
        seg_in[i : i + 1, :] = jnp.concatenate([seg_raw[2 * i : 2 * i + 1, :], seg_raw[2 * i + 1 : 2 * i + 2, :] + 8], axis=1)
    own = pl.ds(pl.multiple_of(f * SHARD, 32), SHARD)
    tiles[pl.ds(f, 1)] = jnp.zeros((1, 16, 128), F32)
    tiles[f, 0:12, 0:SHARD] = vw[...].astype(BF).astype(F32)

    pl.semaphore_wait(barrier, 9 + swapped.astype(jnp.int32))

    stages, drain = gather_stages(lambda p, r, q: w.at[p // 2, r, q], gsems, where)

    def cp_vec(k, j):
        return remote(tiles.at[j], tiles.at[j], vsnd.at[k - 1], vrcv.at[k - 1], (2 * x + c, (f + k) % 8))

    def tok(b, n=1):
        if isinstance(b, int):
            return pl.ds(b * TB, n * TB)
        return pl.ds(pl.multiple_of(b * TB, TB), n * TB)

    def span(fn, lo, n):
        def step(b, carry):
            fn(b)
            return carry

        lax.fori_loop(lo, lo + n, step, 0)

    def x_remote(b):
        return remote(x_in.at[tok(b)], xv.at[tok(b)], xsnd.at[b], xrcv.at[b], partner)

    def x_local(b):
        return pltpu.make_async_copy(x_in.at[tok(b)], xv.at[tok(b)], xrcv.at[b])

    def cot_remote():
        return remote(cot_in, cotv_out, csnd, crcv, partner)

    def seg_remote():
        return remote(seg_in, seg, gsnd, grcv, partner)

    outs = []

    def write(src, dst):
        cp = pltpu.make_async_copy(src, dst, osem.at[len(outs)])
        cp.start()
        outs.append(cp)

    def cast(m):
        if m == 1:
            w[1, own, :] = mw[0].astype(BF)
            return
        if m == 2:
            w[2, own, 0:1536] = mw[1, :, 0:1536].astype(BF)
            return
        w[0, own, :] = aw[...].astype(BF)
        for k in range(1, 8):
            cp_vec(k, f).start()

        @pl.when(swapped)
        def _():
            seg_remote().start()

        @pl.when(jnp.logical_not(swapped))
        def _():
            seg[...] = seg_in[...]
            for b in range(4):
                x_local(b).start()

    def send_x(b):
        pl.when(swapped)(lambda: x_remote(b).start())

    def send_cot(k):
        pl.when(swapped)(lambda: cot_remote().start())

    def gather(p, s):
        stages[s](p)
        if s == 6 and p % 2 == 1:
            write(w.at[p // 2], w_out.at[p // 2])
        if s == 6 and p == 4:
            write(w.at[2, :, 0:1536], wd_out)

    def vectors():
        for k in range(1, 8):
            cp_vec(k, (f + 8 - k) % 8).wait_recv()
        total = jnp.zeros((16, D), F32)
        r = lax.broadcasted_iota(jnp.int32, (128, D), 0)
        q = lax.broadcasted_iota(jnp.int32, (128, D), 1)
        for j in range(8):
            pick = jnp.logical_and(q == r + SHARD * j, r < SHARD).astype(F32).astype(BF)
            total = total + dot_nn(tiles[j].astype(BF), pick)
        vec[...] = total
        for k in range(4):
            ub[0:1, D * k : D * k + D] = total[8 + k : 9 + k, :]

    def first_norm(b):
        @pl.when(swapped)
        def _():
            x_remote(b).wait_recv()

        @pl.when(jnp.logical_not(swapped))
        def _():
            x_local(b).wait()

        hat, _ = norm_parts(xv[tok(b), :].astype(F32))
        nrm[tok(b), :] = (hat * vec[0:1, :] + vec[1:2, :]).astype(BF)

    def queries_keys(b):
        r = dot_nn(nrm[tok(b), :], w[0, :, 0:1536])
        qkvm[tok(b), 0:D] = (r[:, 0:D] + vec[2:3, :]).astype(BF)
        qkvm[tok(b), D : 2 * D] = r[:, D : 2 * D].astype(BF)

    def values(b):
        r = dot_nn(nrm[tok(b), :], w[0, :, 1536:2304])
        qkvm[tok(b), 2 * D : 3 * D] = (r + vec[3:4, :]).astype(BF)

    def attention(i):
        low, high = head_masks()
        bias = segment_bias(seg, i)
        r = pl.ds(pl.multiple_of(i * 128, 128), 128)
        for p in range(6):
            col = 128 * p
            q = qkvm[r, col : col + 128]
            k2 = stack_heads(qkvm[r, D + col : D + col + 128], low, high)
            v2 = stack_heads(qkvm[r, 2 * D + col : 2 * D + col + 128], low, high)
            probs = soft_pair(q, k2, bias).astype(BF)
            qkvm[r, 3 * D + col : 3 * D + col + 128] = dot_nn(probs, v2).astype(BF)

    greeted = []

    def attend(lo, n):
        if not greeted:
            greeted.append(lo)
            pl.when(swapped)(lambda: seg_remote().wait_recv())
        span(attention, 2 * lo, 2 * n)
        write(qkvm.at[tok(lo, n)], qkvm_out.at[tok(lo, n)])

    def out_norm(b):
        att = dot_nn(qkvm[tok(b), 3 * D :], w[0, :, 2304:3072]) + vec[4:5, :]
        r = xv[tok(b), :].astype(F32) + att
        res[tok(b), :] = r
        hat, _ = norm_parts(r)
        n2[tok(b), :] = (hat * vec[5:6, :] + vec[6:7, :]).astype(BF)

    def up(half, b):
        for k in range(2):
            lo = 1536 * half + 768 * k
            u = dot_nn(n2[tok(b), :], w[1, :, lo : lo + 768]) + ub[0:1, lo : lo + 768]
            u2 = u * u
            t = jnp.tanh(u * (GELU_C + (GELU_C * GELU_A) * u2))
            h = 0.5 + 0.5 * t
            out = u * h
            hid[tok(b), lo : lo + 768] = out.astype(BF)
            slope = h + out * (1.0 - h) * (2.0 * GELU_C + (6.0 * GELU_C * GELU_A) * u2)
            gp[tok(b), lo : lo + 768] = slope.astype(BF)

    def spanned(fn, *pairs):
        def run(lo, n):
            span(fn, lo, n)
            for src, dst in pairs:
                write(src.at[tok(lo, n)], dst.at[tok(lo, n)])

        return run

    def up_half(half, lo, n):
        span(functools.partial(up, half), lo, n)
        if half:
            write(hid.at[tok(lo, n)], hid_out.at[tok(lo, n)])
            write(gp.at[tok(lo, n)], gp_out.at[tok(lo, n)])

    does = {
        "g": gather, "cast": cast, "xs": send_x, "cs": send_cot, "vec": lambda k: vectors(),
        "ln": spanned(first_norm, (xv, xv_out), (nrm, nrm_out)), "qk": spanned(queries_keys), "v": spanned(values),
        "at": attend, "on": spanned(out_norm, (res, res_out), (n2, n2_out)), "u": up_half, "end": lambda k: None,
    }
    for name, *at in ORDER_FORWARD:
        does[name](*at)
    vec_out[...] = vec[...]
    seg_out[...] = seg[...]

    for p in range(PIECES):
        drain(p)
    for k in range(1, 8):
        cp_vec(k, f).wait_send()

    @pl.when(swapped)
    def _():
        seg_remote().wait_send()
        for b in range(4):
            x_remote(b).wait_send()
        cot_remote().wait()

    for cp in outs:
        cp.wait()


def forward(x, cot, seg, aw, mw, vw):
    any_ = pl.BlockSpec(memory_space=pl.ANY)
    vm = pl.BlockSpec(memory_space=pltpu.VMEM)
    wide = jax.ShapeDtypeStruct((T, FF), BF)
    slim = jax.ShapeDtypeStruct((T, D), BF)
    dma = pltpu.SemaphoreType.DMA
    return pl.pallas_call(
        forward_kernel,
        out_shape=(
            jax.ShapeDtypeStruct((2, D, FF), BF), wide, wide, wide, slim, slim,
            jax.ShapeDtypeStruct((T, D), F32), slim, slim, jax.ShapeDtypeStruct((D, 1536), BF),
            jax.ShapeDtypeStruct((16, D), F32), jax.ShapeDtypeStruct((8, 128), jnp.int32),
        ),
        in_specs=[any_, any_, vm, vm, vm, vm],
        out_specs=(any_,) * 10 + (vm, vm),
        scratch_shapes=[
            pltpu.VMEM((3, D, FF), BF), pltpu.VMEM((T, D), BF), pltpu.VMEM((T, D), BF), pltpu.VMEM((T, FF), BF),
            pltpu.VMEM((T, D), F32), pltpu.VMEM((T, D), BF), pltpu.VMEM((T, FF), BF), pltpu.VMEM((T, FF), BF),
            pltpu.VMEM((16, D), F32), pltpu.VMEM((8, 128), jnp.int32), pltpu.VMEM((8, 128), jnp.int32),
            pltpu.VMEM((8, 16, 128), F32),
            pltpu.VMEM((1, FF), F32),
            dma((4,)), dma((4,)), dma, dma, dma, dma, dma((7,)), dma((7,)), dma((40,)),
            *GATHER_SEMS(PIECES),
        ],
        compiler_params=pltpu.CompilerParams(collective_id=1, has_side_effects=True, vmem_limit_bytes=60 * 2**20),
        name="forward",
    )(x, cot, seg, aw, mw, vw)


def final_kernel(*refs):
    ins, small, outs, small_outs = refs[:10], refs[10:14], refs[14:24], refs[24:28]
    bufs, rsem, wsem = refs[28:38], refs[38], refs[39]
    reads = [pltpu.make_async_copy(a, b, rsem.at[k]) for k, (a, b) in enumerate(zip(ins, bufs))]
    for cp in reads:
        cp.start()
    for k in range(4):
        if k < 2:
            for r in range(12):
                small_outs[k][r] = small[k][r : r + 1, :]
        else:
            small_outs[k][...] = small[k][...]
    writes = [pltpu.make_async_copy(b, a, wsem.at[k]) for k, (a, b) in enumerate(zip(outs, bufs))]
    for r, w in zip(reads, writes):
        r.wait()
        w.start()
    for w in writes:
        w.wait()


def finish(arrays):
    any_ = pl.BlockSpec(memory_space=pl.ANY)
    vm = pl.BlockSpec(memory_space=pltpu.VMEM)
    big, small = arrays[:10], arrays[10:14]
    shapes = [jax.ShapeDtypeStruct(a.shape, a.dtype) for a in big]
    thin = jax.ShapeDtypeStruct((12, 1, SHARD), F32)
    out = pl.pallas_call(
        final_kernel,
        out_shape=(*shapes, thin, thin, *[jax.ShapeDtypeStruct(a.shape, a.dtype) for a in small[2:]]),
        in_specs=[any_] * 10 + [vm] * 4,
        out_specs=(any_,) * 10 + (vm,) * 4,
        scratch_shapes=[pltpu.VMEM(a.shape, a.dtype) for a in big]
        + [pltpu.SemaphoreType.DMA((10,)), pltpu.SemaphoreType.DMA((10,))],
        compiler_params=pltpu.CompilerParams(vmem_limit_bytes=63 * 2**20),
        name="finish",
    )(*big, *small)
    return (*out[:10], jnp.transpose(out[10], (1, 0, 2)), jnp.transpose(out[11], (1, 0, 2)), out[12], out[13])


RS = 12
RING = 2


def adam_parts(first, second, weight, gradient, rate, decay):
    first_new = BETA_ONE * first + (1.0 - BETA_ONE) * gradient
    second_new = BETA_TWO * second + (1.0 - BETA_TWO) * gradient * gradient
    first_hat = first_new * (1.0 / (1.0 - BETA_ONE**STEP))
    second_hat = second_new * (1.0 / (1.0 - BETA_TWO**STEP))
    delta = rate * (first_hat / (jnp.sqrt(second_hat) + ADAM_EPS) + decay * weight)
    return first_new, second_new, delta


def backward_kernel(
    cot_in, w_in, qkvm_in, hid_in, gp_in, nrm_in, n2_in, res_in, xv_in, cotv_in, wd_in, vec, seg,
    aw, a1, a2, ao, mw, m1, m2, mo, vw, v1, v2, vo,
    out_o, ig_o, am_o, as_o, ap_o, aq_o, mm_o, ms_o, mp_o, mq_o, vm_o, vs_o, vp_o, vq_o, ig_land,
    A, B, W, cot, n2, E, R, G, S, ZI, FIN, DL, IN, OUT, vg, ubs, vsl, vrc, vdl,
    lsem, d2s, d2r, zs, zr, fs, fr, ls, lr, isem, osem, bos, bor, igs, igr, vss, vsr, vds, vdr, *gsems,
):
    x, c, z, y = coords()
    f = 2 * z + y
    g = 2 * x + c
    swapped = c != y
    kept = jnp.logical_not(swapped)
    partner = dev(x, y, z, c)

    barrier = pltpu.get_barrier_semaphore()

    def greet(to):
        pl.semaphore_signal(barrier, inc=1, device_id=to, device_id_type=MESH)

    me16 = c * 8 + f
    for k in range(1, 16):
        other = (me16 + k) % 16
        greet((2 * x + other // 8, other % 8))
    greet(dev(1 - x, c, z, y))
    greet(dev(1 - x, 1 - c, z, y))

    def tok(b, n=1):
        if isinstance(b, int):
            return pl.ds(b * TB, n * TB)
        return pl.ds(pl.multiple_of(b * TB, TB), n * TB)

    def span(fn, lo, n):
        def step(b, carry):
            fn(b)
            return carry

        lax.fori_loop(lo, lo + n, step, 0)

    def spanned(fn, *cps):
        def run(lo, n):
            once(*cps)
            span(fn, lo, n)

        return run

    own = pl.ds(pl.multiple_of(f * SHARD, 32), SHARD)
    stages, gather_drain = gather_stages(lambda p, r, q: W.at[r, q], gsems, (x, c, z, y), 1)

    def load(src, dst, k):
        return pltpu.make_async_copy(src, dst, lsem.at[k])

    ld_cot = load(cotv_in, cot, 0)
    ld_own = load(cot_in, cot, 0)
    ld_hid = load(hid_in, A, 1)
    ld_own_w = [load(mw.at[1, :, pl.ds(768 * k, 768)], IN.at[0, k], 11 + k) for k in (2, 3)]
    ld_wd = load(wd_in, W.at[:, 0:1536], 2)
    ld_gp = load(gp_in, B, 3)
    ld_res = load(res_in, R, 4)
    ld_n2 = load(n2_in, n2, 5)
    ld_wu = load(w_in.at[1], W, 6)
    ld_wa = load(w_in.at[0], W, 7)
    ld_qkvm = load(qkvm_in, A, 8)
    ld_nrm = load(nrm_in, E, 9)
    ld_xv = load(xv_in, cot, 10)
    pl.when(swapped)(lambda: ld_cot.start())
    pl.when(kept)(lambda: ld_own.start())
    for cp in (*ld_own_w, ld_hid, ld_wd, ld_gp, ld_res, ld_n2):
        cp.start()
    vg[...] = jnp.zeros((16, D), F32)
    vsl[...] = jnp.zeros((8, 16, 128), F32)
    vdl[...] = jnp.zeros((4, 16, 128), F32)
    for k, cp in zip((2, 3), ld_own_w):
        cp.wait()
        W[own, 768 * k : 768 * k + 768] = IN[0, k].astype(BF)
    pl.semaphore_wait(barrier, 17)

    def wide(i, n=768):
        return pl.ds(i * n if isinstance(i, int) else pl.multiple_of(i * n, n), n)

    ones = jnp.ones((16, T), BF)

    def gradient(lhs, rhs, slot):
        out = dot_tn(lhs, rhs)
        for j in range(8):
            G[slot, j % 2, j // 2] = out[SHARD * j : SHARD * j + SHARD].astype(BF)

    def t_down(lo, n):
        if lo == 0:
            ld_cot.wait()
            ld_hid.wait()
            vg[7:8, :] = dot_nn(ones, cot[...])[0:1, :]
        span(lambda v: gradient(cot[...], A[:, wide(v)], v % RING), lo, n)

    def out_remote(b):
        return remote(E.at[tok(b)], out_o.at[tok(b)], bos.at[b], bor.at[b], partner)

    def out_local(b):
        return pltpu.make_async_copy(E.at[tok(b)], out_o.at[tok(b)], bor.at[b])

    waited = set()

    def once(*cps):
        for cp in cps:
            if id(cp) not in waited:
                waited.add(id(cp))
                cp.wait()

    def hidden_back(half, b):
        for k in (2 * half, 2 * half + 1):
            lo = 768 * k
            dh = dot_nn(cot[tok(b), :], W[:, lo : lo + 768])
            B[tok(b), lo : lo + 768] = (dh * B[tok(b), lo : lo + 768].astype(F32)).astype(BF)

    def block_output(b):
        branch = dot_nt(A[tok(b), :], W[...])
        E[tok(b), :] = (R[tok(b), :] + branch + vec[7:8, :]).astype(BF)
        send_out(b)

    def send_out(b):
        pl.when(swapped)(lambda: out_remote(b).start())
        pl.when(kept)(lambda: out_local(b).start())

    def loads(k):
        if k == 0:
            gather_drain(0)
            ld_wu.start()
            ld_qkvm.start()
            return
        ld_wa.start()
        ld_xv.start()
        for b in range(4):
            pl.when(swapped)(lambda: out_remote(b).wait_send())
            pl.when(kept)(lambda: out_local(b).wait())
        ld_nrm.start()

    def t_up(lo, n):
        once(ld_n2)

        def one(u):
            ubs[pl.ds(u, 1), :] = dot_nn(ones, B[:, wide(u)])[0:1, :]
            gradient(n2[...], B[:, wide(u)], u % RING)

        span(one, lo, n)
        if lo + n == 4:
            vg[8:12, :] = ubs[0:4, :]

    def norm_back(dn, v, gain):
        hat, scale = norm_parts(v)
        e = dn * gain
        d = (e - jnp.mean(e, axis=-1, keepdims=True) - hat * jnp.mean(e * hat, axis=-1, keepdims=True)) * scale
        return d, jnp.sum(dn * hat, axis=0, keepdims=True), jnp.sum(dn, axis=0, keepdims=True)

    def second_norm(b):
        dn = dot_nt(B[tok(b), :], W[...])
        d, dgain, dshift = norm_back(dn, R[tok(b), :], vec[5:6, :])
        d = d + cot[tok(b), :].astype(F32)
        R[tok(b), :] = d
        B[tok(b), 3 * D :] = d.astype(BF)
        vg[5:6, :] = vg[5:6, :] + dgain
        vg[6:7, :] = vg[6:7, :] + dshift

    def t_out(k):
        once(ld_qkvm)
        vg[4:5, :] = dot_nn(ones, B[:, 3 * D :])[0:1, :]
        gradient(A[:, 3 * D :], B[:, 3 * D :], 8 % RING)

    def mixed_back(b):
        A[tok(b), 3 * D :] = dot_nt(B[tok(b), 3 * D :], W[:, 3 * D :]).astype(BF)

    def attention_back(i):
        low, high = head_masks()
        lane = lax.broadcasted_iota(jnp.int32, (1, 128), 1) < 64
        bias = segment_bias(seg, i)
        r = pl.ds(pl.multiple_of(i * 128, 128), 128)
        for p in range(6):
            col = 128 * p
            q = A[r, col : col + 128]
            k2 = stack_heads(A[r, D + col : D + col + 128], low, high)
            v2 = stack_heads(A[r, 2 * D + col : 2 * D + col + 128], low, high)
            dm = A[r, 3 * D + col : 3 * D + col + 128]
            soft = soft_pair(q, k2, bias)
            dp = dot_nt(dm, v2)
            both = dot_tn(soft.astype(BF), dm)
            B[r, 2 * D + col : 2 * D + col + 128] = jnp.where(lane, both[:128], both[128:]).astype(BF)
            halves = []
            for h in (0, 1):
                part = dp[:, 128 * h : 128 * h + 128]
                so = soft[:, 128 * h : 128 * h + 128]
                halves.append(so * (part - jnp.sum(part * so, axis=-1, keepdims=True)))
            ds = jnp.concatenate(halves, axis=1).astype(BF)
            B[r, col : col + 128] = (dot_nn(ds, k2) * SCALE).astype(BF)
            both = dot_tn(ds, q) * SCALE
            B[r, D + col : D + col + 128] = jnp.where(lane, both[:128], both[128:]).astype(BF)

    def t_att(lo, n):
        span(attention_back, 2 * lo, 2 * n)

    def t_qkv(lo, n):
        once(ld_nrm)
        if lo == 0:
            vg[2:3, :] = dot_nn(ones, B[:, 0:D])[0:1, :]
            vg[3:4, :] = dot_nn(ones, B[:, 2 * D : 3 * D])[0:1, :]
        span(lambda u: gradient(E[...], B[:, wide(u)], (u + 1) % RING), lo, n)

    def ig_remote(b):
        return remote(n2.at[tok(b)], ig_land.at[tok(b)], igs.at[b], igr.at[b], partner)

    def ig_local(b):
        return pltpu.make_async_copy(R.at[tok(b)], ig_o.at[tok(b)], igr.at[b])

    ld_land = load(ig_land, cot, 15)
    ld_ig = pltpu.make_async_copy(R, ig_o, lsem.at[16])

    def land(k):
        @pl.when(swapped)
        def _():
            for b in range(4):
                ig_remote(b).wait_recv()
            ld_land.start()
            ld_land.wait()

            def one(b):
                R[tok(b), :] = cot[tok(b), :].astype(F32)

            span(one, 0, 4)
            ld_ig.start()

    def first_norm_back(b):
        dn = dot_nt(B[tok(b), : 3 * D], W[:, : 3 * D])
        d, dgain, dshift = norm_back(dn, cot[tok(b), :].astype(F32), vec[0:1, :])
        R[tok(b), :] = R[tok(b), :] + d
        vg[0:1, :] = vg[0:1, :] + dgain
        vg[1:2, :] = vg[1:2, :] + dshift
        send_ig(b)

    def send_ig(b):
        @pl.when(swapped)
        def _():
            n2[tok(b), :] = R[tok(b), :].astype(BF)
            ig_remote(b).start()

        pl.when(kept)(lambda: ig_local(b).start())

    def cp_slice(j):
        return remote(vsl.at[j], vrc.at[2 * z + c], vss.at[j], vsr.at[2 * z + c], (2 * x + y, j))

    def each_slice(fn):
        def step(j, carry):
            pl.when(jnp.logical_or(swapped, j != f))(lambda: fn(j))
            return carry

        lax.fori_loop(0, 8, step, 0)

    def send_slices(k):
        for j in range(8):
            vsl[j, :, 0:SHARD] = vg[:, SHARD * j : SHARD * j + SHARD]

        @pl.when(kept)
        def _():
            vrc[pl.ds(2 * z + c, 1)] = vsl[pl.ds(f, 1)]

        each_slice(lambda j: cp_slice(j).start())

    def cp_change(k):
        return remote(vdl.at[g], vdl.at[g], vds.at[k], vdr.at[g], members[k])

    def t_vec_adam(k):
        def step(s, carry):
            pl.when(jnp.logical_or(swapped, s != 2 * z + c))(
                lambda: remote(vrc.at[s], vrc.at[s], vss.at[0], vsr.at[s], partner).wait_recv()
            )
            return carry

        lax.fori_loop(0, 8, step, 0)
        grad = jnp.sum(vrc[...], axis=0)[0:12, 0:SHARD]
        first = jnp.concatenate([v1[r] for r in range(12)], axis=0)
        second = jnp.concatenate([v2[r] for r in range(12)], axis=0)
        mom, sq, delta = adam_parts(first, second, vw[...], grad, RATE_VECTOR, 0.0)
        vm_o[...] = mom
        vs_o[...] = sq
        vdl[g, 0:12, 0:SHARD] = delta
        for k in range(3):
            cp_change(k).start()

    def t_vec_outer(k):
        for k in range(3):
            remote(vdl.at[froms[k]], vdl.at[froms[k]], vds.at[k], vdr.at[froms[k]], members[k]).wait_recv()
        mean = jnp.sum(vdl[...], axis=0)[0:12, 0:SHARD] * 0.25
        mom = OUTER_MOMENTUM * vo[...] + mean
        vp_o[...] = mom
        vq_o[...] = vw[...] - OUTER_RATE * (mean + OUTER_MOMENTUM * mom)

    members = [dev(x, 1 - c, z, y), dev(1 - x, c, z, y), dev(1 - x, 1 - c, z, y)]
    froms = [2 * x + 1 - c, 2 * (1 - x) + c, 2 * (1 - x) + 1 - c]

    def cp_core(p):
        return remote(G.at[p % RING, 1 - c], S.at[p], d2s.at[p], d2r.at[p], dev(x, 1 - c, z, y))

    def hop_up(p, t, k):
        return remote(S.at[p, t], ZI.at[p, t - z - 1], zs.at[p, k], zr.at[p, t - z - 1], dev(x, c, z + 1, y))

    def hop_down(p, t, k):
        return remote(S.at[p, t], ZI.at[p, 5 - z + t], zs.at[p, k], zr.at[p, 5 - z + t], dev(x, c, z - 1, y))

    def got(p, k):
        remote(ZI.at[p, k], ZI.at[p, k], zs.at[p, 0], zr.at[p, k], partner).wait_recv()

    def add_in(p, t, k):
        got(p, k)
        S[p, t] = (S[p, t].astype(F32) + ZI[p, k].astype(F32)).astype(BF)

    def s0(p):
        cp_core(p).start()

    def s1(p):
        cp_core(p).wait_recv()

        def one(t):
            S[p, t] = (S[p, t].astype(F32) + G[p % RING, c, t].astype(F32)).astype(BF)

        span(one, 0, 4)

        @pl.when(z == 0)
        def _():
            for k, t in enumerate((3, 2, 1)):
                hop_up(p, t, k).start()

        @pl.when(z == 3)
        def _():
            for k, t in enumerate((0, 1, 2)):
                hop_down(p, t, k).start()

        cp_core(p).wait_send()

    def s2(p):
        @pl.when(z == 1)
        def _():
            for k, t in enumerate((3, 2)):
                add_in(p, t, t - 1)
                hop_up(p, t, k).start()

        @pl.when(z == 2)
        def _():
            for k, t in enumerate((0, 1)):
                add_in(p, t, 2 + t)
                hop_down(p, t, k).start()

    def s3(p):
        @pl.when(z == 2)
        def _():
            add_in(p, 3, 1)
            hop_up(p, 3, 2).start()

        @pl.when(z == 1)
        def _():
            add_in(p, 0, 3)
            hop_down(p, 0, 2).start()

    def cp_final(p):
        return remote(S.at[p, z], FIN.at[p], fs.at[p], fr.at[p], partner)

    def col(p):
        return pl.ds(768 * (p % 4 if p < 8 else (p + 3) % 4), 768)

    def state_loads(p, fn):
        q = p % 2
        m = 1 - p // 4
        for k, src in enumerate((m1, m2, mw, mo) if p < 8 else (a1, a2, aw, ao)):
            src = src.at[m, :, col(p)] if p < 8 else src.at[:, col(p)]
            fn(pltpu.make_async_copy(src, IN.at[q, k], isem.at[q, k]))

    def state_stores(p, ks, fn):
        q = p % 2
        m = 1 - p // 4
        for k in ks:
            dst = ((mm_o, ms_o, mp_o, mq_o) if p < 8 else (am_o, as_o, ap_o, aq_o))[k]
            dst = dst.at[m, :, col(p)] if p < 8 else dst.at[:, col(p)]
            fn(pltpu.make_async_copy(OUT.at[q, k], dst, osem.at[q, k]))

    def start(cp):
        cp.start()

    def wait(cp):
        cp.wait()

    def s4(p):
        pl.when(z > 0)(lambda: add_in(p, z, 0))
        pl.when(z < 3)(lambda: add_in(p, z, 4))

        @pl.when(swapped)
        def _():
            cp_final(p).start()

        @pl.when(kept)
        def _():
            FIN[p] = S[p, z]

    def cp_delta(p, k):
        i = (g, g, froms[1])[k]
        return remote(DL.at[p, i], DL.at[p, i], ls.at[p, k], lr.at[p, i], members[1 if k == 1 else 0])

    def got_delta(p, k):
        i = froms[k]
        remote(DL.at[p, i], DL.at[p, i], ls.at[p, 0], lr.at[p, i], members[k]).wait_recv()

    def s5(p):
        pl.when(swapped)(lambda: cp_final(p).wait_recv())
        state_loads(p, wait)
        if p >= 2:
            state_stores(p - 2, (0, 1), wait)
        q = p % 2

        def rows(i, carry):
            r = pl.ds(pl.multiple_of(i * 32, 32), 32)
            mom, sq, delta = adam_parts(
                IN[q, 0, r, :], IN[q, 1, r, :], IN[q, 2, r, :], FIN[p, r, :].astype(F32), RATE_MATRIX, WEIGHT_DECAY
            )
            OUT[q, 0, r, :] = mom
            OUT[q, 1, r, :] = sq
            DL[p, g, r, :] = delta.astype(BF)
            return carry

        lax.fori_loop(0, 3, rows, 0)
        for k in (1, 0):
            cp_delta(p, k).start()
        state_stores(p, (0, 1), start)

    def s6(p):
        got_delta(p, 1)
        cp_delta(p, 2).start()

    def s7(p):
        got_delta(p, 0)
        got_delta(p, 2)
        if p >= 2:
            state_stores(p - 2, (2, 3), wait)
        q = p % 2

        def rows(i, carry):
            r = pl.ds(pl.multiple_of(i * 32, 32), 32)
            total = DL[p, 0, r, :].astype(F32)
            for k in (1, 2, 3):
                total = total + DL[p, k, r, :].astype(F32)
            mean = total * 0.25
            mom = OUTER_MOMENTUM * IN[q, 3, r, :] + mean
            OUT[q, 2, r, :] = mom
            OUT[q, 3, r, :] = IN[q, 2, r, :] - OUTER_RATE * (mean + OUTER_MOMENTUM * mom)
            return carry

        lax.fori_loop(0, 3, rows, 0)
        state_stores(p, (2, 3), start)

    sums = (s0, s1, s2, s3, s4, s5, s6, s7)
    does = {
        "g": lambda p, s: stages[s](p), "r": lambda p, k: sums[k](p), "il": lambda p: state_loads(p, start),
        "st": lambda k: None, "gd": t_down, "dh": lambda h, lo, n: spanned(functools.partial(hidden_back, h), ld_wd, ld_gp)(lo, n), "bo": spanned(block_output, ld_res),
        "ld": loads, "gu": t_up, "n2": spanned(second_norm, ld_wu), "go": t_out, "dm": spanned(mixed_back, ld_wa),
        "ab": t_att, "gq": t_qkv, "n1": spanned(first_norm_back, ld_xv), "ic": land,
        "vs": send_slices, "va": t_vec_adam, "vo": t_vec_outer,
    }
    for name, *at in ORDER_BACKWARD:
        does[name](*at)

    for p in range(RS):
        for k in range(3):
            remote(S.at[p, k], ZI.at[p, k], zs.at[p, k], zr.at[p, k], partner).wait_send()
        pl.when(swapped)(lambda: cp_final(p).wait_send())
        for k in range(3):
            cp_delta(p, k).wait_send()
    for p in (RS - 2, RS - 1):
        state_stores(p, (0, 1, 2, 3), wait)
    each_slice(lambda j: cp_slice(j).wait_send())
    for k in range(3):
        cp_change(k).wait_send()
    for b in range(4):

        @pl.when(swapped)
        def _():
            out_remote(b).wait_recv()
            ig_remote(b).wait_send()

        @pl.when(kept)
        def _():
            ig_local(b).wait()

    pl.when(swapped)(lambda: ld_ig.wait())


def backward(cot, fwd, states):
    any_ = pl.BlockSpec(memory_space=pl.ANY)
    vm = pl.BlockSpec(memory_space=pltpu.VMEM)
    dma = pltpu.SemaphoreType.DMA
    attn = jax.ShapeDtypeStruct((SHARD, FF), F32)
    mlp = jax.ShapeDtypeStruct((2, SHARD, FF), F32)
    vect = jax.ShapeDtypeStruct((12, SHARD), F32)
    return pl.pallas_call(
        backward_kernel,
        out_shape=(
            jax.ShapeDtypeStruct((T, D), BF), jax.ShapeDtypeStruct((T, D), F32),
            attn, attn, attn, attn, mlp, mlp, mlp, mlp, vect, vect, vect, vect,
            jax.ShapeDtypeStruct((T, D), BF),
        ),
        in_specs=[any_] * 11 + [vm, vm] + [any_] * 8 + [vm] * 4,
        out_specs=(any_,) * 10 + (vm,) * 4 + (any_,),
        scratch_shapes=[
            pltpu.VMEM((T, FF), BF), pltpu.VMEM((T, FF), BF), pltpu.VMEM((D, FF), BF),
            pltpu.VMEM((T, D), BF), pltpu.VMEM((T, D), BF), pltpu.VMEM((T, D), BF), pltpu.VMEM((T, D), F32),
            pltpu.VMEM((RING, 2, 4, SHARD, 768), BF), pltpu.VMEM((RS, 4, SHARD, 768), BF),
            pltpu.VMEM((RS, 5, SHARD, 768), BF), pltpu.VMEM((RS, SHARD, 768), BF),
            pltpu.VMEM((RS, 4, SHARD, 768), BF),
            pltpu.VMEM((2, 4, SHARD, 768), F32), pltpu.VMEM((2, 4, SHARD, 768), F32),
            pltpu.VMEM((16, D), F32), pltpu.VMEM((8, D), F32),
            pltpu.VMEM((8, 16, 128), F32), pltpu.VMEM((8, 16, 128), F32), pltpu.VMEM((4, 16, 128), F32),
            dma((17,)), dma((RS,)), dma((RS,)), dma((RS, 3)), dma((RS, 5)), dma((RS,)), dma((RS,)),
            dma((RS, 3)), dma((RS, 4)), dma((2, 4)), dma((2, 4)), dma((4,)), dma((4,)), dma((4,)), dma((4,)),
            dma((8,)), dma((8,)), dma((3,)), dma((4,)),
            *GATHER_SEMS(1),
        ],
        compiler_params=pltpu.CompilerParams(collective_id=2, has_side_effects=True, vmem_limit_bytes=63 * 2**20),
        name="backward",
    )(cot, *fwd, *states)


def fast(
    inputs, segments, cotangent,
    attn_weight, attn_first, attn_second, attn_outer,
    mlp_weight, mlp_first, mlp_second, mlp_outer,
    vector_weight, vector_first, vector_second, vector_outer,
):
    fwd = forward(inputs[0], cotangent[0], segments[0], attn_weight, mlp_weight, vector_weight)
    out = backward(
        cotangent[0],
        fwd,
        (
            attn_weight, attn_first[0], attn_second[0], attn_outer,
            mlp_weight, mlp_first[0], mlp_second[0], mlp_outer,
            vector_weight, jnp.transpose(vector_first, (1, 0, 2)), jnp.transpose(vector_second, (1, 0, 2)), vector_outer,
        ),
    )
    lead = (1, 1, 1, 1, 0, 0, 1, 1, 0, 0, 0, 0, 0, 0)
    return tuple(v[None] if k else v for v, k in zip(finish(out[:14]), lead))


def norm_apply(values, gain, shift):
    centre = values - jnp.mean(values, axis=-1, keepdims=True)
    spread = jnp.mean(centre * centre, axis=-1, keepdims=True)
    return centre * lax.rsqrt(spread + EPS_NORM) * gain + shift


def gelu_tanh(values):
    return jax.nn.gelu(values, approximate=True)


def adam_step(weight, first, second, gradient, step_rate, weight_decay):
    first_new = BETA_ONE * first + (1.0 - BETA_ONE) * gradient
    second_new = BETA_TWO * second + (1.0 - BETA_TWO) * gradient * gradient
    first_hat = first_new / (1.0 - BETA_ONE**STEP)
    second_hat = second_new / (1.0 - BETA_TWO**STEP)
    local_weight = weight - step_rate * (
        first_hat / (jnp.sqrt(second_hat) + ADAM_EPS) + weight_decay * weight
    )
    return (first_new, second_new, weight - local_weight)


def local(
    inputs,
    segments,
    cotangent,
    attn_weight,
    attn_first,
    attn_second,
    attn_outer,
    mlp_weight,
    mlp_first,
    mlp_second,
    mlp_outer,
    vector_weight,
    vector_first,
    vector_second,
    vector_outer,
):
    bf16 = jnp.bfloat16
    f32 = jnp.float32
    attn_cast = attn_weight.astype(bf16)
    mlp_cast = mlp_weight.astype(bf16)
    attn_low, mlp_low, vector_low = (
        lax.all_gather(attn_cast, "fsdp", axis=0, tiled=True),
        lax.all_gather(mlp_cast, "fsdp", axis=1, tiled=True),
        lax.all_gather(vector_weight.astype(bf16), "fsdp", axis=1, tiled=True),
    )
    vectors = vector_low.astype(f32)
    tokens_f = inputs[0].astype(f32)
    seg_ids = segments[0]
    back_f = cotangent[0].astype(f32)
    model_width = attn_low.shape[0]
    head_dim = model_width // HEADS
    score_scale = head_dim ** (-0.5)
    tok_count = tokens_f.shape[0]
    row_count = tok_count // SEQ
    shape_four = (row_count, SEQ, HEADS, head_dim)
    normed_f, norm_pull = jax.vjp(norm_apply, tokens_f, vectors[0], vectors[1])
    normed = normed_f.astype(bf16)
    project = jnp.dot(normed, attn_low[:, : 3 * model_width], preferred_element_type=f32)
    queries = (project[:, :model_width] + vectors[2]).astype(bf16).reshape(shape_four)
    keys_all = project[:, model_width : 2 * model_width].astype(bf16).reshape(shape_four)
    values_all = (
        (project[:, 2 * model_width : 3 * model_width] + vectors[3])
        .astype(bf16)
        .reshape(shape_four)
    )
    scores = (
        jnp.einsum("rqhd,rkhd->rhqk", queries, keys_all, preferred_element_type=f32) * score_scale
    )
    same_seg = (seg_ids[:, :, None] == seg_ids[:, None, :])[:, None]
    masked = jnp.where(same_seg, scores, NEG_LARGE)
    exponent = jnp.exp(masked - jnp.max(masked, axis=-1, keepdims=True))
    soft = exponent / jnp.sum(exponent, axis=-1, keepdims=True)
    probs = soft.astype(bf16)
    mixed = (
        jnp.einsum("rhqk,rkhd->rqhd", probs, values_all, preferred_element_type=f32)
        .reshape(tok_count, model_width)
        .astype(bf16)
    )
    attended = (
        jnp.dot(mixed, attn_low[:, 3 * model_width :], preferred_element_type=f32) + vectors[4]
    )
    residual = tokens_f + attended
    normed_two_f, norm_two_pull = jax.vjp(norm_apply, residual, vectors[5], vectors[6])
    normed_two = normed_two_f.astype(bf16)
    up_pre = jnp.dot(normed_two, mlp_low[0], preferred_element_type=f32) + vectors[8:12].reshape(-1)
    hidden_f, gelu_pull = jax.vjp(gelu_tanh, up_pre)
    hidden = hidden_f.astype(bf16)
    branch = jnp.einsum("nf,df->nd", hidden, mlp_low[1], preferred_element_type=f32) + vectors[7]
    block_out = (residual + branch).astype(bf16)
    d_branch = cotangent[0]
    d_down_bias = jnp.sum(back_f, axis=0)
    grad_down = jnp.einsum("nd,nf->df", d_branch, hidden, preferred_element_type=f32)
    d_hidden = jnp.einsum("nd,df->nf", d_branch, mlp_low[1], preferred_element_type=f32)
    (d_up_f,) = gelu_pull(d_hidden)
    d_up = d_up_f.astype(bf16)
    d_up_bias = jnp.sum(d_up.astype(f32), axis=0)
    grad_up = jnp.einsum("nd,nf->df", normed_two, d_up, preferred_element_type=f32)
    mlp_grad = jnp.stack([grad_up, grad_down])
    d_normed_two = jnp.einsum("nf,df->nd", d_up, mlp_low[0], preferred_element_type=f32)
    d_res_norm, d_gain_two, d_shift_two = norm_two_pull(d_normed_two)
    d_res = back_f + d_res_norm
    d_att = d_res.astype(bf16)
    d_out_bias = jnp.sum(d_att.astype(f32), axis=0)
    grad_out = jnp.einsum("nc,nd->cd", mixed, d_att, preferred_element_type=f32)
    d_mixed = (
        jnp.einsum("nd,cd->nc", d_att, attn_low[:, 3 * model_width :], preferred_element_type=f32)
        .astype(bf16)
        .reshape(shape_four)
    )
    d_values = (
        jnp.einsum("rhqk,rqhd->rkhd", probs, d_mixed, preferred_element_type=f32)
        .reshape(tok_count, model_width)
        .astype(bf16)
    )
    d_probs = jnp.einsum("rqhd,rkhd->rhqk", d_mixed, values_all, preferred_element_type=f32)
    d_scores = (soft * (d_probs - jnp.sum(d_probs * soft, axis=-1, keepdims=True))).astype(bf16)
    d_queries = (
        (
            jnp.einsum("rhqk,rkhd->rqhd", d_scores, keys_all, preferred_element_type=f32)
            * score_scale
        )
        .reshape(tok_count, model_width)
        .astype(bf16)
    )
    d_keys = (
        (jnp.einsum("rhqk,rqhd->rkhd", d_scores, queries, preferred_element_type=f32) * score_scale)
        .reshape(tok_count, model_width)
        .astype(bf16)
    )
    d_query_bias = jnp.sum(d_queries.astype(f32), axis=0)
    d_value_bias = jnp.sum(d_values.astype(f32), axis=0)
    d_project = jnp.concatenate([d_queries, d_keys, d_values], axis=1)
    grad_qkv = jnp.einsum("nc,nd->cd", normed, d_project, preferred_element_type=f32)
    d_normed = jnp.einsum(
        "nd,cd->nc", d_project, attn_low[:, : 3 * model_width], preferred_element_type=f32
    )
    d_tok_norm, d_gain_one, d_shift_one = norm_pull(d_normed)
    input_grad = d_res + d_tok_norm
    attn_grad = jnp.concatenate([grad_qkv, grad_out], axis=1)
    vector_grad = jnp.concatenate(
        [
            jnp.stack(
                [
                    d_gain_one,
                    d_shift_one,
                    d_query_bias,
                    d_value_bias,
                    d_out_bias,
                    d_gain_two,
                    d_shift_two,
                    d_down_bias,
                ]
            ),
            d_up_bias.reshape(4, model_width),
        ],
        axis=0,
    )
    attn_sum, mlp_sum, vector_sum = (
        lax.psum_scatter(attn_grad.astype(bf16), "fsdp", scatter_dimension=0, tiled=True).astype(f32),
        lax.psum_scatter(mlp_grad.astype(bf16), "fsdp", scatter_dimension=1, tiled=True).astype(f32),
        lax.psum_scatter(vector_grad, "fsdp", scatter_dimension=1, tiled=True),
    )
    attn_moment, attn_square, attn_delta = adam_step(
        attn_weight, attn_first[0], attn_second[0], attn_sum, RATE_MATRIX, WEIGHT_DECAY
    )
    mlp_moment, mlp_square, mlp_delta = adam_step(
        mlp_weight, mlp_first[0], mlp_second[0], mlp_sum, RATE_MATRIX, WEIGHT_DECAY
    )
    vector_moment, vector_square, vector_delta = adam_step(
        vector_weight, vector_first[0], vector_second[0], vector_sum, RATE_VECTOR, 0.0
    )
    group_count = lax.axis_size("group")
    attn_total, mlp_total, vector_total = (
        lax.psum(attn_delta.astype(jnp.bfloat16), "group").astype(jnp.float32),
        lax.psum(mlp_delta.astype(jnp.bfloat16), "group").astype(jnp.float32),
        lax.psum(vector_delta.astype(jnp.bfloat16), "group").astype(jnp.float32),
    )
    attn_mean = attn_total / group_count
    mlp_mean = mlp_total / group_count
    vector_mean = vector_total / group_count
    attn_momentum = OUTER_MOMENTUM * attn_outer + attn_mean
    mlp_momentum = OUTER_MOMENTUM * mlp_outer + mlp_mean
    vector_momentum = OUTER_MOMENTUM * vector_outer + vector_mean
    attn_master = attn_weight - OUTER_RATE * (attn_mean + OUTER_MOMENTUM * attn_momentum)
    mlp_master = mlp_weight - OUTER_RATE * (mlp_mean + OUTER_MOMENTUM * mlp_momentum)
    vector_master = vector_weight - OUTER_RATE * (vector_mean + OUTER_MOMENTUM * vector_momentum)
    return (
        block_out[None],
        input_grad[None],
        attn_moment[None],
        attn_square[None],
        attn_momentum,
        attn_master,
        mlp_moment[None],
        mlp_square[None],
        mlp_momentum,
        mlp_master,
        vector_moment[None],
        vector_square[None],
        vector_momentum,
        vector_master,
    )


def solution(mesh):
    in_specs = (
        P("group", "fsdp", None),
        P("group", "fsdp", None),
        P("group", "fsdp", None),
        P("fsdp", None),
        P("group", "fsdp", None),
        P("group", "fsdp", None),
        P("fsdp", None),
        P(None, "fsdp", None),
        P("group", None, "fsdp", None),
        P("group", None, "fsdp", None),
        P(None, "fsdp", None),
        P(None, "fsdp"),
        P("group", None, "fsdp"),
        P("group", None, "fsdp"),
        P(None, "fsdp"),
    )
    out_specs = (
        P("group", "fsdp", None),
        P("group", "fsdp", None),
        P("group", "fsdp", None),
        P("group", "fsdp", None),
        P("fsdp", None),
        P("fsdp", None),
        P("group", None, "fsdp", None),
        P("group", None, "fsdp", None),
        P(None, "fsdp", None),
        P(None, "fsdp", None),
        P("group", None, "fsdp"),
        P("group", None, "fsdp"),
        P(None, "fsdp"),
        P(None, "fsdp"),
    )
    fits = mesh.shape["group"] == 4 and mesh.shape["fsdp"] == 8
    return jax.shard_map(fast if fits else local, mesh=mesh, in_specs=in_specs, out_specs=out_specs, check_vma=False)
```

```python
import functools

import jax
import jax.numpy as jnp
from jax import lax
from jax.experimental import pallas as pl
from jax.experimental.pallas import tpu as pltpu
from jax.sharding import PartitionSpec as P

EPS_NORM = 1e-05
NEG_LARGE = -1e30
HEADS = 12
SEQ = 64
STEP = 10
BETA_ONE = 0.9
BETA_TWO = 0.999
ADAM_EPS = 1e-08
RATE_MATRIX = 0.05
RATE_VECTOR = 0.5
WEIGHT_DECAY = 0.1
OUTER_RATE = 0.7
OUTER_MOMENTUM = 0.9


ORDER_FORWARD = (
    ("cast", 0), ("g", 0, 0), ("g", 1, 0), ("xs", 0), ("cast", 1), ("cast", 2), ("g", 2, 0), ("g", 3, 0),
    ("xs", 3), ("xs", 1), ("xs", 2), ("g", 0, 1), ("g", 4, 0), ("g", 1, 1), ("g", 0, 2), ("vec", 0), ("g", 1, 2),
    ("cs", 0), ("g", 0, 3), ("g", 1, 3), ("g", 2, 1), ("g", 0, 4), ("g", 1, 4), ("g", 2, 2), ("g", 3, 1),
    ("g", 0, 5), ("g", 1, 5), ("g", 2, 3), ("ln", 0, 4), ("g", 3, 2), ("g", 1, 6), ("g", 0, 6), ("v", 0, 4),
    ("qk", 0, 4), ("g", 3, 3), ("g", 2, 4), ("g", 4, 1), ("at", 0, 2), ("g", 3, 4), ("at", 2, 2), ("g", 2, 5),
    ("g", 4, 2), ("on", 0, 4), ("g", 4, 3), ("g", 2, 6), ("u", 0, 0, 2), ("g", 3, 5), ("u", 0, 2, 2), ("g", 4, 4),
    ("g", 3, 6), ("u", 1, 2, 2), ("u", 1, 0, 2), ("g", 4, 5), ("g", 4, 6), ("end", 0),
)

ORDER_BACKWARD = (
    ("st", 0), ("g", 0, 0), ("gd", 0, 2), ("r", 0, 0), ("r", 1, 0), ("g", 0, 1), ("il", 1), ("r", 0, 1),
    ("r", 1, 1), ("g", 0, 2), ("gd", 2, 2), ("r", 3, 0), ("r", 2, 0), ("il", 0), ("g", 0, 3), ("dh", 0, 0, 4),
    ("g", 0, 4), ("r", 2, 1), ("r", 0, 2), ("r", 3, 1), ("g", 0, 5), ("gu", 0, 2), ("r", 1, 2), ("r", 0, 3),
    ("r", 5, 0), ("r", 4, 0), ("g", 0, 6), ("dh", 1, 0, 4), ("r", 0, 4), ("r", 1, 3), ("r", 5, 1), ("bo", 0, 4),
    ("r", 2, 2), ("ld", 0), ("r", 0, 5), ("r", 4, 1), ("gu", 2, 2), ("r", 7, 0), ("r", 6, 0), ("r", 2, 3),
    ("n2", 2, 2), ("r", 7, 1), ("r", 5, 2), ("r", 0, 6), ("n2", 0, 2), ("ld", 1), ("r", 6, 1), ("r", 2, 4),
    ("r", 1, 4), ("r", 3, 2), ("go", 0), ("dm", 0, 4), ("r", 5, 3), ("r", 0, 7), ("r", 4, 2), ("r", 3, 3),
    ("r", 1, 5), ("il", 2), ("ab", 2, 2), ("r", 8, 0), ("r", 5, 4), ("r", 1, 6), ("r", 2, 5), ("r", 4, 3),
    ("ab", 0, 2), ("r", 6, 2), ("r", 7, 2), ("r", 2, 6), ("r", 8, 1), ("gq", 0, 2), ("r", 9, 0), ("r", 1, 7),
    ("r", 3, 4), ("r", 6, 3), ("r", 4, 4), ("n1", 0, 2), ("r", 8, 2), ("r", 2, 7), ("il", 4), ("il", 3),
    ("r", 9, 1), ("r", 10, 0), ("r", 3, 5), ("r", 7, 3), ("r", 4, 5), ("r", 9, 2), ("r", 6, 4), ("n1", 2, 2),
    ("r", 3, 6), ("r", 8, 3), ("r", 10, 1), ("r", 3, 7), ("il", 5), ("r", 9, 3), ("r", 5, 5), ("r", 4, 6),
    ("r", 10, 2), ("gq", 2, 1), ("r", 11, 0), ("r", 4, 7), ("il", 6), ("r", 6, 5), ("r", 7, 4), ("r", 10, 3),
    ("r", 11, 1), ("r", 5, 6), ("r", 5, 7), ("il", 7), ("r", 8, 4), ("r", 6, 6), ("r", 7, 5), ("r", 11, 2),
    ("r", 6, 7), ("il", 8), ("r", 9, 4), ("r", 8, 5), ("r", 10, 4), ("vs", 0), ("r", 7, 6), ("r", 11, 3),
    ("r", 7, 7), ("il", 9), ("r", 9, 5), ("r", 8, 6), ("r", 8, 7), ("il", 10), ("r", 11, 4), ("r", 10, 5),
    ("r", 9, 6), ("va", 0), ("r", 9, 7), ("il", 11), ("r", 11, 5), ("ic", 0), ("r", 10, 6), ("r", 10, 7),
    ("r", 11, 6), ("vo", 0), ("r", 11, 7),
)


MESH = pl.DeviceIdType.MESH
BF = jnp.bfloat16
F32 = jnp.float32
D = 768
FF = 3072
T = 1024
TB = 256
SHARD = 96
GELU_C = 0.7978845608028654
GELU_A = 0.044715
SCALE = 0.125


def dot_nn(a, b):
    return jnp.dot(a, b, preferred_element_type=F32)


def dot_nt(a, b):
    return lax.dot_general(a, b, (((1,), (1,)), ((), ())), preferred_element_type=F32)


def dot_tn(a, b):
    return lax.dot_general(a, b, (((0,), (0,)), ((), ())), preferred_element_type=F32)


def coords():
    g = lax.axis_index("group")
    f = lax.axis_index("fsdp")
    return g // 2, g % 2, f // 2, f % 2


def dev(x, c, z, y):
    return (2 * x + c, 2 * z + y)


def remote(src, dst, ssem, rsem, to):
    return pltpu.make_async_remote_copy(
        src_ref=src, dst_ref=dst, send_sem=ssem, recv_sem=rsem, device_id=to, device_id_type=MESH
    )


def norm_parts(v):
    centre = v - jnp.mean(v, axis=-1, keepdims=True)
    spread = jnp.mean(centre * centre, axis=-1, keepdims=True)
    scale = lax.rsqrt(spread + EPS_NORM)
    return centre * scale, scale


def head_masks():
    lane = lax.broadcasted_iota(jnp.int32, (1, 128), 1)
    low = (lane < 64).astype(F32).astype(BF)
    high = (lane >= 64).astype(F32).astype(BF)
    return low, high


def segment_bias(seg_ref, i):
    row = seg_ref[pl.ds(i, 1), :]
    classes = lax.broadcasted_iota(jnp.int32, (16, 128), 0)
    hot = (classes == row).astype(F32).astype(BF)
    same = dot_tn(hot, hot)
    bias = (same - 1.0) * (-NEG_LARGE)
    return jnp.concatenate([bias, bias], axis=1)


def soft_pair(q, k2, bias):
    s = dot_nt(q, k2) * SCALE + bias
    halves = []
    for h in (0, 1):
        part = s[:, 128 * h : 128 * h + 128]
        e = jnp.exp(part - jnp.max(part, axis=-1, keepdims=True))
        halves.append(e * (1.0 / jnp.sum(e, axis=-1, keepdims=True)))
    return jnp.concatenate(halves, axis=1)


def stack_heads(v, low, high):
    return jnp.concatenate([v * low, v * high], axis=0)


def gather_stages(view, sems, where, shift=0):
    x, c, z, y = where
    ys, yr, us, ds, zr, xs, xr, cs, cr = sems
    f = 2 * z + y
    other = 2 * z + 1 - y

    def rows(i):
        return pl.ds(pl.multiple_of(i * SHARD, 32), SHARD)

    def pair(i):
        return pl.ds(pl.multiple_of(i * 2 * SHARD, 64), 2 * SHARD)

    mine = 2 * x + c
    across = 2 * (1 - x) + c
    sib = 2 * x + 1 - c
    sib_across = 2 * (1 - x) + 1 - c

    def at(p, r, q):
        return view(p, r, pl.ds(pl.multiple_of(1536 * ((p + shift) % 2) + 384 * q, 128), 384))

    def cp_y(p, r):
        return remote(at(p, r, mine), at(p, r, mine), ys.at[p], yr.at[p], dev(x, c, z, 1 - y))

    def cp_up(p, i):
        return remote(at(p, pair(i), mine), at(p, pair(i), mine), us.at[p, i], zr.at[p, i], dev(x, c, z + 1, y))

    def cp_down(p, i):
        return remote(at(p, pair(i), mine), at(p, pair(i), mine), ds.at[p, i], zr.at[p, i], dev(x, c, z - 1, y))

    def cp_x(p, r, i, q):
        return remote(at(p, r, q), at(p, r, q), xs.at[p, i], xr.at[p, i], dev(1 - x, c, z, y))

    def cp_c(p, r, i, q, k):
        return remote(at(p, r, q), at(p, r, q), cs.at[p, 4 * k + i], cr.at[p, 4 * k + i], dev(x, 1 - c, z, y))

    def others(fn):
        for k in (1, 2, 3):
            pl.when(z >= k)(functools.partial(fn, z - k))
            pl.when(z + k <= 3)(functools.partial(fn, z + k))

    def sa(p):
        cp_y(p, rows(f)).start()

    def sb(p):
        cp_y(p, rows(other)).wait_recv()
        pl.when(z < 3)(lambda: cp_up(p, z).start())
        pl.when(z > 0)(lambda: cp_down(p, z).start())
        cp_x(p, rows(other), z, mine).start()
        cp_c(p, rows(other), z, mine, 0).start()

    def hop(k, p):
        def from_below():
            i = z - k
            cp_up(p, i).wait_recv()
            pl.when(z < 3)(lambda: cp_up(p, i).start())
            cp_x(p, pair(i), i, mine).start()
            cp_c(p, pair(i), i, mine, 0).start()

        def from_above():
            i = z + k
            cp_down(p, i).wait_recv()
            pl.when(z > 0)(lambda: cp_down(p, i).start())
            cp_x(p, pair(i), i, mine).start()
            cp_c(p, pair(i), i, mine, 0).start()

        pl.when(z >= k)(from_below)
        pl.when(z + k <= 3)(from_above)

    def sf(p):
        cp_x(p, rows(other), z, across).wait_recv()
        cp_c(p, rows(other), z, across, 1).start()

        def fwd(i):
            cp_x(p, pair(i), i, across).wait_recv()
            cp_c(p, pair(i), i, across, 1).start()

        others(fwd)

    def sg(p):
        cp_c(p, rows(other), z, sib, 0).wait_recv()
        cp_c(p, rows(other), z, sib_across, 1).wait_recv()

        def got(i):
            cp_c(p, pair(i), i, sib, 0).wait_recv()
            cp_c(p, pair(i), i, sib_across, 1).wait_recv()

        others(got)

    def drain(p):
        cp_y(p, rows(f)).wait_send()
        pl.when(z < 3)(lambda: cp_up(p, z).wait_send())
        pl.when(z > 0)(lambda: cp_down(p, z).wait_send())
        cp_x(p, rows(other), z, mine).wait_send()
        cp_c(p, rows(other), z, mine, 0).wait_send()
        cp_c(p, rows(other), z, across, 1).wait_send()
        for k in (1, 2, 3):

            @pl.when(z >= k)
            def _():
                pl.when(z < 3)(lambda: cp_up(p, z - k).wait_send())

            @pl.when(z + k <= 3)
            def _():
                pl.when(z > 0)(lambda: cp_down(p, z + k).wait_send())

        def sent(i):
            cp_x(p, pair(i), i, mine).wait_send()
            cp_c(p, pair(i), i, mine, 0).wait_send()
            cp_c(p, pair(i), i, across, 1).wait_send()

        others(sent)

    stages = [sa, sb, functools.partial(hop, 1), functools.partial(hop, 2), functools.partial(hop, 3), sf, sg]
    return stages, drain


GATHER_SEMS = lambda n: [
    pltpu.SemaphoreType.DMA((n,)),
    pltpu.SemaphoreType.DMA((n,)),
    pltpu.SemaphoreType.DMA((n, 4)),
    pltpu.SemaphoreType.DMA((n, 4)),
    pltpu.SemaphoreType.DMA((n, 4)),
    pltpu.SemaphoreType.DMA((n, 4)),
    pltpu.SemaphoreType.DMA((n, 4)),
    pltpu.SemaphoreType.DMA((n, 8)),
    pltpu.SemaphoreType.DMA((n, 8)),
]
PIECES = 5


def forward_kernel(
    x_in, cot_in, seg_raw, aw, mw, vw,
    w_out, qkvm_out, hid_out, gp_out, nrm_out, n2_out, res_out, xv_out, cotv_out, wd_out, vec_out, seg_out,
    w, xv, nrm, qkvm, res, n2, hid, gp, vec, seg, seg_in, tiles, ub,
    xsnd, xrcv, csnd, crcv, gsnd, grcv, vsnd, vrcv, osem,
    *gsems,
):
    where = coords()
    x, c, z, y = where
    f = 2 * z + y
    swapped = c != y
    partner = dev(x, y, z, c)

    barrier = pltpu.get_barrier_semaphore()

    def greet(to):
        pl.semaphore_signal(barrier, inc=1, device_id=to, device_id_type=MESH)

    for k in range(1, 8):
        greet((2 * x + c, (f + k) % 8))
    greet(dev(x, 1 - c, z, y))
    greet(dev(1 - x, c, z, y))
    pl.when(swapped)(lambda: greet(partner))

    for i in range(8):
        seg_in[i : i + 1, :] = jnp.concatenate([seg_raw[2 * i : 2 * i + 1, :], seg_raw[2 * i + 1 : 2 * i + 2, :] + 8], axis=1)
    own = pl.ds(pl.multiple_of(f * SHARD, 32), SHARD)
    tiles[pl.ds(f, 1)] = jnp.zeros((1, 16, 128), F32)
    tiles[f, 0:12, 0:SHARD] = vw[...].astype(BF).astype(F32)

    pl.semaphore_wait(barrier, 9 + swapped.astype(jnp.int32))

    stages, drain = gather_stages(lambda p, r, q: w.at[p // 2, r, q], gsems, where)

    def cp_vec(k, j):
        return remote(tiles.at[j], tiles.at[j], vsnd.at[k - 1], vrcv.at[k - 1], (2 * x + c, (f + k) % 8))

    def tok(b, n=1):
        if isinstance(b, int):
            return pl.ds(b * TB, n * TB)
        return pl.ds(pl.multiple_of(b * TB, TB), n * TB)

    def span(fn, lo, n):
        def step(b, carry):
            fn(b)
            return carry

        lax.fori_loop(lo, lo + n, step, 0)

    def x_remote(b):
        return remote(x_in.at[tok(b)], xv.at[tok(b)], xsnd.at[b], xrcv.at[b], partner)

    def x_local(b):
        return pltpu.make_async_copy(x_in.at[tok(b)], xv.at[tok(b)], xrcv.at[b])

    def cot_remote():
        return remote(cot_in, cotv_out, csnd, crcv, partner)

    def seg_remote():
        return remote(seg_in, seg, gsnd, grcv, partner)

    outs = []

    def write(src, dst):
        cp = pltpu.make_async_copy(src, dst, osem.at[len(outs)])
        cp.start()
        outs.append(cp)

    def cast(m):
        if m == 1:
            w[1, own, :] = mw[0].astype(BF)
            return
        if m == 2:
            w[2, own, 0:1536] = mw[1, :, 0:1536].astype(BF)
            return
        w[0, own, :] = aw[...].astype(BF)
        for k in range(1, 8):
            cp_vec(k, f).start()

        @pl.when(swapped)
        def _():
            seg_remote().start()

        @pl.when(jnp.logical_not(swapped))
        def _():
            seg[...] = seg_in[...]
            for b in range(4):
                x_local(b).start()

    def send_x(b):
        pl.when(swapped)(lambda: x_remote(b).start())

    def send_cot(k):
        pl.when(swapped)(lambda: cot_remote().start())

    def gather(p, s):
        stages[s](p)
        if s == 6:
            half_at = pl.ds(1536 * (p % 2), 1536)
            write(w.at[p // 2, :, half_at], w_out.at[p // 2, :, half_at] if p < 4 else wd_out)

    def vectors():
        for k in range(1, 8):
            cp_vec(k, (f + 8 - k) % 8).wait_recv()
        total = jnp.zeros((16, D), F32)
        r = lax.broadcasted_iota(jnp.int32, (128, D), 0)
        q = lax.broadcasted_iota(jnp.int32, (128, D), 1)
        for j in range(8):
            pick = jnp.logical_and(q == r + SHARD * j, r < SHARD).astype(F32).astype(BF)
            total = total + dot_nn(tiles[j].astype(BF), pick)
        vec[...] = total
        for k in range(4):
            ub[0:1, D * k : D * k + D] = total[8 + k : 9 + k, :]

    def first_norm(b):
        @pl.when(swapped)
        def _():
            x_remote(b).wait_recv()

        @pl.when(jnp.logical_not(swapped))
        def _():
            x_local(b).wait()

        hat, _ = norm_parts(xv[tok(b), :].astype(F32))
        nrm[tok(b), :] = (hat * vec[0:1, :] + vec[1:2, :]).astype(BF)

    def queries_keys(b):
        r = dot_nn(nrm[tok(b), :], w[0, :, 0:1536])
        qkvm[tok(b), 0:D] = (r[:, 0:D] + vec[2:3, :]).astype(BF)
        qkvm[tok(b), D : 2 * D] = r[:, D : 2 * D].astype(BF)

    def values(b):
        r = dot_nn(nrm[tok(b), :], w[0, :, 1536:2304])
        qkvm[tok(b), 2 * D : 3 * D] = (r + vec[3:4, :]).astype(BF)

    def attention(i):
        low, high = head_masks()
        bias = segment_bias(seg, i)
        r = pl.ds(pl.multiple_of(i * 128, 128), 128)
        for p in range(6):
            col = 128 * p
            q = qkvm[r, col : col + 128]
            k2 = stack_heads(qkvm[r, D + col : D + col + 128], low, high)
            v2 = stack_heads(qkvm[r, 2 * D + col : 2 * D + col + 128], low, high)
            probs = soft_pair(q, k2, bias).astype(BF)
            qkvm[r, 3 * D + col : 3 * D + col + 128] = dot_nn(probs, v2).astype(BF)

    greeted = []

    def attend(lo, n):
        if not greeted:
            greeted.append(lo)
            pl.when(swapped)(lambda: seg_remote().wait_recv())
        span(attention, 2 * lo, 2 * n)
        write(qkvm.at[tok(lo, n)], qkvm_out.at[tok(lo, n)])

    def out_norm(b):
        att = dot_nn(qkvm[tok(b), 3 * D :], w[0, :, 2304:3072]) + vec[4:5, :]
        r = xv[tok(b), :].astype(F32) + att
        res[tok(b), :] = r
        hat, _ = norm_parts(r)
        n2[tok(b), :] = (hat * vec[5:6, :] + vec[6:7, :]).astype(BF)

    def up(half, b):
        for k in range(2):
            lo = 1536 * half + 768 * k
            u = dot_nn(n2[tok(b), :], w[1, :, lo : lo + 768]) + ub[0:1, lo : lo + 768]
            u2 = u * u
            t = jnp.tanh(u * (GELU_C + (GELU_C * GELU_A) * u2))
            h = 0.5 + 0.5 * t
            out = u * h
            hid[tok(b), lo : lo + 768] = out.astype(BF)
            slope = h + out * (1.0 - h) * (2.0 * GELU_C + (6.0 * GELU_C * GELU_A) * u2)
            gp[tok(b), lo : lo + 768] = slope.astype(BF)

    def spanned(fn, *pairs):
        def run(lo, n):
            span(fn, lo, n)
            for src, dst in pairs:
                write(src.at[tok(lo, n)], dst.at[tok(lo, n)])

        return run

    def up_half(half, lo, n):
        span(functools.partial(up, half), lo, n)
        half_at = pl.ds(1536 * half, 1536)
        write(hid.at[tok(lo, n), half_at], hid_out.at[tok(lo, n), half_at])
        write(gp.at[tok(lo, n), half_at], gp_out.at[tok(lo, n), half_at])

    does = {
        "g": gather, "cast": cast, "xs": send_x, "cs": send_cot, "vec": lambda k: vectors(),
        "ln": spanned(first_norm, (xv, xv_out), (nrm, nrm_out)), "qk": spanned(queries_keys), "v": spanned(values),
        "at": attend, "on": spanned(out_norm, (res, res_out), (n2, n2_out)), "u": up_half, "end": lambda k: None,
    }
    for name, *at in ORDER_FORWARD:
        does[name](*at)
    vec_out[...] = vec[...]
    seg_out[...] = seg[...]

    for p in range(PIECES):
        drain(p)
    for k in range(1, 8):
        cp_vec(k, f).wait_send()

    @pl.when(swapped)
    def _():
        seg_remote().wait_send()
        for b in range(4):
            x_remote(b).wait_send()
        cot_remote().wait()

    for cp in outs:
        cp.wait()


def forward(x, cot, seg, aw, mw, vw):
    any_ = pl.BlockSpec(memory_space=pl.ANY)
    vm = pl.BlockSpec(memory_space=pltpu.VMEM)
    wide = jax.ShapeDtypeStruct((T, FF), BF)
    slim = jax.ShapeDtypeStruct((T, D), BF)
    dma = pltpu.SemaphoreType.DMA
    return pl.pallas_call(
        forward_kernel,
        out_shape=(
            jax.ShapeDtypeStruct((2, D, FF), BF), wide, wide, wide, slim, slim,
            jax.ShapeDtypeStruct((T, D), F32), slim, slim, jax.ShapeDtypeStruct((D, 1536), BF),
            jax.ShapeDtypeStruct((16, D), F32), jax.ShapeDtypeStruct((8, 128), jnp.int32),
        ),
        in_specs=[any_, any_, vm, vm, vm, vm],
        out_specs=(any_,) * 10 + (vm, vm),
        scratch_shapes=[
            pltpu.VMEM((3, D, FF), BF), pltpu.VMEM((T, D), BF), pltpu.VMEM((T, D), BF), pltpu.VMEM((T, FF), BF),
            pltpu.VMEM((T, D), F32), pltpu.VMEM((T, D), BF), pltpu.VMEM((T, FF), BF), pltpu.VMEM((T, FF), BF),
            pltpu.VMEM((16, D), F32), pltpu.VMEM((8, 128), jnp.int32), pltpu.VMEM((8, 128), jnp.int32),
            pltpu.VMEM((8, 16, 128), F32),
            pltpu.VMEM((1, FF), F32),
            dma((4,)), dma((4,)), dma, dma, dma, dma, dma((7,)), dma((7,)), dma((40,)),
            *GATHER_SEMS(PIECES),
        ],
        compiler_params=pltpu.CompilerParams(collective_id=1, has_side_effects=True, vmem_limit_bytes=60 * 2**20),
        name="forward",
    )(x, cot, seg, aw, mw, vw)


def final_kernel(*refs):
    ins, small, outs, small_outs = refs[:10], refs[10:14], refs[14:24], refs[24:28]
    bufs, rsem, wsem = refs[28:38], refs[38], refs[39]
    reads = [pltpu.make_async_copy(a, b, rsem.at[k]) for k, (a, b) in enumerate(zip(ins, bufs))]
    for cp in reads:
        cp.start()
    for k in range(4):
        if k < 2:
            for r in range(12):
                small_outs[k][r] = small[k][r : r + 1, :]
        else:
            small_outs[k][...] = small[k][...]
    writes = [pltpu.make_async_copy(b, a, wsem.at[k]) for k, (a, b) in enumerate(zip(outs, bufs))]
    for r, w in zip(reads, writes):
        r.wait()
        w.start()
    for w in writes:
        w.wait()


def finish(arrays):
    any_ = pl.BlockSpec(memory_space=pl.ANY)
    vm = pl.BlockSpec(memory_space=pltpu.VMEM)
    big, small = arrays[:10], arrays[10:14]
    shapes = [jax.ShapeDtypeStruct(a.shape, a.dtype) for a in big]
    thin = jax.ShapeDtypeStruct((12, 1, SHARD), F32)
    out = pl.pallas_call(
        final_kernel,
        out_shape=(*shapes, thin, thin, *[jax.ShapeDtypeStruct(a.shape, a.dtype) for a in small[2:]]),
        in_specs=[any_] * 10 + [vm] * 4,
        out_specs=(any_,) * 10 + (vm,) * 4,
        scratch_shapes=[pltpu.VMEM(a.shape, a.dtype) for a in big]
        + [pltpu.SemaphoreType.DMA((10,)), pltpu.SemaphoreType.DMA((10,))],
        compiler_params=pltpu.CompilerParams(vmem_limit_bytes=63 * 2**20),
        name="finish",
    )(*big, *small)
    return (*out[:10], jnp.transpose(out[10], (1, 0, 2)), jnp.transpose(out[11], (1, 0, 2)), out[12], out[13])


RS = 12
RING = 2


def adam_parts(first, second, weight, gradient, rate, decay):
    first_new = BETA_ONE * first + (1.0 - BETA_ONE) * gradient
    second_new = BETA_TWO * second + (1.0 - BETA_TWO) * gradient * gradient
    first_hat = first_new * (1.0 / (1.0 - BETA_ONE**STEP))
    second_hat = second_new * (1.0 / (1.0 - BETA_TWO**STEP))
    delta = rate * (first_hat / (jnp.sqrt(second_hat) + ADAM_EPS) + decay * weight)
    return first_new, second_new, delta


def backward_kernel(
    cot_in, w_in, qkvm_in, hid_in, gp_in, nrm_in, n2_in, res_in, xv_in, cotv_in, wd_in, vec, seg,
    aw, a1, a2, ao, mw, m1, m2, mo, vw, v1, v2, vo,
    out_o, ig_o, am_o, as_o, ap_o, aq_o, mm_o, ms_o, mp_o, mq_o, vm_o, vs_o, vp_o, vq_o, ig_land,
    A, B, W, cot, n2, E, R, G, S, ZI, FIN, DL, IN, OUT, vg, ubs, vsl, vrc, vdl,
    lsem, d2s, d2r, zs, zr, fs, fr, ls, lr, isem, osem, bos, bor, igs, igr, vss, vsr, vds, vdr, *gsems,
):
    x, c, z, y = coords()
    f = 2 * z + y
    g = 2 * x + c
    swapped = c != y
    kept = jnp.logical_not(swapped)
    partner = dev(x, y, z, c)

    barrier = pltpu.get_barrier_semaphore()

    def greet(to):
        pl.semaphore_signal(barrier, inc=1, device_id=to, device_id_type=MESH)

    me16 = c * 8 + f
    for k in range(1, 16):
        other = (me16 + k) % 16
        greet((2 * x + other // 8, other % 8))
    greet(dev(1 - x, c, z, y))
    greet(dev(1 - x, 1 - c, z, y))

    def tok(b, n=1):
        if isinstance(b, int):
            return pl.ds(b * TB, n * TB)
        return pl.ds(pl.multiple_of(b * TB, TB), n * TB)

    def span(fn, lo, n):
        def step(b, carry):
            fn(b)
            return carry

        lax.fori_loop(lo, lo + n, step, 0)

    def spanned(fn, *cps):
        def run(lo, n):
            once(*cps)
            span(fn, lo, n)

        return run

    own = pl.ds(pl.multiple_of(f * SHARD, 32), SHARD)
    stages, gather_drain = gather_stages(lambda p, r, q: W.at[r, q], gsems, (x, c, z, y), 1)

    def load(src, dst, k):
        return pltpu.make_async_copy(src, dst, lsem.at[k])

    ld_cot = load(cotv_in, cot, 0)
    ld_own = load(cot_in, cot, 0)
    ld_hid = [load(hid_in.at[:, 768 * i : 768 * i + 768], A.at[:, 768 * i : 768 * i + 768], 17 + i) for i in range(4)]
    ld_own_w = [load(mw.at[1, :, pl.ds(768 * k, 768)], IN.at[0, k], 11 + k) for k in (2, 3)]
    ld_wd = load(wd_in, W.at[:, 0:1536], 2)
    ld_gp = load(gp_in, B, 3)
    ld_res = load(res_in, R, 4)
    ld_n2 = load(n2_in, n2, 5)
    ld_wu = load(w_in.at[1], W, 6)
    ld_wa = load(w_in.at[0], W, 7)
    ld_qkvm = load(qkvm_in, A, 8)
    ld_nrm = load(nrm_in, E, 9)
    ld_xv = load(xv_in, cot, 10)
    for cp in ld_own_w:
        cp.start()
    pl.when(swapped)(lambda: ld_cot.start())
    pl.when(kept)(lambda: ld_own.start())
    for cp in (*ld_hid, ld_wd, ld_gp, ld_res, ld_n2):
        cp.start()
    vg[...] = jnp.zeros((16, D), F32)
    vsl[...] = jnp.zeros((8, 16, 128), F32)
    vdl[...] = jnp.zeros((4, 16, 128), F32)
    for k, cp in zip((2, 3), ld_own_w):
        cp.wait()
        W[own, 768 * k : 768 * k + 768] = IN[0, k].astype(BF)
    pl.semaphore_wait(barrier, 17)

    def wide(i, n=768):
        return pl.ds(i * n if isinstance(i, int) else pl.multiple_of(i * n, n), n)

    ones = jnp.ones((16, T), BF)

    def gradient(lhs, rhs, slot):
        out = dot_tn(lhs, rhs)
        for j in range(8):
            G[slot, j % 2, j // 2] = out[SHARD * j : SHARD * j + SHARD].astype(BF)

    def t_down(lo, n):
        if lo == 0:
            ld_cot.wait()
            vg[7:8, :] = dot_nn(ones, cot[...])[0:1, :]
        for i in range(lo, lo + n):
            ld_hid[i].wait()
        span(lambda v: gradient(cot[...], A[:, wide(v)], v % RING), lo, n)

    def out_remote(b):
        return remote(E.at[tok(b)], out_o.at[tok(b)], bos.at[b], bor.at[b], partner)

    def out_local(b):
        return pltpu.make_async_copy(E.at[tok(b)], out_o.at[tok(b)], bor.at[b])

    waited = set()

    def once(*cps):
        for cp in cps:
            if id(cp) not in waited:
                waited.add(id(cp))
                cp.wait()

    def hidden_back(half, b):
        for k in (2 * half, 2 * half + 1):
            lo = 768 * k
            dh = dot_nn(cot[tok(b), :], W[:, lo : lo + 768])
            B[tok(b), lo : lo + 768] = (dh * B[tok(b), lo : lo + 768].astype(F32)).astype(BF)

    def block_output(b):
        branch = dot_nt(A[tok(b), :], W[...])
        E[tok(b), :] = (R[tok(b), :] + branch + vec[7:8, :]).astype(BF)
        send_out(b)

    def send_out(b):
        pl.when(swapped)(lambda: out_remote(b).start())
        pl.when(kept)(lambda: out_local(b).start())

    def loads(k):
        if k == 0:
            gather_drain(0)
            ld_wu.start()
            ld_qkvm.start()
            return
        ld_wa.start()
        ld_xv.start()
        for b in range(4):
            pl.when(swapped)(lambda: out_remote(b).wait_send())
            pl.when(kept)(lambda: out_local(b).wait())
        ld_nrm.start()

    def t_up(lo, n):
        once(ld_n2)

        def one(u):
            ubs[pl.ds(u, 1), :] = dot_nn(ones, B[:, wide(u)])[0:1, :]
            gradient(n2[...], B[:, wide(u)], u % RING)

        span(one, lo, n)
        if lo + n == 4:
            vg[8:12, :] = ubs[0:4, :]

    def norm_back(dn, v, gain):
        hat, scale = norm_parts(v)
        e = dn * gain
        d = (e - jnp.mean(e, axis=-1, keepdims=True) - hat * jnp.mean(e * hat, axis=-1, keepdims=True)) * scale
        return d, jnp.sum(dn * hat, axis=0, keepdims=True), jnp.sum(dn, axis=0, keepdims=True)

    def second_norm(b):
        dn = dot_nt(B[tok(b), :], W[...])
        d, dgain, dshift = norm_back(dn, R[tok(b), :], vec[5:6, :])
        d = d + cot[tok(b), :].astype(F32)
        R[tok(b), :] = d
        B[tok(b), 3 * D :] = d.astype(BF)
        vg[5:6, :] = vg[5:6, :] + dgain
        vg[6:7, :] = vg[6:7, :] + dshift

    def t_out(k):
        once(ld_qkvm)
        vg[4:5, :] = dot_nn(ones, B[:, 3 * D :])[0:1, :]
        gradient(A[:, 3 * D :], B[:, 3 * D :], 8 % RING)

    def mixed_back(b):
        A[tok(b), 3 * D :] = dot_nt(B[tok(b), 3 * D :], W[:, 3 * D :]).astype(BF)

    def attention_back(i):
        low, high = head_masks()
        lane = lax.broadcasted_iota(jnp.int32, (1, 128), 1) < 64
        bias = segment_bias(seg, i)
        r = pl.ds(pl.multiple_of(i * 128, 128), 128)
        for p in range(6):
            col = 128 * p
            q = A[r, col : col + 128]
            k2 = stack_heads(A[r, D + col : D + col + 128], low, high)
            v2 = stack_heads(A[r, 2 * D + col : 2 * D + col + 128], low, high)
            dm = A[r, 3 * D + col : 3 * D + col + 128]
            soft = soft_pair(q, k2, bias)
            dp = dot_nt(dm, v2)
            both = dot_tn(soft.astype(BF), dm)
            B[r, 2 * D + col : 2 * D + col + 128] = jnp.where(lane, both[:128], both[128:]).astype(BF)
            halves = []
            for h in (0, 1):
                part = dp[:, 128 * h : 128 * h + 128]
                so = soft[:, 128 * h : 128 * h + 128]
                halves.append(so * (part - jnp.sum(part * so, axis=-1, keepdims=True)))
            ds = jnp.concatenate(halves, axis=1).astype(BF)
            B[r, col : col + 128] = (dot_nn(ds, k2) * SCALE).astype(BF)
            both = dot_tn(ds, q) * SCALE
            B[r, D + col : D + col + 128] = jnp.where(lane, both[:128], both[128:]).astype(BF)

    def t_att(lo, n):
        span(attention_back, 2 * lo, 2 * n)

    def t_qkv(lo, n):
        once(ld_nrm)
        if lo == 0:
            vg[2:3, :] = dot_nn(ones, B[:, 0:D])[0:1, :]
            vg[3:4, :] = dot_nn(ones, B[:, 2 * D : 3 * D])[0:1, :]
        span(lambda u: gradient(E[...], B[:, wide(u)], (u + 1) % RING), lo, n)

    def ig_remote(b):
        return remote(n2.at[tok(b)], ig_land.at[tok(b)], igs.at[b], igr.at[b], partner)

    def ig_local(b):
        return pltpu.make_async_copy(R.at[tok(b)], ig_o.at[tok(b)], igr.at[b])

    ld_land = load(ig_land, cot, 15)
    ld_ig = pltpu.make_async_copy(R, ig_o, lsem.at[16])

    def land(k):
        @pl.when(swapped)
        def _():
            for b in range(4):
                ig_remote(b).wait_recv()
            ld_land.start()
            ld_land.wait()

            def one(b):
                R[tok(b), :] = cot[tok(b), :].astype(F32)

            span(one, 0, 4)
            ld_ig.start()

    def first_norm_back(b):
        dn = dot_nt(B[tok(b), : 3 * D], W[:, : 3 * D])
        d, dgain, dshift = norm_back(dn, cot[tok(b), :].astype(F32), vec[0:1, :])
        R[tok(b), :] = R[tok(b), :] + d
        vg[0:1, :] = vg[0:1, :] + dgain
        vg[1:2, :] = vg[1:2, :] + dshift
        send_ig(b)

    def send_ig(b):
        @pl.when(swapped)
        def _():
            n2[tok(b), :] = R[tok(b), :].astype(BF)
            ig_remote(b).start()

        pl.when(kept)(lambda: ig_local(b).start())

    def cp_slice(j):
        return remote(vsl.at[j], vrc.at[2 * z + c], vss.at[j], vsr.at[2 * z + c], (2 * x + y, j))

    def each_slice(fn):
        def step(j, carry):
            pl.when(jnp.logical_or(swapped, j != f))(lambda: fn(j))
            return carry

        lax.fori_loop(0, 8, step, 0)

    def send_slices(k):
        for j in range(8):
            vsl[j, :, 0:SHARD] = vg[:, SHARD * j : SHARD * j + SHARD]

        @pl.when(kept)
        def _():
            vrc[pl.ds(2 * z + c, 1)] = vsl[pl.ds(f, 1)]

        each_slice(lambda j: cp_slice(j).start())

    def cp_change(k):
        return remote(vdl.at[g], vdl.at[g], vds.at[k], vdr.at[g], members[k])

    def t_vec_adam(k):
        def step(s, carry):
            pl.when(jnp.logical_or(swapped, s != 2 * z + c))(
                lambda: remote(vrc.at[s], vrc.at[s], vss.at[0], vsr.at[s], partner).wait_recv()
            )
            return carry

        lax.fori_loop(0, 8, step, 0)
        grad = jnp.sum(vrc[...], axis=0)[0:12, 0:SHARD]
        first = jnp.concatenate([v1[r] for r in range(12)], axis=0)
        second = jnp.concatenate([v2[r] for r in range(12)], axis=0)
        mom, sq, delta = adam_parts(first, second, vw[...], grad, RATE_VECTOR, 0.0)
        vm_o[...] = mom
        vs_o[...] = sq
        vdl[g, 0:12, 0:SHARD] = delta
        for k in range(3):
            cp_change(k).start()

    def t_vec_outer(k):
        for k in range(3):
            remote(vdl.at[froms[k]], vdl.at[froms[k]], vds.at[k], vdr.at[froms[k]], members[k]).wait_recv()
        mean = jnp.sum(vdl[...], axis=0)[0:12, 0:SHARD] * 0.25
        mom = OUTER_MOMENTUM * vo[...] + mean
        vp_o[...] = mom
        vq_o[...] = vw[...] - OUTER_RATE * (mean + OUTER_MOMENTUM * mom)

    members = [dev(x, 1 - c, z, y), dev(1 - x, c, z, y), dev(1 - x, 1 - c, z, y)]
    froms = [2 * x + 1 - c, 2 * (1 - x) + c, 2 * (1 - x) + 1 - c]

    def cp_core(p):
        return remote(G.at[p % RING, 1 - c], S.at[p], d2s.at[p], d2r.at[p], dev(x, 1 - c, z, y))

    def hop_up(p, t, k):
        return remote(S.at[p, t], ZI.at[p, t - z - 1], zs.at[p, k], zr.at[p, t - z - 1], dev(x, c, z + 1, y))

    def hop_down(p, t, k):
        return remote(S.at[p, t], ZI.at[p, 5 - z + t], zs.at[p, k], zr.at[p, 5 - z + t], dev(x, c, z - 1, y))

    def got(p, k):
        remote(ZI.at[p, k], ZI.at[p, k], zs.at[p, 0], zr.at[p, k], partner).wait_recv()

    def add_in(p, t, k):
        got(p, k)
        S[p, t] = (S[p, t].astype(F32) + ZI[p, k].astype(F32)).astype(BF)

    def s0(p):
        cp_core(p).start()

    def s1(p):
        cp_core(p).wait_recv()

        def one(t):
            S[p, t] = (S[p, t].astype(F32) + G[p % RING, c, t].astype(F32)).astype(BF)

        span(one, 0, 4)

        @pl.when(z == 0)
        def _():
            for k, t in enumerate((3, 2, 1)):
                hop_up(p, t, k).start()

        @pl.when(z == 3)
        def _():
            for k, t in enumerate((0, 1, 2)):
                hop_down(p, t, k).start()

        cp_core(p).wait_send()

    def s2(p):
        @pl.when(z == 1)
        def _():
            for k, t in enumerate((3, 2)):
                add_in(p, t, t - 1)
                hop_up(p, t, k).start()

        @pl.when(z == 2)
        def _():
            for k, t in enumerate((0, 1)):
                add_in(p, t, 2 + t)
                hop_down(p, t, k).start()

    def s3(p):
        @pl.when(z == 2)
        def _():
            add_in(p, 3, 1)
            hop_up(p, 3, 2).start()

        @pl.when(z == 1)
        def _():
            add_in(p, 0, 3)
            hop_down(p, 0, 2).start()

    def cp_final(p):
        return remote(S.at[p, z], FIN.at[p], fs.at[p], fr.at[p], partner)

    def col(p):
        return pl.ds(768 * (p % 4 if p < 8 else (p + 3) % 4), 768)

    def state_loads(p, fn):
        q = p % 2
        m = 1 - p // 4
        for k, src in enumerate((m1, m2, mw, mo) if p < 8 else (a1, a2, aw, ao)):
            src = src.at[m, :, col(p)] if p < 8 else src.at[:, col(p)]
            fn(pltpu.make_async_copy(src, IN.at[q, k], isem.at[q, k]))

    def state_stores(p, ks, fn):
        q = p % 2
        m = 1 - p // 4
        for k in ks:
            dst = ((mm_o, ms_o, mp_o, mq_o) if p < 8 else (am_o, as_o, ap_o, aq_o))[k]
            dst = dst.at[m, :, col(p)] if p < 8 else dst.at[:, col(p)]
            fn(pltpu.make_async_copy(OUT.at[q, k], dst, osem.at[q, k]))

    def start(cp):
        cp.start()

    def wait(cp):
        cp.wait()

    def s4(p):
        pl.when(z > 0)(lambda: add_in(p, z, 0))
        pl.when(z < 3)(lambda: add_in(p, z, 4))

        @pl.when(swapped)
        def _():
            cp_final(p).start()

        @pl.when(kept)
        def _():
            FIN[p] = S[p, z]

    def cp_delta(p, k):
        i = (g, g, froms[1])[k]
        return remote(DL.at[p, i], DL.at[p, i], ls.at[p, k], lr.at[p, i], members[1 if k == 1 else 0])

    def got_delta(p, k):
        i = froms[k]
        remote(DL.at[p, i], DL.at[p, i], ls.at[p, 0], lr.at[p, i], members[k]).wait_recv()

    def s5(p):
        pl.when(swapped)(lambda: cp_final(p).wait_recv())
        state_loads(p, wait)
        if p >= 2:
            state_stores(p - 2, (0, 1), wait)
        q = p % 2

        def rows(i, carry):
            r = pl.ds(pl.multiple_of(i * 32, 32), 32)
            mom, sq, delta = adam_parts(
                IN[q, 0, r, :], IN[q, 1, r, :], IN[q, 2, r, :], FIN[p, r, :].astype(F32), RATE_MATRIX, WEIGHT_DECAY
            )
            OUT[q, 0, r, :] = mom
            OUT[q, 1, r, :] = sq
            DL[p, g, r, :] = delta.astype(BF)
            return carry

        lax.fori_loop(0, 3, rows, 0)
        for k in (1, 0):
            cp_delta(p, k).start()
        state_stores(p, (0, 1), start)

    def s6(p):
        got_delta(p, 1)
        cp_delta(p, 2).start()

    def s7(p):
        got_delta(p, 0)
        got_delta(p, 2)
        if p >= 2:
            state_stores(p - 2, (2, 3), wait)
        q = p % 2

        def rows(i, carry):
            r = pl.ds(pl.multiple_of(i * 32, 32), 32)
            total = DL[p, 0, r, :].astype(F32)
            for k in (1, 2, 3):
                total = total + DL[p, k, r, :].astype(F32)
            mean = total * 0.25
            mom = OUTER_MOMENTUM * IN[q, 3, r, :] + mean
            OUT[q, 2, r, :] = mom
            OUT[q, 3, r, :] = IN[q, 2, r, :] - OUTER_RATE * (mean + OUTER_MOMENTUM * mom)
            return carry

        lax.fori_loop(0, 3, rows, 0)
        state_stores(p, (2, 3), start)

    sums = (s0, s1, s2, s3, s4, s5, s6, s7)
    does = {
        "g": lambda p, s: stages[s](p), "r": lambda p, k: sums[k](p), "il": lambda p: state_loads(p, start),
        "st": lambda k: None, "gd": t_down, "dh": lambda h, lo, n: spanned(functools.partial(hidden_back, h), ld_wd, ld_gp)(lo, n), "bo": spanned(block_output, ld_res),
        "ld": loads, "gu": t_up, "n2": spanned(second_norm, ld_wu), "go": t_out, "dm": spanned(mixed_back, ld_wa),
        "ab": t_att, "gq": t_qkv, "n1": spanned(first_norm_back, ld_xv), "ic": land,
        "vs": send_slices, "va": t_vec_adam, "vo": t_vec_outer,
    }
    for name, *at in ORDER_BACKWARD:
        does[name](*at)

    for p in range(RS):
        for k in range(3):
            remote(S.at[p, k], ZI.at[p, k], zs.at[p, k], zr.at[p, k], partner).wait_send()
        pl.when(swapped)(lambda: cp_final(p).wait_send())
        for k in range(3):
            cp_delta(p, k).wait_send()
    for p in (RS - 2, RS - 1):
        state_stores(p, (0, 1, 2, 3), wait)
    each_slice(lambda j: cp_slice(j).wait_send())
    for k in range(3):
        cp_change(k).wait_send()
    for b in range(4):

        @pl.when(swapped)
        def _():
            out_remote(b).wait_recv()
            ig_remote(b).wait_send()

        @pl.when(kept)
        def _():
            ig_local(b).wait()

    pl.when(swapped)(lambda: ld_ig.wait())


def backward(cot, fwd, states):
    any_ = pl.BlockSpec(memory_space=pl.ANY)
    vm = pl.BlockSpec(memory_space=pltpu.VMEM)
    dma = pltpu.SemaphoreType.DMA
    attn = jax.ShapeDtypeStruct((SHARD, FF), F32)
    mlp = jax.ShapeDtypeStruct((2, SHARD, FF), F32)
    vect = jax.ShapeDtypeStruct((12, SHARD), F32)
    return pl.pallas_call(
        backward_kernel,
        out_shape=(
            jax.ShapeDtypeStruct((T, D), BF), jax.ShapeDtypeStruct((T, D), F32),
            attn, attn, attn, attn, mlp, mlp, mlp, mlp, vect, vect, vect, vect,
            jax.ShapeDtypeStruct((T, D), BF),
        ),
        in_specs=[any_] * 11 + [vm, vm] + [any_] * 8 + [vm] * 4,
        out_specs=(any_,) * 10 + (vm,) * 4 + (any_,),
        scratch_shapes=[
            pltpu.VMEM((T, FF), BF), pltpu.VMEM((T, FF), BF), pltpu.VMEM((D, FF), BF),
            pltpu.VMEM((T, D), BF), pltpu.VMEM((T, D), BF), pltpu.VMEM((T, D), BF), pltpu.VMEM((T, D), F32),
            pltpu.VMEM((RING, 2, 4, SHARD, 768), BF), pltpu.VMEM((RS, 4, SHARD, 768), BF),
            pltpu.VMEM((RS, 5, SHARD, 768), BF), pltpu.VMEM((RS, SHARD, 768), BF),
            pltpu.VMEM((RS, 4, SHARD, 768), BF),
            pltpu.VMEM((2, 4, SHARD, 768), F32), pltpu.VMEM((2, 4, SHARD, 768), F32),
            pltpu.VMEM((16, D), F32), pltpu.VMEM((8, D), F32),
            pltpu.VMEM((8, 16, 128), F32), pltpu.VMEM((8, 16, 128), F32), pltpu.VMEM((4, 16, 128), F32),
            dma((21,)), dma((RS,)), dma((RS,)), dma((RS, 3)), dma((RS, 5)), dma((RS,)), dma((RS,)),
            dma((RS, 3)), dma((RS, 4)), dma((2, 4)), dma((2, 4)), dma((4,)), dma((4,)), dma((4,)), dma((4,)),
            dma((8,)), dma((8,)), dma((3,)), dma((4,)),
            *GATHER_SEMS(1),
        ],
        compiler_params=pltpu.CompilerParams(collective_id=2, has_side_effects=True, vmem_limit_bytes=63 * 2**20),
        name="backward",
    )(cot, *fwd, *states)


def fast(
    inputs, segments, cotangent,
    attn_weight, attn_first, attn_second, attn_outer,
    mlp_weight, mlp_first, mlp_second, mlp_outer,
    vector_weight, vector_first, vector_second, vector_outer,
):
    fwd = forward(inputs[0], cotangent[0], segments[0], attn_weight, mlp_weight, vector_weight)
    out = backward(
        cotangent[0],
        fwd,
        (
            attn_weight, attn_first[0], attn_second[0], attn_outer,
            mlp_weight, mlp_first[0], mlp_second[0], mlp_outer,
            vector_weight, jnp.transpose(vector_first, (1, 0, 2)), jnp.transpose(vector_second, (1, 0, 2)), vector_outer,
        ),
    )
    lead = (1, 1, 1, 1, 0, 0, 1, 1, 0, 0, 0, 0, 0, 0)
    return tuple(v[None] if k else v for v, k in zip(finish(out[:14]), lead))


def norm_apply(values, gain, shift):
    centre = values - jnp.mean(values, axis=-1, keepdims=True)
    spread = jnp.mean(centre * centre, axis=-1, keepdims=True)
    return centre * lax.rsqrt(spread + EPS_NORM) * gain + shift


def gelu_tanh(values):
    return jax.nn.gelu(values, approximate=True)


def adam_step(weight, first, second, gradient, step_rate, weight_decay):
    first_new = BETA_ONE * first + (1.0 - BETA_ONE) * gradient
    second_new = BETA_TWO * second + (1.0 - BETA_TWO) * gradient * gradient
    first_hat = first_new / (1.0 - BETA_ONE**STEP)
    second_hat = second_new / (1.0 - BETA_TWO**STEP)
    local_weight = weight - step_rate * (
        first_hat / (jnp.sqrt(second_hat) + ADAM_EPS) + weight_decay * weight
    )
    return (first_new, second_new, weight - local_weight)


def local(
    inputs,
    segments,
    cotangent,
    attn_weight,
    attn_first,
    attn_second,
    attn_outer,
    mlp_weight,
    mlp_first,
    mlp_second,
    mlp_outer,
    vector_weight,
    vector_first,
    vector_second,
    vector_outer,
):
    bf16 = jnp.bfloat16
    f32 = jnp.float32
    attn_cast = attn_weight.astype(bf16)
    mlp_cast = mlp_weight.astype(bf16)
    attn_low, mlp_low, vector_low = (
        lax.all_gather(attn_cast, "fsdp", axis=0, tiled=True),
        lax.all_gather(mlp_cast, "fsdp", axis=1, tiled=True),
        lax.all_gather(vector_weight.astype(bf16), "fsdp", axis=1, tiled=True),
    )
    vectors = vector_low.astype(f32)
    tokens_f = inputs[0].astype(f32)
    seg_ids = segments[0]
    back_f = cotangent[0].astype(f32)
    model_width = attn_low.shape[0]
    head_dim = model_width // HEADS
    score_scale = head_dim ** (-0.5)
    tok_count = tokens_f.shape[0]
    row_count = tok_count // SEQ
    shape_four = (row_count, SEQ, HEADS, head_dim)
    normed_f, norm_pull = jax.vjp(norm_apply, tokens_f, vectors[0], vectors[1])
    normed = normed_f.astype(bf16)
    project = jnp.dot(normed, attn_low[:, : 3 * model_width], preferred_element_type=f32)
    queries = (project[:, :model_width] + vectors[2]).astype(bf16).reshape(shape_four)
    keys_all = project[:, model_width : 2 * model_width].astype(bf16).reshape(shape_four)
    values_all = (
        (project[:, 2 * model_width : 3 * model_width] + vectors[3])
        .astype(bf16)
        .reshape(shape_four)
    )
    scores = (
        jnp.einsum("rqhd,rkhd->rhqk", queries, keys_all, preferred_element_type=f32) * score_scale
    )
    same_seg = (seg_ids[:, :, None] == seg_ids[:, None, :])[:, None]
    masked = jnp.where(same_seg, scores, NEG_LARGE)
    exponent = jnp.exp(masked - jnp.max(masked, axis=-1, keepdims=True))
    soft = exponent / jnp.sum(exponent, axis=-1, keepdims=True)
    probs = soft.astype(bf16)
    mixed = (
        jnp.einsum("rhqk,rkhd->rqhd", probs, values_all, preferred_element_type=f32)
        .reshape(tok_count, model_width)
        .astype(bf16)
    )
    attended = (
        jnp.dot(mixed, attn_low[:, 3 * model_width :], preferred_element_type=f32) + vectors[4]
    )
    residual = tokens_f + attended
    normed_two_f, norm_two_pull = jax.vjp(norm_apply, residual, vectors[5], vectors[6])
    normed_two = normed_two_f.astype(bf16)
    up_pre = jnp.dot(normed_two, mlp_low[0], preferred_element_type=f32) + vectors[8:12].reshape(-1)
    hidden_f, gelu_pull = jax.vjp(gelu_tanh, up_pre)
    hidden = hidden_f.astype(bf16)
    branch = jnp.einsum("nf,df->nd", hidden, mlp_low[1], preferred_element_type=f32) + vectors[7]
    block_out = (residual + branch).astype(bf16)
    d_branch = cotangent[0]
    d_down_bias = jnp.sum(back_f, axis=0)
    grad_down = jnp.einsum("nd,nf->df", d_branch, hidden, preferred_element_type=f32)
    d_hidden = jnp.einsum("nd,df->nf", d_branch, mlp_low[1], preferred_element_type=f32)
    (d_up_f,) = gelu_pull(d_hidden)
    d_up = d_up_f.astype(bf16)
    d_up_bias = jnp.sum(d_up.astype(f32), axis=0)
    grad_up = jnp.einsum("nd,nf->df", normed_two, d_up, preferred_element_type=f32)
    mlp_grad = jnp.stack([grad_up, grad_down])
    d_normed_two = jnp.einsum("nf,df->nd", d_up, mlp_low[0], preferred_element_type=f32)
    d_res_norm, d_gain_two, d_shift_two = norm_two_pull(d_normed_two)
    d_res = back_f + d_res_norm
    d_att = d_res.astype(bf16)
    d_out_bias = jnp.sum(d_att.astype(f32), axis=0)
    grad_out = jnp.einsum("nc,nd->cd", mixed, d_att, preferred_element_type=f32)
    d_mixed = (
        jnp.einsum("nd,cd->nc", d_att, attn_low[:, 3 * model_width :], preferred_element_type=f32)
        .astype(bf16)
        .reshape(shape_four)
    )
    d_values = (
        jnp.einsum("rhqk,rqhd->rkhd", probs, d_mixed, preferred_element_type=f32)
        .reshape(tok_count, model_width)
        .astype(bf16)
    )
    d_probs = jnp.einsum("rqhd,rkhd->rhqk", d_mixed, values_all, preferred_element_type=f32)
    d_scores = (soft * (d_probs - jnp.sum(d_probs * soft, axis=-1, keepdims=True))).astype(bf16)
    d_queries = (
        (
            jnp.einsum("rhqk,rkhd->rqhd", d_scores, keys_all, preferred_element_type=f32)
            * score_scale
        )
        .reshape(tok_count, model_width)
        .astype(bf16)
    )
    d_keys = (
        (jnp.einsum("rhqk,rqhd->rkhd", d_scores, queries, preferred_element_type=f32) * score_scale)
        .reshape(tok_count, model_width)
        .astype(bf16)
    )
    d_query_bias = jnp.sum(d_queries.astype(f32), axis=0)
    d_value_bias = jnp.sum(d_values.astype(f32), axis=0)
    d_project = jnp.concatenate([d_queries, d_keys, d_values], axis=1)
    grad_qkv = jnp.einsum("nc,nd->cd", normed, d_project, preferred_element_type=f32)
    d_normed = jnp.einsum(
        "nd,cd->nc", d_project, attn_low[:, : 3 * model_width], preferred_element_type=f32
    )
    d_tok_norm, d_gain_one, d_shift_one = norm_pull(d_normed)
    input_grad = d_res + d_tok_norm
    attn_grad = jnp.concatenate([grad_qkv, grad_out], axis=1)
    vector_grad = jnp.concatenate(
        [
            jnp.stack(
                [
                    d_gain_one,
                    d_shift_one,
                    d_query_bias,
                    d_value_bias,
                    d_out_bias,
                    d_gain_two,
                    d_shift_two,
                    d_down_bias,
                ]
            ),
            d_up_bias.reshape(4, model_width),
        ],
        axis=0,
    )
    attn_sum, mlp_sum, vector_sum = (
        lax.psum_scatter(attn_grad.astype(bf16), "fsdp", scatter_dimension=0, tiled=True).astype(f32),
        lax.psum_scatter(mlp_grad.astype(bf16), "fsdp", scatter_dimension=1, tiled=True).astype(f32),
        lax.psum_scatter(vector_grad, "fsdp", scatter_dimension=1, tiled=True),
    )
    attn_moment, attn_square, attn_delta = adam_step(
        attn_weight, attn_first[0], attn_second[0], attn_sum, RATE_MATRIX, WEIGHT_DECAY
    )
    mlp_moment, mlp_square, mlp_delta = adam_step(
        mlp_weight, mlp_first[0], mlp_second[0], mlp_sum, RATE_MATRIX, WEIGHT_DECAY
    )
    vector_moment, vector_square, vector_delta = adam_step(
        vector_weight, vector_first[0], vector_second[0], vector_sum, RATE_VECTOR, 0.0
    )
    group_count = lax.axis_size("group")
    attn_total, mlp_total, vector_total = (
        lax.psum(attn_delta.astype(jnp.bfloat16), "group").astype(jnp.float32),
        lax.psum(mlp_delta.astype(jnp.bfloat16), "group").astype(jnp.float32),
        lax.psum(vector_delta.astype(jnp.bfloat16), "group").astype(jnp.float32),
    )
    attn_mean = attn_total / group_count
    mlp_mean = mlp_total / group_count
    vector_mean = vector_total / group_count
    attn_momentum = OUTER_MOMENTUM * attn_outer + attn_mean
    mlp_momentum = OUTER_MOMENTUM * mlp_outer + mlp_mean
    vector_momentum = OUTER_MOMENTUM * vector_outer + vector_mean
    attn_master = attn_weight - OUTER_RATE * (attn_mean + OUTER_MOMENTUM * attn_momentum)
    mlp_master = mlp_weight - OUTER_RATE * (mlp_mean + OUTER_MOMENTUM * mlp_momentum)
    vector_master = vector_weight - OUTER_RATE * (vector_mean + OUTER_MOMENTUM * vector_momentum)
    return (
        block_out[None],
        input_grad[None],
        attn_moment[None],
        attn_square[None],
        attn_momentum,
        attn_master,
        mlp_moment[None],
        mlp_square[None],
        mlp_momentum,
        mlp_master,
        vector_moment[None],
        vector_square[None],
        vector_momentum,
        vector_master,
    )


def solution(mesh):
    in_specs = (
        P("group", "fsdp", None),
        P("group", "fsdp", None),
        P("group", "fsdp", None),
        P("fsdp", None),
        P("group", "fsdp", None),
        P("group", "fsdp", None),
        P("fsdp", None),
        P(None, "fsdp", None),
        P("group", None, "fsdp", None),
        P("group", None, "fsdp", None),
        P(None, "fsdp", None),
        P(None, "fsdp"),
        P("group", None, "fsdp"),
        P("group", None, "fsdp"),
        P(None, "fsdp"),
    )
    out_specs = (
        P("group", "fsdp", None),
        P("group", "fsdp", None),
        P("group", "fsdp", None),
        P("group", "fsdp", None),
        P("fsdp", None),
        P("fsdp", None),
        P("group", None, "fsdp", None),
        P("group", None, "fsdp", None),
        P(None, "fsdp", None),
        P(None, "fsdp", None),
        P("group", None, "fsdp"),
        P("group", None, "fsdp"),
        P(None, "fsdp"),
        P(None, "fsdp"),
    )
    fits = mesh.shape["group"] == 4 and mesh.shape["fsdp"] == 8
    return jax.shard_map(fast if fits else local, mesh=mesh, in_specs=in_specs, out_specs=out_specs, check_vma=False)
```

```python
import functools

import jax
import jax.numpy as jnp
from jax import lax
from jax.experimental import pallas as pl
from jax.experimental.pallas import tpu as pltpu
from jax.sharding import PartitionSpec as P

EPS_NORM = 1e-05
NEG_LARGE = -1e30
HEADS = 12
SEQ = 64
STEP = 10
BETA_ONE = 0.9
BETA_TWO = 0.999
ADAM_EPS = 1e-08
RATE_MATRIX = 0.05
RATE_VECTOR = 0.5
WEIGHT_DECAY = 0.1
OUTER_RATE = 0.7
OUTER_MOMENTUM = 0.9


ORDER_FORWARD = (
    ("cast", 0), ("g", 0, 0), ("g", 1, 0), ("xs", 0), ("cast", 1), ("cast", 2), ("g", 2, 0), ("g", 3, 0),
    ("xs", 3), ("xs", 1), ("xs", 2), ("g", 0, 1), ("g", 4, 0), ("g", 1, 1), ("g", 0, 2), ("vec", 0), ("g", 1, 2),
    ("cs", 0), ("g", 0, 3), ("g", 1, 3), ("g", 2, 1), ("g", 0, 4), ("g", 1, 4), ("g", 2, 2), ("g", 3, 1),
    ("g", 0, 5), ("g", 1, 5), ("g", 2, 3), ("ln", 0, 4), ("g", 3, 2), ("g", 1, 6), ("g", 0, 6), ("v", 0, 4),
    ("qk", 0, 4), ("g", 3, 3), ("g", 2, 4), ("g", 4, 1), ("at", 0, 2), ("g", 3, 4), ("at", 2, 2), ("g", 2, 5),
    ("g", 4, 2), ("on", 0, 4), ("g", 4, 3), ("g", 2, 6), ("u", 0, 0, 2), ("g", 3, 5), ("u", 0, 2, 2), ("g", 4, 4),
    ("g", 3, 6), ("u", 1, 2, 2), ("u", 1, 0, 2), ("g", 4, 5), ("g", 4, 6), ("end", 0),
)

ORDER_BACKWARD = (
    ("st", 0), ("g", 0, 0), ("gd", 0, 2), ("r", 0, 0), ("r", 1, 0), ("g", 0, 1), ("il", 1), ("r", 0, 1),
    ("r", 1, 1), ("g", 0, 2), ("gd", 2, 2), ("r", 3, 0), ("r", 2, 0), ("il", 0), ("g", 0, 3), ("dh", 0, 0, 4),
    ("g", 0, 4), ("r", 2, 1), ("r", 0, 2), ("r", 3, 1), ("g", 0, 5), ("gu", 0, 2), ("r", 1, 2), ("r", 0, 3),
    ("r", 5, 0), ("r", 4, 0), ("g", 0, 6), ("dh", 1, 0, 4), ("r", 0, 4), ("r", 1, 3), ("r", 5, 1), ("bo", 0, 4),
    ("r", 2, 2), ("ld", 0), ("r", 0, 5), ("r", 4, 1), ("gu", 2, 2), ("r", 7, 0), ("r", 6, 0), ("r", 2, 3),
    ("n2", 2, 2), ("r", 7, 1), ("r", 5, 2), ("r", 0, 6), ("n2", 0, 2), ("ld", 1), ("r", 6, 1), ("r", 2, 4),
    ("r", 1, 4), ("r", 3, 2), ("go", 0), ("dm", 0, 4), ("r", 5, 3), ("r", 0, 7), ("r", 4, 2), ("r", 3, 3),
    ("r", 1, 5), ("il", 2), ("ab", 2, 2), ("r", 8, 0), ("r", 5, 4), ("r", 1, 6), ("r", 2, 5), ("r", 4, 3),
    ("ab", 0, 2), ("r", 6, 2), ("r", 7, 2), ("r", 2, 6), ("r", 8, 1), ("gq", 0, 2), ("r", 9, 0), ("r", 1, 7),
    ("r", 3, 4), ("r", 6, 3), ("r", 4, 4), ("n1", 0, 2), ("r", 8, 2), ("r", 2, 7), ("il", 4), ("il", 3),
    ("r", 9, 1), ("r", 10, 0), ("r", 3, 5), ("r", 7, 3), ("r", 4, 5), ("r", 9, 2), ("r", 6, 4), ("n1", 2, 2),
    ("r", 3, 6), ("r", 8, 3), ("r", 10, 1), ("r", 3, 7), ("il", 5), ("r", 9, 3), ("r", 5, 5), ("r", 4, 6),
    ("r", 10, 2), ("gq", 2, 1), ("r", 11, 0), ("r", 4, 7), ("il", 6), ("r", 6, 5), ("r", 7, 4), ("r", 10, 3),
    ("r", 11, 1), ("r", 5, 6), ("r", 5, 7), ("il", 7), ("r", 8, 4), ("r", 6, 6), ("r", 7, 5), ("r", 11, 2),
    ("r", 6, 7), ("il", 8), ("r", 9, 4), ("r", 8, 5), ("r", 10, 4), ("vs", 0), ("r", 7, 6), ("r", 11, 3),
    ("r", 7, 7), ("il", 9), ("r", 9, 5), ("r", 8, 6), ("r", 8, 7), ("il", 10), ("r", 11, 4), ("r", 10, 5),
    ("r", 9, 6), ("va", 0), ("r", 9, 7), ("il", 11), ("r", 11, 5), ("ic", 0), ("r", 10, 6), ("r", 10, 7),
    ("r", 11, 6), ("vo", 0), ("r", 11, 7),
)


MESH = pl.DeviceIdType.MESH
BF = jnp.bfloat16
F32 = jnp.float32
D = 768
FF = 3072
T = 1024
TB = 256
SHARD = 96
GELU_C = 0.7978845608028654
GELU_A = 0.044715
SCALE = 0.125


def dot_nn(a, b):
    return jnp.dot(a, b, preferred_element_type=F32)


def dot_nt(a, b):
    return lax.dot_general(a, b, (((1,), (1,)), ((), ())), preferred_element_type=F32)


def dot_tn(a, b):
    return lax.dot_general(a, b, (((0,), (0,)), ((), ())), preferred_element_type=F32)


def coords():
    g = lax.axis_index("group")
    f = lax.axis_index("fsdp")
    return g // 2, g % 2, f // 2, f % 2


def dev(x, c, z, y):
    return (2 * x + c, 2 * z + y)


def remote(src, dst, ssem, rsem, to):
    return pltpu.make_async_remote_copy(
        src_ref=src, dst_ref=dst, send_sem=ssem, recv_sem=rsem, device_id=to, device_id_type=MESH
    )


def norm_parts(v):
    centre = v - jnp.mean(v, axis=-1, keepdims=True)
    spread = jnp.mean(centre * centre, axis=-1, keepdims=True)
    scale = lax.rsqrt(spread + EPS_NORM)
    return centre * scale, scale


def head_masks():
    lane = lax.broadcasted_iota(jnp.int32, (1, 128), 1)
    low = (lane < 64).astype(F32).astype(BF)
    high = (lane >= 64).astype(F32).astype(BF)
    return low, high


def segment_bias(seg_ref, i):
    row = seg_ref[pl.ds(i, 1), :]
    classes = lax.broadcasted_iota(jnp.int32, (16, 128), 0)
    hot = (classes == row).astype(F32).astype(BF)
    same = dot_tn(hot, hot)
    bias = (same - 1.0) * (-NEG_LARGE)
    return jnp.concatenate([bias, bias], axis=1)


def soft_pair(q, k2, bias):
    s = dot_nt(q, k2) * SCALE + bias
    halves = []
    for h in (0, 1):
        part = s[:, 128 * h : 128 * h + 128]
        e = jnp.exp(part - jnp.max(part, axis=-1, keepdims=True))
        halves.append(e * (1.0 / jnp.sum(e, axis=-1, keepdims=True)))
    return jnp.concatenate(halves, axis=1)


def stack_heads(v, low, high):
    return jnp.concatenate([v * low, v * high], axis=0)


def gather_stages(view, sems, where, shift=0):
    x, c, z, y = where
    ys, yr, us, ds, zr, xs, xr, cs, cr = sems
    f = 2 * z + y
    other = 2 * z + 1 - y

    def rows(i):
        return pl.ds(pl.multiple_of(i * SHARD, 32), SHARD)

    def pair(i):
        return pl.ds(pl.multiple_of(i * 2 * SHARD, 64), 2 * SHARD)

    mine = 2 * x + c
    across = 2 * (1 - x) + c
    sib = 2 * x + 1 - c
    sib_across = 2 * (1 - x) + 1 - c

    def at(p, r, q):
        return view(p, r, pl.ds(pl.multiple_of(1536 * ((p + shift) % 2) + 384 * q, 128), 384))

    def cp_y(p, r):
        return remote(at(p, r, mine), at(p, r, mine), ys.at[p], yr.at[p], dev(x, c, z, 1 - y))

    def cp_up(p, i):
        return remote(at(p, pair(i), mine), at(p, pair(i), mine), us.at[p, i], zr.at[p, i], dev(x, c, z + 1, y))

    def cp_down(p, i):
        return remote(at(p, pair(i), mine), at(p, pair(i), mine), ds.at[p, i], zr.at[p, i], dev(x, c, z - 1, y))

    def cp_x(p, r, i, q):
        return remote(at(p, r, q), at(p, r, q), xs.at[p, i], xr.at[p, i], dev(1 - x, c, z, y))

    def cp_c(p, r, i, q, k):
        return remote(at(p, r, q), at(p, r, q), cs.at[p, 4 * k + i], cr.at[p, 4 * k + i], dev(x, 1 - c, z, y))

    def others(fn):
        for k in (1, 2, 3):
            pl.when(z >= k)(functools.partial(fn, z - k))
            pl.when(z + k <= 3)(functools.partial(fn, z + k))

    def sa(p):
        cp_y(p, rows(f)).start()

    def sb(p):
        cp_y(p, rows(other)).wait_recv()
        pl.when(z < 3)(lambda: cp_up(p, z).start())
        pl.when(z > 0)(lambda: cp_down(p, z).start())
        cp_x(p, rows(other), z, mine).start()
        cp_c(p, rows(other), z, mine, 0).start()

    def hop(k, p):
        def from_below():
            i = z - k
            cp_up(p, i).wait_recv()
            pl.when(z < 3)(lambda: cp_up(p, i).start())
            cp_x(p, pair(i), i, mine).start()
            cp_c(p, pair(i), i, mine, 0).start()

        def from_above():
            i = z + k
            cp_down(p, i).wait_recv()
            pl.when(z > 0)(lambda: cp_down(p, i).start())
            cp_x(p, pair(i), i, mine).start()
            cp_c(p, pair(i), i, mine, 0).start()

        pl.when(z >= k)(from_below)
        pl.when(z + k <= 3)(from_above)

    def sf(p):
        cp_x(p, rows(other), z, across).wait_recv()
        cp_c(p, rows(other), z, across, 1).start()

        def fwd(i):
            cp_x(p, pair(i), i, across).wait_recv()
            cp_c(p, pair(i), i, across, 1).start()

        others(fwd)

    def sg(p):
        cp_c(p, rows(other), z, sib, 0).wait_recv()
        cp_c(p, rows(other), z, sib_across, 1).wait_recv()

        def got(i):
            cp_c(p, pair(i), i, sib, 0).wait_recv()
            cp_c(p, pair(i), i, sib_across, 1).wait_recv()

        others(got)

    def drain(p):
        cp_y(p, rows(f)).wait_send()
        pl.when(z < 3)(lambda: cp_up(p, z).wait_send())
        pl.when(z > 0)(lambda: cp_down(p, z).wait_send())
        cp_x(p, rows(other), z, mine).wait_send()
        cp_c(p, rows(other), z, mine, 0).wait_send()
        cp_c(p, rows(other), z, across, 1).wait_send()
        for k in (1, 2, 3):

            @pl.when(z >= k)
            def _():
                pl.when(z < 3)(lambda: cp_up(p, z - k).wait_send())

            @pl.when(z + k <= 3)
            def _():
                pl.when(z > 0)(lambda: cp_down(p, z + k).wait_send())

        def sent(i):
            cp_x(p, pair(i), i, mine).wait_send()
            cp_c(p, pair(i), i, mine, 0).wait_send()
            cp_c(p, pair(i), i, across, 1).wait_send()

        others(sent)

    stages = [sa, sb, functools.partial(hop, 1), functools.partial(hop, 2), functools.partial(hop, 3), sf, sg]
    return stages, drain


GATHER_SEMS = lambda n: [
    pltpu.SemaphoreType.DMA((n,)),
    pltpu.SemaphoreType.DMA((n,)),
    pltpu.SemaphoreType.DMA((n, 4)),
    pltpu.SemaphoreType.DMA((n, 4)),
    pltpu.SemaphoreType.DMA((n, 4)),
    pltpu.SemaphoreType.DMA((n, 4)),
    pltpu.SemaphoreType.DMA((n, 4)),
    pltpu.SemaphoreType.DMA((n, 8)),
    pltpu.SemaphoreType.DMA((n, 8)),
]
PIECES = 5


def forward_kernel(
    x_in, cot_in, seg_raw, aw_in, mw_in, vw,
    w_out, qkvm_out, hid_out, gp_out, nrm_out, n2_out, res_out, xv_out, cotv_out, wd_out, vec_out, seg_out,
    w, xv, nrm, qkvm, res, n2, hid, gp, vec, seg, seg_in, tiles, ub,
    aw, mw, xsnd, xrcv, csnd, crcv, gsnd, grcv, vsnd, vrcv, osem, wsem,
    *gsems,
):
    where = coords()
    x, c, z, y = where
    f = 2 * z + y
    swapped = c != y
    partner = dev(x, y, z, c)

    shards = [pltpu.make_async_copy(aw_in, aw, wsem.at[0])]
    shards += [pltpu.make_async_copy(mw_in.at[k], mw.at[k], wsem.at[1 + k]) for k in range(2)]
    for cp in shards:
        cp.start()

    barrier = pltpu.get_barrier_semaphore()

    def greet(to):
        pl.semaphore_signal(barrier, inc=1, device_id=to, device_id_type=MESH)

    for k in range(1, 8):
        greet((2 * x + c, (f + k) % 8))
    greet(dev(x, 1 - c, z, y))
    greet(dev(1 - x, c, z, y))
    pl.when(swapped)(lambda: greet(partner))

    for i in range(8):
        seg_in[i : i + 1, :] = jnp.concatenate([seg_raw[2 * i : 2 * i + 1, :], seg_raw[2 * i + 1 : 2 * i + 2, :] + 8], axis=1)
    own = pl.ds(pl.multiple_of(f * SHARD, 32), SHARD)
    tiles[pl.ds(f, 1)] = jnp.zeros((1, 16, 128), F32)
    tiles[f, 0:12, 0:SHARD] = vw[...].astype(BF).astype(F32)

    pl.semaphore_wait(barrier, 9 + swapped.astype(jnp.int32))

    stages, drain = gather_stages(lambda p, r, q: w.at[p // 2, r, q], gsems, where)

    def cp_vec(k, j):
        return remote(tiles.at[j], tiles.at[j], vsnd.at[k - 1], vrcv.at[k - 1], (2 * x + c, (f + k) % 8))

    def tok(b, n=1):
        if isinstance(b, int):
            return pl.ds(b * TB, n * TB)
        return pl.ds(pl.multiple_of(b * TB, TB), n * TB)

    def span(fn, lo, n):
        def step(b, carry):
            fn(b)
            return carry

        lax.fori_loop(lo, lo + n, step, 0)

    def x_remote(b):
        return remote(x_in.at[tok(b)], xv.at[tok(b)], xsnd.at[b], xrcv.at[b], partner)

    def x_local(b):
        return pltpu.make_async_copy(x_in.at[tok(b)], xv.at[tok(b)], xrcv.at[b])

    def cot_remote():
        return remote(cot_in, cotv_out, csnd, crcv, partner)

    def seg_remote():
        return remote(seg_in, seg, gsnd, grcv, partner)

    outs = []

    def write(src, dst):
        cp = pltpu.make_async_copy(src, dst, osem.at[len(outs)])
        cp.start()
        outs.append(cp)

    def cast(m):
        shards[m].wait()
        if m == 1:
            w[1, own, :] = mw[0].astype(BF)
            return
        if m == 2:
            w[2, own, 0:1536] = mw[1, :, 0:1536].astype(BF)
            return
        w[0, own, :] = aw[...].astype(BF)
        for k in range(1, 8):
            cp_vec(k, f).start()

        @pl.when(swapped)
        def _():
            seg_remote().start()

        @pl.when(jnp.logical_not(swapped))
        def _():
            seg[...] = seg_in[...]
            for b in range(4):
                x_local(b).start()

    def send_x(b):
        pl.when(swapped)(lambda: x_remote(b).start())

    def send_cot(k):
        pl.when(swapped)(lambda: cot_remote().start())

    def gather(p, s):
        stages[s](p)
        if s == 6:
            half_at = pl.ds(1536 * (p % 2), 1536)
            write(w.at[p // 2, :, half_at], w_out.at[p // 2, :, half_at] if p < 4 else wd_out)

    def vectors():
        for k in range(1, 8):
            cp_vec(k, (f + 8 - k) % 8).wait_recv()
        total = jnp.zeros((16, D), F32)
        r = lax.broadcasted_iota(jnp.int32, (128, D), 0)
        q = lax.broadcasted_iota(jnp.int32, (128, D), 1)
        for j in range(8):
            pick = jnp.logical_and(q == r + SHARD * j, r < SHARD).astype(F32).astype(BF)
            total = total + dot_nn(tiles[j].astype(BF), pick)
        vec[...] = total
        for k in range(4):
            ub[0:1, D * k : D * k + D] = total[8 + k : 9 + k, :]

    def first_norm(b):
        @pl.when(swapped)
        def _():
            x_remote(b).wait_recv()

        @pl.when(jnp.logical_not(swapped))
        def _():
            x_local(b).wait()

        hat, _ = norm_parts(xv[tok(b), :].astype(F32))
        nrm[tok(b), :] = (hat * vec[0:1, :] + vec[1:2, :]).astype(BF)

    def queries_keys(b):
        r = dot_nn(nrm[tok(b), :], w[0, :, 0:1536])
        qkvm[tok(b), 0:D] = (r[:, 0:D] + vec[2:3, :]).astype(BF)
        qkvm[tok(b), D : 2 * D] = r[:, D : 2 * D].astype(BF)

    def values(b):
        r = dot_nn(nrm[tok(b), :], w[0, :, 1536:2304])
        qkvm[tok(b), 2 * D : 3 * D] = (r + vec[3:4, :]).astype(BF)

    def attention(i):
        low, high = head_masks()
        bias = segment_bias(seg, i)
        r = pl.ds(pl.multiple_of(i * 128, 128), 128)
        for p in range(6):
            col = 128 * p
            q = qkvm[r, col : col + 128]
            k2 = stack_heads(qkvm[r, D + col : D + col + 128], low, high)
            v2 = stack_heads(qkvm[r, 2 * D + col : 2 * D + col + 128], low, high)
            probs = soft_pair(q, k2, bias).astype(BF)
            qkvm[r, 3 * D + col : 3 * D + col + 128] = dot_nn(probs, v2).astype(BF)

    greeted = []

    def attend(lo, n):
        if not greeted:
            greeted.append(lo)
            pl.when(swapped)(lambda: seg_remote().wait_recv())
        span(attention, 2 * lo, 2 * n)
        write(qkvm.at[tok(lo, n)], qkvm_out.at[tok(lo, n)])

    def out_norm(b):
        att = dot_nn(qkvm[tok(b), 3 * D :], w[0, :, 2304:3072]) + vec[4:5, :]
        r = xv[tok(b), :].astype(F32) + att
        res[tok(b), :] = r
        hat, _ = norm_parts(r)
        n2[tok(b), :] = (hat * vec[5:6, :] + vec[6:7, :]).astype(BF)

    def up(half, b):
        for k in range(2):
            lo = 1536 * half + 768 * k
            u = dot_nn(n2[tok(b), :], w[1, :, lo : lo + 768]) + ub[0:1, lo : lo + 768]
            u2 = u * u
            t = jnp.tanh(u * (GELU_C + (GELU_C * GELU_A) * u2))
            h = 0.5 + 0.5 * t
            out = u * h
            hid[tok(b), lo : lo + 768] = out.astype(BF)
            slope = h + out * (1.0 - h) * (2.0 * GELU_C + (6.0 * GELU_C * GELU_A) * u2)
            gp[tok(b), lo : lo + 768] = slope.astype(BF)

    def spanned(fn, *pairs):
        def run(lo, n):
            span(fn, lo, n)
            for src, dst in pairs:
                write(src.at[tok(lo, n)], dst.at[tok(lo, n)])

        return run

    def up_half(half, lo, n):
        span(functools.partial(up, half), lo, n)
        half_at = pl.ds(1536 * half, 1536)
        write(hid.at[tok(lo, n), half_at], hid_out.at[tok(lo, n), half_at])
        write(gp.at[tok(lo, n), half_at], gp_out.at[tok(lo, n), half_at])

    does = {
        "g": gather, "cast": cast, "xs": send_x, "cs": send_cot, "vec": lambda k: vectors(),
        "ln": spanned(first_norm, (xv, xv_out), (nrm, nrm_out)), "qk": spanned(queries_keys), "v": spanned(values),
        "at": attend, "on": spanned(out_norm, (res, res_out), (n2, n2_out)), "u": up_half, "end": lambda k: None,
    }
    for name, *at in ORDER_FORWARD:
        does[name](*at)
    vec_out[...] = vec[...]
    seg_out[...] = seg[...]

    for p in range(PIECES):
        drain(p)
    for k in range(1, 8):
        cp_vec(k, f).wait_send()

    @pl.when(swapped)
    def _():
        seg_remote().wait_send()
        for b in range(4):
            x_remote(b).wait_send()
        cot_remote().wait()

    for cp in outs:
        cp.wait()


def forward(x, cot, seg, aw, mw, vw):
    any_ = pl.BlockSpec(memory_space=pl.ANY)
    vm = pl.BlockSpec(memory_space=pltpu.VMEM)
    wide = jax.ShapeDtypeStruct((T, FF), BF)
    slim = jax.ShapeDtypeStruct((T, D), BF)
    dma = pltpu.SemaphoreType.DMA
    return pl.pallas_call(
        forward_kernel,
        out_shape=(
            jax.ShapeDtypeStruct((2, D, FF), BF), wide, wide, wide, slim, slim,
            jax.ShapeDtypeStruct((T, D), F32), slim, slim, jax.ShapeDtypeStruct((D, 1536), BF),
            jax.ShapeDtypeStruct((16, D), F32), jax.ShapeDtypeStruct((8, 128), jnp.int32),
        ),
        in_specs=[any_, any_, vm, any_, any_, vm],
        out_specs=(any_,) * 10 + (vm, vm),
        scratch_shapes=[
            pltpu.VMEM((3, D, FF), BF), pltpu.VMEM((T, D), BF), pltpu.VMEM((T, D), BF), pltpu.VMEM((T, FF), BF),
            pltpu.VMEM((T, D), F32), pltpu.VMEM((T, D), BF), pltpu.VMEM((T, FF), BF), pltpu.VMEM((T, FF), BF),
            pltpu.VMEM((16, D), F32), pltpu.VMEM((8, 128), jnp.int32), pltpu.VMEM((8, 128), jnp.int32),
            pltpu.VMEM((8, 16, 128), F32),
            pltpu.VMEM((1, FF), F32),
            pltpu.VMEM((SHARD, FF), F32), pltpu.VMEM((2, SHARD, FF), F32),
            dma((4,)), dma((4,)), dma, dma, dma, dma, dma((7,)), dma((7,)), dma((40,)), dma((3,)),
            *GATHER_SEMS(PIECES),
        ],
        compiler_params=pltpu.CompilerParams(collective_id=1, has_side_effects=True, vmem_limit_bytes=60 * 2**20),
        name="forward",
    )(x, cot, seg, aw, mw, vw)


def final_kernel(*refs):
    ins, small, outs, small_outs = refs[:10], refs[10:14], refs[14:24], refs[24:28]
    bufs, rsem, wsem = refs[28:38], refs[38], refs[39]
    reads = [pltpu.make_async_copy(a, b, rsem.at[k]) for k, (a, b) in enumerate(zip(ins, bufs))]
    for cp in reads:
        cp.start()
    for k in range(4):
        if k < 2:
            for r in range(12):
                small_outs[k][r] = small[k][r : r + 1, :]
        else:
            small_outs[k][...] = small[k][...]
    writes = [pltpu.make_async_copy(b, a, wsem.at[k]) for k, (a, b) in enumerate(zip(outs, bufs))]
    for r, w in zip(reads, writes):
        r.wait()
        w.start()
    for w in writes:
        w.wait()


def finish(arrays):
    any_ = pl.BlockSpec(memory_space=pl.ANY)
    vm = pl.BlockSpec(memory_space=pltpu.VMEM)
    big, small = arrays[:10], arrays[10:14]
    shapes = [jax.ShapeDtypeStruct(a.shape, a.dtype) for a in big]
    thin = jax.ShapeDtypeStruct((12, 1, SHARD), F32)
    out = pl.pallas_call(
        final_kernel,
        out_shape=(*shapes, thin, thin, *[jax.ShapeDtypeStruct(a.shape, a.dtype) for a in small[2:]]),
        in_specs=[any_] * 10 + [vm] * 4,
        out_specs=(any_,) * 10 + (vm,) * 4,
        scratch_shapes=[pltpu.VMEM(a.shape, a.dtype) for a in big]
        + [pltpu.SemaphoreType.DMA((10,)), pltpu.SemaphoreType.DMA((10,))],
        compiler_params=pltpu.CompilerParams(vmem_limit_bytes=63 * 2**20),
        name="finish",
    )(*big, *small)
    return (*out[:10], jnp.transpose(out[10], (1, 0, 2)), jnp.transpose(out[11], (1, 0, 2)), out[12], out[13])


RS = 12
RING = 2


def adam_parts(first, second, weight, gradient, rate, decay):
    first_new = BETA_ONE * first + (1.0 - BETA_ONE) * gradient
    second_new = BETA_TWO * second + (1.0 - BETA_TWO) * gradient * gradient
    first_hat = first_new * (1.0 / (1.0 - BETA_ONE**STEP))
    second_hat = second_new * (1.0 / (1.0 - BETA_TWO**STEP))
    delta = rate * (first_hat / (jnp.sqrt(second_hat) + ADAM_EPS) + decay * weight)
    return first_new, second_new, delta


def backward_kernel(
    cot_in, w_in, qkvm_in, hid_in, gp_in, nrm_in, n2_in, res_in, xv_in, cotv_in, wd_in, vec, seg,
    aw, a1, a2, ao, mw, m1, m2, mo, vw, v1, v2, vo,
    out_o, ig_o, am_o, as_o, ap_o, aq_o, mm_o, ms_o, mp_o, mq_o, vm_o, vs_o, vp_o, vq_o, ig_land,
    A, B, W, cot, n2, E, R, G, S, ZI, FIN, DL, IN, OUT, vg, ubs, vsl, vrc, vdl,
    lsem, d2s, d2r, zs, zr, fs, fr, ls, lr, isem, osem, bos, bor, igs, igr, vss, vsr, vds, vdr, *gsems,
):
    x, c, z, y = coords()
    f = 2 * z + y
    g = 2 * x + c
    swapped = c != y
    kept = jnp.logical_not(swapped)
    partner = dev(x, y, z, c)

    barrier = pltpu.get_barrier_semaphore()

    def greet(to):
        pl.semaphore_signal(barrier, inc=1, device_id=to, device_id_type=MESH)

    me16 = c * 8 + f
    for k in range(1, 16):
        other = (me16 + k) % 16
        greet((2 * x + other // 8, other % 8))
    greet(dev(1 - x, c, z, y))
    greet(dev(1 - x, 1 - c, z, y))

    def tok(b, n=1):
        if isinstance(b, int):
            return pl.ds(b * TB, n * TB)
        return pl.ds(pl.multiple_of(b * TB, TB), n * TB)

    def span(fn, lo, n):
        def step(b, carry):
            fn(b)
            return carry

        lax.fori_loop(lo, lo + n, step, 0)

    def spanned(fn, *cps):
        def run(lo, n):
            once(*cps)
            span(fn, lo, n)

        return run

    own = pl.ds(pl.multiple_of(f * SHARD, 32), SHARD)
    stages, gather_drain = gather_stages(lambda p, r, q: W.at[r, q], gsems, (x, c, z, y), 1)

    def load(src, dst, k):
        return pltpu.make_async_copy(src, dst, lsem.at[k])

    ld_cot = load(cotv_in, cot, 0)
    ld_own = load(cot_in, cot, 0)
    ld_hid = [load(hid_in.at[:, 768 * i : 768 * i + 768], A.at[:, 768 * i : 768 * i + 768], 17 + i) for i in range(4)]
    ld_own_w = [load(mw.at[1, :, pl.ds(768 * k, 768)], IN.at[0, k], 11 + k) for k in (2, 3)]
    ld_wd = load(wd_in, W.at[:, 0:1536], 2)
    ld_gp = load(gp_in, B, 3)
    ld_res = load(res_in, R, 4)
    ld_n2 = load(n2_in, n2, 5)
    ld_wu = load(w_in.at[1], W, 6)
    ld_wa = load(w_in.at[0], W, 7)
    ld_qkvm = load(qkvm_in, A, 8)
    ld_nrm = load(nrm_in, E, 9)
    ld_xv = load(xv_in, cot, 10)
    for cp in ld_own_w:
        cp.start()
    pl.when(swapped)(lambda: ld_cot.start())
    pl.when(kept)(lambda: ld_own.start())
    for cp in (*ld_hid, ld_wd, ld_gp, ld_res, ld_n2):
        cp.start()
    vg[...] = jnp.zeros((16, D), F32)
    vsl[...] = jnp.zeros((8, 16, 128), F32)
    vdl[...] = jnp.zeros((4, 16, 128), F32)
    for k, cp in zip((2, 3), ld_own_w):
        cp.wait()
        W[own, 768 * k : 768 * k + 768] = IN[0, k].astype(BF)
    pl.semaphore_wait(barrier, 17)

    def wide(i, n=768):
        return pl.ds(i * n if isinstance(i, int) else pl.multiple_of(i * n, n), n)

    ones = jnp.ones((16, T), BF)

    def gradient(lhs, rhs, slot):
        out = dot_tn(lhs, rhs)
        for j in range(8):
            G[slot, j % 2, j // 2] = out[SHARD * j : SHARD * j + SHARD].astype(BF)

    def t_down(lo, n):
        if lo == 0:
            ld_cot.wait()
            vg[7:8, :] = dot_nn(ones, cot[...])[0:1, :]
        for i in range(lo, lo + n):
            ld_hid[i].wait()
        span(lambda v: gradient(cot[...], A[:, wide(v)], v % RING), lo, n)

    def out_remote(b):
        return remote(E.at[tok(b)], out_o.at[tok(b)], bos.at[b], bor.at[b], partner)

    def out_local(b):
        return pltpu.make_async_copy(E.at[tok(b)], out_o.at[tok(b)], bor.at[b])

    waited = set()

    def once(*cps):
        for cp in cps:
            if id(cp) not in waited:
                waited.add(id(cp))
                cp.wait()

    def hidden_back(half, b):
        for k in (2 * half, 2 * half + 1):
            lo = 768 * k
            dh = dot_nn(cot[tok(b), :], W[:, lo : lo + 768])
            B[tok(b), lo : lo + 768] = (dh * B[tok(b), lo : lo + 768].astype(F32)).astype(BF)

    def block_output(b):
        branch = dot_nt(A[tok(b), :], W[...])
        E[tok(b), :] = (R[tok(b), :] + branch + vec[7:8, :]).astype(BF)
        send_out(b)

    def send_out(b):
        pl.when(swapped)(lambda: out_remote(b).start())
        pl.when(kept)(lambda: out_local(b).start())

    def loads(k):
        if k == 0:
            gather_drain(0)
            ld_wu.start()
            ld_qkvm.start()
            return
        ld_wa.start()
        ld_xv.start()
        for b in range(4):
            pl.when(swapped)(lambda: out_remote(b).wait_send())
            pl.when(kept)(lambda: out_local(b).wait())
        ld_nrm.start()

    def t_up(lo, n):
        once(ld_n2)

        def one(u):
            ubs[pl.ds(u, 1), :] = dot_nn(ones, B[:, wide(u)])[0:1, :]
            gradient(n2[...], B[:, wide(u)], u % RING)

        span(one, lo, n)
        if lo + n == 4:
            vg[8:12, :] = ubs[0:4, :]

    def norm_back(dn, v, gain):
        hat, scale = norm_parts(v)
        e = dn * gain
        d = (e - jnp.mean(e, axis=-1, keepdims=True) - hat * jnp.mean(e * hat, axis=-1, keepdims=True)) * scale
        return d, jnp.sum(dn * hat, axis=0, keepdims=True), jnp.sum(dn, axis=0, keepdims=True)

    def second_norm(b):
        dn = dot_nt(B[tok(b), :], W[...])
        d, dgain, dshift = norm_back(dn, R[tok(b), :], vec[5:6, :])
        d = d + cot[tok(b), :].astype(F32)
        R[tok(b), :] = d
        B[tok(b), 3 * D :] = d.astype(BF)
        vg[5:6, :] = vg[5:6, :] + dgain
        vg[6:7, :] = vg[6:7, :] + dshift

    def t_out(k):
        once(ld_qkvm)
        vg[4:5, :] = dot_nn(ones, B[:, 3 * D :])[0:1, :]
        gradient(A[:, 3 * D :], B[:, 3 * D :], 8 % RING)

    def mixed_back(b):
        A[tok(b), 3 * D :] = dot_nt(B[tok(b), 3 * D :], W[:, 3 * D :]).astype(BF)

    def attention_back(i):
        low, high = head_masks()
        lane = lax.broadcasted_iota(jnp.int32, (1, 128), 1) < 64
        bias = segment_bias(seg, i)
        r = pl.ds(pl.multiple_of(i * 128, 128), 128)
        for p in range(6):
            col = 128 * p
            q = A[r, col : col + 128]
            k2 = stack_heads(A[r, D + col : D + col + 128], low, high)
            v2 = stack_heads(A[r, 2 * D + col : 2 * D + col + 128], low, high)
            dm = A[r, 3 * D + col : 3 * D + col + 128]
            soft = soft_pair(q, k2, bias)
            dp = dot_nt(dm, v2)
            both = dot_tn(soft.astype(BF), dm)
            B[r, 2 * D + col : 2 * D + col + 128] = jnp.where(lane, both[:128], both[128:]).astype(BF)
            halves = []
            for h in (0, 1):
                part = dp[:, 128 * h : 128 * h + 128]
                so = soft[:, 128 * h : 128 * h + 128]
                halves.append(so * (part - jnp.sum(part * so, axis=-1, keepdims=True)))
            ds = jnp.concatenate(halves, axis=1).astype(BF)
            B[r, col : col + 128] = (dot_nn(ds, k2) * SCALE).astype(BF)
            both = dot_tn(ds, q) * SCALE
            B[r, D + col : D + col + 128] = jnp.where(lane, both[:128], both[128:]).astype(BF)

    def t_att(lo, n):
        span(attention_back, 2 * lo, 2 * n)

    def t_qkv(lo, n):
        once(ld_nrm)
        if lo == 0:
            vg[2:3, :] = dot_nn(ones, B[:, 0:D])[0:1, :]
            vg[3:4, :] = dot_nn(ones, B[:, 2 * D : 3 * D])[0:1, :]
        span(lambda u: gradient(E[...], B[:, wide(u)], (u + 1) % RING), lo, n)

    def ig_remote(b):
        return remote(n2.at[tok(b)], ig_land.at[tok(b)], igs.at[b], igr.at[b], partner)

    def ig_local(b):
        return pltpu.make_async_copy(R.at[tok(b)], ig_o.at[tok(b)], igr.at[b])

    ld_land = load(ig_land, cot, 15)
    ld_ig = pltpu.make_async_copy(R, ig_o, lsem.at[16])

    def land(k):
        @pl.when(swapped)
        def _():
            for b in range(4):
                ig_remote(b).wait_recv()
            ld_land.start()
            ld_land.wait()

            def one(b):
                R[tok(b), :] = cot[tok(b), :].astype(F32)

            span(one, 0, 4)
            ld_ig.start()

    def first_norm_back(b):
        dn = dot_nt(B[tok(b), : 3 * D], W[:, : 3 * D])
        d, dgain, dshift = norm_back(dn, cot[tok(b), :].astype(F32), vec[0:1, :])
        R[tok(b), :] = R[tok(b), :] + d
        vg[0:1, :] = vg[0:1, :] + dgain
        vg[1:2, :] = vg[1:2, :] + dshift
        send_ig(b)

    def send_ig(b):
        @pl.when(swapped)
        def _():
            n2[tok(b), :] = R[tok(b), :].astype(BF)
            ig_remote(b).start()

        pl.when(kept)(lambda: ig_local(b).start())

    def cp_slice(j):
        return remote(vsl.at[j], vrc.at[2 * z + c], vss.at[j], vsr.at[2 * z + c], (2 * x + y, j))

    def each_slice(fn):
        def step(j, carry):
            pl.when(jnp.logical_or(swapped, j != f))(lambda: fn(j))
            return carry

        lax.fori_loop(0, 8, step, 0)

    def send_slices(k):
        for j in range(8):
            vsl[j, :, 0:SHARD] = vg[:, SHARD * j : SHARD * j + SHARD]

        @pl.when(kept)
        def _():
            vrc[pl.ds(2 * z + c, 1)] = vsl[pl.ds(f, 1)]

        each_slice(lambda j: cp_slice(j).start())

    def cp_change(k):
        return remote(vdl.at[g], vdl.at[g], vds.at[k], vdr.at[g], members[k])

    def t_vec_adam(k):
        def step(s, carry):
            pl.when(jnp.logical_or(swapped, s != 2 * z + c))(
                lambda: remote(vrc.at[s], vrc.at[s], vss.at[0], vsr.at[s], partner).wait_recv()
            )
            return carry

        lax.fori_loop(0, 8, step, 0)
        grad = jnp.sum(vrc[...], axis=0)[0:12, 0:SHARD]
        first = jnp.concatenate([v1[r] for r in range(12)], axis=0)
        second = jnp.concatenate([v2[r] for r in range(12)], axis=0)
        mom, sq, delta = adam_parts(first, second, vw[...], grad, RATE_VECTOR, 0.0)
        vm_o[...] = mom
        vs_o[...] = sq
        vdl[g, 0:12, 0:SHARD] = delta
        for k in range(3):
            cp_change(k).start()

    def t_vec_outer(k):
        for k in range(3):
            remote(vdl.at[froms[k]], vdl.at[froms[k]], vds.at[k], vdr.at[froms[k]], members[k]).wait_recv()
        mean = jnp.sum(vdl[...], axis=0)[0:12, 0:SHARD] * 0.25
        mom = OUTER_MOMENTUM * vo[...] + mean
        vp_o[...] = mom
        vq_o[...] = vw[...] - OUTER_RATE * (mean + OUTER_MOMENTUM * mom)

    members = [dev(x, 1 - c, z, y), dev(1 - x, c, z, y), dev(1 - x, 1 - c, z, y)]
    froms = [2 * x + 1 - c, 2 * (1 - x) + c, 2 * (1 - x) + 1 - c]

    def cp_core(p):
        return remote(G.at[p % RING, 1 - c], S.at[p], d2s.at[p], d2r.at[p], dev(x, 1 - c, z, y))

    def hop_up(p, t, k):
        return remote(S.at[p, t], ZI.at[p, t - z - 1], zs.at[p, k], zr.at[p, t - z - 1], dev(x, c, z + 1, y))

    def hop_down(p, t, k):
        return remote(S.at[p, t], ZI.at[p, 5 - z + t], zs.at[p, k], zr.at[p, 5 - z + t], dev(x, c, z - 1, y))

    def got(p, k):
        remote(ZI.at[p, k], ZI.at[p, k], zs.at[p, 0], zr.at[p, k], partner).wait_recv()

    def add_in(p, t, k):
        got(p, k)
        S[p, t] = (S[p, t].astype(F32) + ZI[p, k].astype(F32)).astype(BF)

    def s0(p):
        cp_core(p).start()

    def s1(p):
        cp_core(p).wait_recv()

        def one(t):
            S[p, t] = (S[p, t].astype(F32) + G[p % RING, c, t].astype(F32)).astype(BF)

        span(one, 0, 4)

        @pl.when(z == 0)
        def _():
            for k, t in enumerate((3, 2, 1)):
                hop_up(p, t, k).start()

        @pl.when(z == 3)
        def _():
            for k, t in enumerate((0, 1, 2)):
                hop_down(p, t, k).start()

        cp_core(p).wait_send()

    def s2(p):
        @pl.when(z == 1)
        def _():
            for k, t in enumerate((3, 2)):
                add_in(p, t, t - 1)
                hop_up(p, t, k).start()

        @pl.when(z == 2)
        def _():
            for k, t in enumerate((0, 1)):
                add_in(p, t, 2 + t)
                hop_down(p, t, k).start()

    def s3(p):
        @pl.when(z == 2)
        def _():
            add_in(p, 3, 1)
            hop_up(p, 3, 2).start()

        @pl.when(z == 1)
        def _():
            add_in(p, 0, 3)
            hop_down(p, 0, 2).start()

    def cp_final(p):
        return remote(S.at[p, z], FIN.at[p], fs.at[p], fr.at[p], partner)

    def col(p):
        return pl.ds(768 * (p % 4 if p < 8 else (p + 3) % 4), 768)

    def state_loads(p, fn):
        q = p % 2
        m = 1 - p // 4
        for k, src in enumerate((m1, m2, mw, mo) if p < 8 else (a1, a2, aw, ao)):
            src = src.at[m, :, col(p)] if p < 8 else src.at[:, col(p)]
            fn(pltpu.make_async_copy(src, IN.at[q, k], isem.at[q, k]))

    def state_stores(p, ks, fn):
        q = p % 2
        m = 1 - p // 4
        for k in ks:
            dst = ((mm_o, ms_o, mp_o, mq_o) if p < 8 else (am_o, as_o, ap_o, aq_o))[k]
            dst = dst.at[m, :, col(p)] if p < 8 else dst.at[:, col(p)]
            fn(pltpu.make_async_copy(OUT.at[q, k], dst, osem.at[q, k]))

    def start(cp):
        cp.start()

    def wait(cp):
        cp.wait()

    def s4(p):
        pl.when(z > 0)(lambda: add_in(p, z, 0))
        pl.when(z < 3)(lambda: add_in(p, z, 4))

        @pl.when(swapped)
        def _():
            cp_final(p).start()

        @pl.when(kept)
        def _():
            FIN[p] = S[p, z]

    def cp_delta(p, k):
        i = (g, g, froms[1])[k]
        return remote(DL.at[p, i], DL.at[p, i], ls.at[p, k], lr.at[p, i], members[1 if k == 1 else 0])

    def got_delta(p, k):
        i = froms[k]
        remote(DL.at[p, i], DL.at[p, i], ls.at[p, 0], lr.at[p, i], members[k]).wait_recv()

    def s5(p):
        pl.when(swapped)(lambda: cp_final(p).wait_recv())
        state_loads(p, wait)
        if p >= 2:
            state_stores(p - 2, (0, 1), wait)
        q = p % 2

        def rows(i, carry):
            r = pl.ds(pl.multiple_of(i * 32, 32), 32)
            mom, sq, delta = adam_parts(
                IN[q, 0, r, :], IN[q, 1, r, :], IN[q, 2, r, :], FIN[p, r, :].astype(F32), RATE_MATRIX, WEIGHT_DECAY
            )
            OUT[q, 0, r, :] = mom
            OUT[q, 1, r, :] = sq
            DL[p, g, r, :] = delta.astype(BF)
            return carry

        lax.fori_loop(0, 3, rows, 0)
        for k in (1, 0):
            cp_delta(p, k).start()
        state_stores(p, (0, 1), start)

    def s6(p):
        got_delta(p, 1)
        cp_delta(p, 2).start()

    def s7(p):
        got_delta(p, 0)
        got_delta(p, 2)
        if p >= 2:
            state_stores(p - 2, (2, 3), wait)
        q = p % 2

        def rows(i, carry):
            r = pl.ds(pl.multiple_of(i * 32, 32), 32)
            total = DL[p, 0, r, :].astype(F32)
            for k in (1, 2, 3):
                total = total + DL[p, k, r, :].astype(F32)
            mean = total * 0.25
            mom = OUTER_MOMENTUM * IN[q, 3, r, :] + mean
            OUT[q, 2, r, :] = mom
            OUT[q, 3, r, :] = IN[q, 2, r, :] - OUTER_RATE * (mean + OUTER_MOMENTUM * mom)
            return carry

        lax.fori_loop(0, 3, rows, 0)
        state_stores(p, (2, 3), start)

    sums = (s0, s1, s2, s3, s4, s5, s6, s7)
    does = {
        "g": lambda p, s: stages[s](p), "r": lambda p, k: sums[k](p), "il": lambda p: state_loads(p, start),
        "st": lambda k: None, "gd": t_down, "dh": lambda h, lo, n: spanned(functools.partial(hidden_back, h), ld_wd, ld_gp)(lo, n), "bo": spanned(block_output, ld_res),
        "ld": loads, "gu": t_up, "n2": spanned(second_norm, ld_wu), "go": t_out, "dm": spanned(mixed_back, ld_wa),
        "ab": t_att, "gq": t_qkv, "n1": spanned(first_norm_back, ld_xv), "ic": land,
        "vs": send_slices, "va": t_vec_adam, "vo": t_vec_outer,
    }
    for name, *at in ORDER_BACKWARD:
        does[name](*at)

    for p in range(RS):
        for k in range(3):
            remote(S.at[p, k], ZI.at[p, k], zs.at[p, k], zr.at[p, k], partner).wait_send()
        pl.when(swapped)(lambda: cp_final(p).wait_send())
        for k in range(3):
            cp_delta(p, k).wait_send()
    for p in (RS - 2, RS - 1):
        state_stores(p, (0, 1, 2, 3), wait)
    each_slice(lambda j: cp_slice(j).wait_send())
    for k in range(3):
        cp_change(k).wait_send()
    for b in range(4):

        @pl.when(swapped)
        def _():
            out_remote(b).wait_recv()
            ig_remote(b).wait_send()

        @pl.when(kept)
        def _():
            ig_local(b).wait()

    pl.when(swapped)(lambda: ld_ig.wait())


def backward(cot, fwd, states):
    any_ = pl.BlockSpec(memory_space=pl.ANY)
    vm = pl.BlockSpec(memory_space=pltpu.VMEM)
    dma = pltpu.SemaphoreType.DMA
    attn = jax.ShapeDtypeStruct((SHARD, FF), F32)
    mlp = jax.ShapeDtypeStruct((2, SHARD, FF), F32)
    vect = jax.ShapeDtypeStruct((12, SHARD), F32)
    return pl.pallas_call(
        backward_kernel,
        out_shape=(
            jax.ShapeDtypeStruct((T, D), BF), jax.ShapeDtypeStruct((T, D), F32),
            attn, attn, attn, attn, mlp, mlp, mlp, mlp, vect, vect, vect, vect,
            jax.ShapeDtypeStruct((T, D), BF),
        ),
        in_specs=[any_] * 11 + [vm, vm] + [any_] * 8 + [vm] * 4,
        out_specs=(any_,) * 10 + (vm,) * 4 + (any_,),
        scratch_shapes=[
            pltpu.VMEM((T, FF), BF), pltpu.VMEM((T, FF), BF), pltpu.VMEM((D, FF), BF),
            pltpu.VMEM((T, D), BF), pltpu.VMEM((T, D), BF), pltpu.VMEM((T, D), BF), pltpu.VMEM((T, D), F32),
            pltpu.VMEM((RING, 2, 4, SHARD, 768), BF), pltpu.VMEM((RS, 4, SHARD, 768), BF),
            pltpu.VMEM((RS, 5, SHARD, 768), BF), pltpu.VMEM((RS, SHARD, 768), BF),
            pltpu.VMEM((RS, 4, SHARD, 768), BF),
            pltpu.VMEM((2, 4, SHARD, 768), F32), pltpu.VMEM((2, 4, SHARD, 768), F32),
            pltpu.VMEM((16, D), F32), pltpu.VMEM((8, D), F32),
            pltpu.VMEM((8, 16, 128), F32), pltpu.VMEM((8, 16, 128), F32), pltpu.VMEM((4, 16, 128), F32),
            dma((21,)), dma((RS,)), dma((RS,)), dma((RS, 3)), dma((RS, 5)), dma((RS,)), dma((RS,)),
            dma((RS, 3)), dma((RS, 4)), dma((2, 4)), dma((2, 4)), dma((4,)), dma((4,)), dma((4,)), dma((4,)),
            dma((8,)), dma((8,)), dma((3,)), dma((4,)),
            *GATHER_SEMS(1),
        ],
        compiler_params=pltpu.CompilerParams(collective_id=2, has_side_effects=True, vmem_limit_bytes=63 * 2**20),
        name="backward",
    )(cot, *fwd, *states)


def fast(
    inputs, segments, cotangent,
    attn_weight, attn_first, attn_second, attn_outer,
    mlp_weight, mlp_first, mlp_second, mlp_outer,
    vector_weight, vector_first, vector_second, vector_outer,
):
    fwd = forward(inputs[0], cotangent[0], segments[0], attn_weight, mlp_weight, vector_weight)
    out = backward(
        cotangent[0],
        fwd,
        (
            attn_weight, attn_first[0], attn_second[0], attn_outer,
            mlp_weight, mlp_first[0], mlp_second[0], mlp_outer,
            vector_weight, jnp.transpose(vector_first, (1, 0, 2)), jnp.transpose(vector_second, (1, 0, 2)), vector_outer,
        ),
    )
    lead = (1, 1, 1, 1, 0, 0, 1, 1, 0, 0, 0, 0, 0, 0)
    return tuple(v[None] if k else v for v, k in zip(finish(out[:14]), lead))


def norm_apply(values, gain, shift):
    centre = values - jnp.mean(values, axis=-1, keepdims=True)
    spread = jnp.mean(centre * centre, axis=-1, keepdims=True)
    return centre * lax.rsqrt(spread + EPS_NORM) * gain + shift


def gelu_tanh(values):
    return jax.nn.gelu(values, approximate=True)


def adam_step(weight, first, second, gradient, step_rate, weight_decay):
    first_new = BETA_ONE * first + (1.0 - BETA_ONE) * gradient
    second_new = BETA_TWO * second + (1.0 - BETA_TWO) * gradient * gradient
    first_hat = first_new / (1.0 - BETA_ONE**STEP)
    second_hat = second_new / (1.0 - BETA_TWO**STEP)
    local_weight = weight - step_rate * (
        first_hat / (jnp.sqrt(second_hat) + ADAM_EPS) + weight_decay * weight
    )
    return (first_new, second_new, weight - local_weight)


def local(
    inputs,
    segments,
    cotangent,
    attn_weight,
    attn_first,
    attn_second,
    attn_outer,
    mlp_weight,
    mlp_first,
    mlp_second,
    mlp_outer,
    vector_weight,
    vector_first,
    vector_second,
    vector_outer,
):
    bf16 = jnp.bfloat16
    f32 = jnp.float32
    attn_cast = attn_weight.astype(bf16)
    mlp_cast = mlp_weight.astype(bf16)
    attn_low, mlp_low, vector_low = (
        lax.all_gather(attn_cast, "fsdp", axis=0, tiled=True),
        lax.all_gather(mlp_cast, "fsdp", axis=1, tiled=True),
        lax.all_gather(vector_weight.astype(bf16), "fsdp", axis=1, tiled=True),
    )
    vectors = vector_low.astype(f32)
    tokens_f = inputs[0].astype(f32)
    seg_ids = segments[0]
    back_f = cotangent[0].astype(f32)
    model_width = attn_low.shape[0]
    head_dim = model_width // HEADS
    score_scale = head_dim ** (-0.5)
    tok_count = tokens_f.shape[0]
    row_count = tok_count // SEQ
    shape_four = (row_count, SEQ, HEADS, head_dim)
    normed_f, norm_pull = jax.vjp(norm_apply, tokens_f, vectors[0], vectors[1])
    normed = normed_f.astype(bf16)
    project = jnp.dot(normed, attn_low[:, : 3 * model_width], preferred_element_type=f32)
    queries = (project[:, :model_width] + vectors[2]).astype(bf16).reshape(shape_four)
    keys_all = project[:, model_width : 2 * model_width].astype(bf16).reshape(shape_four)
    values_all = (
        (project[:, 2 * model_width : 3 * model_width] + vectors[3])
        .astype(bf16)
        .reshape(shape_four)
    )
    scores = (
        jnp.einsum("rqhd,rkhd->rhqk", queries, keys_all, preferred_element_type=f32) * score_scale
    )
    same_seg = (seg_ids[:, :, None] == seg_ids[:, None, :])[:, None]
    masked = jnp.where(same_seg, scores, NEG_LARGE)
    exponent = jnp.exp(masked - jnp.max(masked, axis=-1, keepdims=True))
    soft = exponent / jnp.sum(exponent, axis=-1, keepdims=True)
    probs = soft.astype(bf16)
    mixed = (
        jnp.einsum("rhqk,rkhd->rqhd", probs, values_all, preferred_element_type=f32)
        .reshape(tok_count, model_width)
        .astype(bf16)
    )
    attended = (
        jnp.dot(mixed, attn_low[:, 3 * model_width :], preferred_element_type=f32) + vectors[4]
    )
    residual = tokens_f + attended
    normed_two_f, norm_two_pull = jax.vjp(norm_apply, residual, vectors[5], vectors[6])
    normed_two = normed_two_f.astype(bf16)
    up_pre = jnp.dot(normed_two, mlp_low[0], preferred_element_type=f32) + vectors[8:12].reshape(-1)
    hidden_f, gelu_pull = jax.vjp(gelu_tanh, up_pre)
    hidden = hidden_f.astype(bf16)
    branch = jnp.einsum("nf,df->nd", hidden, mlp_low[1], preferred_element_type=f32) + vectors[7]
    block_out = (residual + branch).astype(bf16)
    d_branch = cotangent[0]
    d_down_bias = jnp.sum(back_f, axis=0)
    grad_down = jnp.einsum("nd,nf->df", d_branch, hidden, preferred_element_type=f32)
    d_hidden = jnp.einsum("nd,df->nf", d_branch, mlp_low[1], preferred_element_type=f32)
    (d_up_f,) = gelu_pull(d_hidden)
    d_up = d_up_f.astype(bf16)
    d_up_bias = jnp.sum(d_up.astype(f32), axis=0)
    grad_up = jnp.einsum("nd,nf->df", normed_two, d_up, preferred_element_type=f32)
    mlp_grad = jnp.stack([grad_up, grad_down])
    d_normed_two = jnp.einsum("nf,df->nd", d_up, mlp_low[0], preferred_element_type=f32)
    d_res_norm, d_gain_two, d_shift_two = norm_two_pull(d_normed_two)
    d_res = back_f + d_res_norm
    d_att = d_res.astype(bf16)
    d_out_bias = jnp.sum(d_att.astype(f32), axis=0)
    grad_out = jnp.einsum("nc,nd->cd", mixed, d_att, preferred_element_type=f32)
    d_mixed = (
        jnp.einsum("nd,cd->nc", d_att, attn_low[:, 3 * model_width :], preferred_element_type=f32)
        .astype(bf16)
        .reshape(shape_four)
    )
    d_values = (
        jnp.einsum("rhqk,rqhd->rkhd", probs, d_mixed, preferred_element_type=f32)
        .reshape(tok_count, model_width)
        .astype(bf16)
    )
    d_probs = jnp.einsum("rqhd,rkhd->rhqk", d_mixed, values_all, preferred_element_type=f32)
    d_scores = (soft * (d_probs - jnp.sum(d_probs * soft, axis=-1, keepdims=True))).astype(bf16)
    d_queries = (
        (
            jnp.einsum("rhqk,rkhd->rqhd", d_scores, keys_all, preferred_element_type=f32)
            * score_scale
        )
        .reshape(tok_count, model_width)
        .astype(bf16)
    )
    d_keys = (
        (jnp.einsum("rhqk,rqhd->rkhd", d_scores, queries, preferred_element_type=f32) * score_scale)
        .reshape(tok_count, model_width)
        .astype(bf16)
    )
    d_query_bias = jnp.sum(d_queries.astype(f32), axis=0)
    d_value_bias = jnp.sum(d_values.astype(f32), axis=0)
    d_project = jnp.concatenate([d_queries, d_keys, d_values], axis=1)
    grad_qkv = jnp.einsum("nc,nd->cd", normed, d_project, preferred_element_type=f32)
    d_normed = jnp.einsum(
        "nd,cd->nc", d_project, attn_low[:, : 3 * model_width], preferred_element_type=f32
    )
    d_tok_norm, d_gain_one, d_shift_one = norm_pull(d_normed)
    input_grad = d_res + d_tok_norm
    attn_grad = jnp.concatenate([grad_qkv, grad_out], axis=1)
    vector_grad = jnp.concatenate(
        [
            jnp.stack(
                [
                    d_gain_one,
                    d_shift_one,
                    d_query_bias,
                    d_value_bias,
                    d_out_bias,
                    d_gain_two,
                    d_shift_two,
                    d_down_bias,
                ]
            ),
            d_up_bias.reshape(4, model_width),
        ],
        axis=0,
    )
    attn_sum, mlp_sum, vector_sum = (
        lax.psum_scatter(attn_grad.astype(bf16), "fsdp", scatter_dimension=0, tiled=True).astype(f32),
        lax.psum_scatter(mlp_grad.astype(bf16), "fsdp", scatter_dimension=1, tiled=True).astype(f32),
        lax.psum_scatter(vector_grad, "fsdp", scatter_dimension=1, tiled=True),
    )
    attn_moment, attn_square, attn_delta = adam_step(
        attn_weight, attn_first[0], attn_second[0], attn_sum, RATE_MATRIX, WEIGHT_DECAY
    )
    mlp_moment, mlp_square, mlp_delta = adam_step(
        mlp_weight, mlp_first[0], mlp_second[0], mlp_sum, RATE_MATRIX, WEIGHT_DECAY
    )
    vector_moment, vector_square, vector_delta = adam_step(
        vector_weight, vector_first[0], vector_second[0], vector_sum, RATE_VECTOR, 0.0
    )
    group_count = lax.axis_size("group")
    attn_total, mlp_total, vector_total = (
        lax.psum(attn_delta.astype(jnp.bfloat16), "group").astype(jnp.float32),
        lax.psum(mlp_delta.astype(jnp.bfloat16), "group").astype(jnp.float32),
        lax.psum(vector_delta.astype(jnp.bfloat16), "group").astype(jnp.float32),
    )
    attn_mean = attn_total / group_count
    mlp_mean = mlp_total / group_count
    vector_mean = vector_total / group_count
    attn_momentum = OUTER_MOMENTUM * attn_outer + attn_mean
    mlp_momentum = OUTER_MOMENTUM * mlp_outer + mlp_mean
    vector_momentum = OUTER_MOMENTUM * vector_outer + vector_mean
    attn_master = attn_weight - OUTER_RATE * (attn_mean + OUTER_MOMENTUM * attn_momentum)
    mlp_master = mlp_weight - OUTER_RATE * (mlp_mean + OUTER_MOMENTUM * mlp_momentum)
    vector_master = vector_weight - OUTER_RATE * (vector_mean + OUTER_MOMENTUM * vector_momentum)
    return (
        block_out[None],
        input_grad[None],
        attn_moment[None],
        attn_square[None],
        attn_momentum,
        attn_master,
        mlp_moment[None],
        mlp_square[None],
        mlp_momentum,
        mlp_master,
        vector_moment[None],
        vector_square[None],
        vector_momentum,
        vector_master,
    )


def solution(mesh):
    in_specs = (
        P("group", "fsdp", None),
        P("group", "fsdp", None),
        P("group", "fsdp", None),
        P("fsdp", None),
        P("group", "fsdp", None),
        P("group", "fsdp", None),
        P("fsdp", None),
        P(None, "fsdp", None),
        P("group", None, "fsdp", None),
        P("group", None, "fsdp", None),
        P(None, "fsdp", None),
        P(None, "fsdp"),
        P("group", None, "fsdp"),
        P("group", None, "fsdp"),
        P(None, "fsdp"),
    )
    out_specs = (
        P("group", "fsdp", None),
        P("group", "fsdp", None),
        P("group", "fsdp", None),
        P("group", "fsdp", None),
        P("fsdp", None),
        P("fsdp", None),
        P("group", None, "fsdp", None),
        P("group", None, "fsdp", None),
        P(None, "fsdp", None),
        P(None, "fsdp", None),
        P("group", None, "fsdp"),
        P("group", None, "fsdp"),
        P(None, "fsdp"),
        P(None, "fsdp"),
    )
    fits = mesh.shape["group"] == 4 and mesh.shape["fsdp"] == 8
    return jax.shard_map(fast if fits else local, mesh=mesh, in_specs=in_specs, out_specs=out_specs, check_vma=False)
```
